32 devices in a mesh: seq: 8 (over z, y), grp: 4 (over x, core).
Axes of the slice: x: 2, y: 2, z: 4, core: 2. Of those that a mesh axis runs over, the one named last changes fastest.
Arguments:
- hidden: bfloat16 [4096, 2688], P(('seq', 'grp')), may hold values from -30 to 30
- conv_input: bfloat16 [4096, 3072], P(('seq', 'grp')), may hold values from -30 to 30
- z_stream: bfloat16 [4096, 2048], P(('seq', 'grp')), may hold values from -6 to 6
- log_decay: float32 [32, 4096], P(None, ('seq', 'grp')), may hold values from -1.5 to 0
- conv_weight: float32 [4, 3072], replicated, may hold values from -3 to 3
- norm_gain: float32 [2048], replicated, may hold values from 0.5 to 1.5
- out_weight: bfloat16 [2048, 2688], P('grp'), may hold values from -0.125 to 0.125
- moe_gain: float32 [2688], replicated, may hold values from 0.5 to 1.5
- routes: int32 [4096, 6], P(('seq', 'grp')), may hold values from 0 to 31, all different within a row; in each aligned block of 128 rows (0 to 127, 128 to 255, ...) at most 36 rows name the same one
- gate_weights: float32 [4096, 6], P(('seq', 'grp')), may hold values from 0.1 to 1
- expert_home: int32 [32], replicated, may hold values from 0 to 31, each once
- up_weight: bfloat16 [32, 2688, 1024], P(('seq', 'grp')), may hold values from -0.125 to 0.125
- down_weight: bfloat16 [32, 1024, 2688], P(('seq', 'grp')), may hold values from -0.1875 to 0.1875
Outputs:
- output: bfloat16 [4096, 2688], P(('seq', 'grp'))
The draws below stay inside these ranges and needn't reach their ends.
Inputs may be any that keep to these rules, and one draw needn't show every extreme that they name: `routes`: among the rows of one device no expert is named more than 36 times, a bound that some block reaches. `expert_home`: each expert is held by exactly one device, and each device holds one expert.
All inputs are finite; a program needn't handle non-finite values.
Results may differ from the reference program's by a relative error of at most 0.013.
Values may be sent and summed in bfloat16 or wider, within the bound.
No kernel may reach another device: no remote copies, remote signals or barrier semaphores. Data moves between devices by JAX's collectives and lax.ppermute only.
A program may use at most 128 MiB of HBM per device.

```python
import math
import jax
import jax.numpy as jnp
import numpy as np
from jax import lax

D = 2688
H = 32
P_SIZE = 64
N = 64
G = 8
KERNEL = 4
TOPK = 6
FFW = 1024
QB = 128
TOK_DEV = 128
INNER = 2048
CHANNELS = 3072
TOKENS = 4096
EXPERTS = 32
CAP = 36
N_SEQ = 8
N_GRP = 4


def scaled_field(key, row_count, col_count):
    subkeys = jax.random.split(key, 3)
    row_scale = jnp.exp(jax.random.uniform(subkeys[0], (row_count, 1), minval=jnp.log(0.3), maxval=jnp.log(3.0)))
    col_scale = jnp.exp(jax.random.uniform(subkeys[1], (1, col_count), minval=jnp.log(0.3), maxval=jnp.log(3.0)))
    drawn = jax.random.normal(subkeys[2], (row_count, col_count)) * row_scale * col_scale
    return jnp.clip(drawn, -30.0, 30.0)


def draw_hidden(key, part):
    return scaled_field(jax.random.fold_in(key, 11), TOKENS, D).astype(jnp.bfloat16)


def draw_conv_input(key, part):
    return scaled_field(jax.random.fold_in(key, 12), TOKENS, CHANNELS).astype(jnp.bfloat16)


def draw_log_decay(key, part):
    subkeys = jax.random.split(jax.random.fold_in(key, 13), 7)
    fast_share = 0.5
    forgetful = jax.random.uniform(subkeys[0], (H, 1)) < fast_share
    fast_rate = jnp.exp(jax.random.uniform(subkeys[1], (H, 1), minval=jnp.log(1.0 / 50.0), maxval=jnp.log(1.0 / 30.0)))
    slow_rate = jnp.exp(jax.random.uniform(subkeys[2], (H, 1), minval=jnp.log(0.05), maxval=jnp.log(0.35))) / TOKENS
    reference_speed = jnp.where(forgetful, fast_rate, slow_rate)
    shard_count = TOKENS // TOK_DEV
    lines_each_partition = jnp.exp(jax.random.uniform(subkeys[3], (H, shard_count, 1), minval=jnp.log(0.6), maxval=jnp.log(1.5)))
    lines_each_partition = jnp.broadcast_to(lines_each_partition, (H, shard_count, TOK_DEV)).reshape(H, TOKENS)
    uneven_division = jax.random.uniform(subkeys[4], (H, TOKENS), minval=0.5, maxval=1.5)
    vacant_places = jax.random.randint(subkeys[5], (2,), 0, TOKENS)
    discarded_words = jax.random.uniform(subkeys[6], (H, 2), minval=0.22, maxval=0.69)
    assignment_seats = jnp.arange(TOKENS)
    spike_occurrences = discarded_words[:, 0:1] * (assignment_seats[None, :] == vacant_places[0]) + discarded_words[:, 1:2] * (assignment_seats[None, :] == vacant_places[1])
    return -(reference_speed * lines_each_partition * uneven_division + spike_occurrences)


def shard_levels(stream_key, extent, cuts, least, high):
    level, own = 1.0, jax.random.fold_in(stream_key, 6)
    for dim, parts in cuts:
        steps = jnp.exp(jax.random.uniform(jax.random.fold_in(own, dim), (parts,), jnp.float32, least / len(cuts), high / len(cuts)))
        level = level * jnp.repeat(steps, extent[dim] // parts).reshape([-1 if axis == dim else 1 for axis in range(len(extent))])
    return level


def deal_out(own_key, own, number, rows, count, top, most, lean):
    sequence = jax.random.permutation(own_key, count)
    crowded, usual = portions_of(count, rows * top, most, lean, True), portions_of(count, rows * top, most, lean, False)
    places = jnp.arange(count)

    def named(sizes, offset_by):
        used = int((sizes > 0).sum())
        fixed = max(1, used // 4)
        shifted = fixed + (places - fixed + offset_by * (used - fixed)) % max(1, count - fixed)
        return jnp.zeros((count,), jnp.int32).at[sequence[jnp.where(places < fixed, places, shifted)]].set(jnp.asarray(sizes, jnp.int32))

    sizes = jnp.where(number % 4 == 0, named(crowded, number // 4), named(usual, number - number // 4 - 1))
    mixed = jax.random.permutation(jax.random.fold_in(own, 3), count)
    giver, receiver = mixed[0:count // 2 * 2:2], mixed[1:count // 2 * 2:2]
    room = jnp.minimum(sizes[giver] - 1, most - sizes[receiver]) // 2
    room = jnp.where((giver == sequence[0]) | (receiver == sequence[0]) | (sizes[receiver] == 0), 0, jnp.maximum(room, 0))
    shifted = jax.random.randint(jax.random.fold_in(own, 4), (count // 2,), 0, 1 << 20) % (room + 1)
    sizes = sizes.at[giver].add(-shifted).at[receiver].add(shifted)
    items = jnp.searchsorted(jnp.cumsum(sizes), jnp.arange(rows * top), side="right").astype(jnp.int32)
    table = items.reshape(top, rows).T
    table = table[jax.random.permutation(jax.random.fold_in(own, 1), rows)]
    offset_by = jax.random.randint(jax.random.fold_in(own, 2), (rows, 1), 0, top)
    return jnp.take_along_axis(table, (jnp.arange(top)[None, :] + offset_by) % top, axis=1)


def portions_of(number_of, total, limit, lean, full):
    weights = [(1 << 20) // math.isqrt(grade ** lean) + 1 for grade in range(1, number_of + 1)]
    largest = limit if full else min(limit, max(-(-total // number_of), total * weights[0] // sum(weights)))
    least = 1 if total - largest >= number_of - 1 else 0
    given, rest = [largest] + [least] * (number_of - 1), total - largest - least * (number_of - 1)
    while rest > 0:
        candidates = [i for i in range(1, number_of) if given[i] < largest] or [i for i in range(1, number_of) if given[i] < limit]
        whole, remaining = sum([weights[i] for i in candidates]), rest
        for i in candidates:
            extra = min(limit - given[i], max(1, remaining * weights[i] // whole), rest)
            given[i] = given[i] + extra
            rest = rest - extra
    return np.array(given)


def centred(stream_key, shape, scale, most, shards=(), held_as=jnp.bfloat16):
    values = jax.random.normal(stream_key, shape, jnp.float32) * scale
    if len(shards) > 0:
        values = shard_levels(stream_key, shape, shards, -0.22, 0.18) * values
    return jnp.clip(values, min=-most, max=most).astype(held_as)


def setup_inputs(seed: int = 0) -> dict:
    key_list = jax.random.split(jax.random.key(seed), 14)
    hidden = draw_hidden(jax.random.fold_in(key_list[13], 71), 0)
    conv_input = draw_conv_input(jax.random.fold_in(key_list[13], 71), 0)
    z_stream = centred(key_list[2], (TOKENS, INNER), 1.0, 6.0, ((0, 32),))
    log_decay = draw_log_decay(jax.random.fold_in(key_list[13], 71), 0)
    conv_weight = centred(key_list[4], (KERNEL, CHANNELS), 0.5, 3.0, (), jnp.float32)
    norm_gain = jnp.clip(1.0 + 0.1 * jax.random.normal(key_list[5], (INNER,), jnp.float32), 0.5, 1.5)
    out_weight = centred(key_list[6], (INNER, D), INNER ** -0.5, 0.125, ((0, 4),))
    moe_gain = jnp.clip(1.0 + 0.1 * jax.random.normal(key_list[7], (D,), jnp.float32), 0.5, 1.5)
    routes_keys = jax.random.split(jax.random.fold_in(key_list[8], 1), TOKENS // TOK_DEV)
    routes_turns = jax.random.permutation(jax.random.fold_in(key_list[8], 3), TOKENS // TOK_DEV)
    routes = jax.vmap(lambda own, number: deal_out(jax.random.fold_in(key_list[8], 2), own, number, TOK_DEV, EXPERTS, TOPK, CAP, 2))(routes_keys, routes_turns).reshape((TOKENS, TOPK))
    gate_weights = jnp.clip(0.1 + 0.9 * jax.random.uniform(key_list[9], (TOKENS, TOPK), jnp.float32) ** shard_levels(key_list[9], (TOKENS, TOPK), ((0, 32),), -0.2, 0.2), 0.1, 1.0)
    expert_home = jax.random.permutation(key_list[10], EXPERTS).astype(jnp.int32)
    up_weight = centred(key_list[11], (EXPERTS, D, FFW), D ** -0.5, 0.125, ((0, 32),))
    down_weight = centred(key_list[12], (EXPERTS, FFW, D), FFW ** -0.5, 0.1875, ((0, 32),))
    return {"hidden": hidden, "conv_input": conv_input, "z_stream": z_stream, "log_decay": log_decay, "conv_weight": conv_weight, "norm_gain": norm_gain, "out_weight": out_weight, "moe_gain": moe_gain, "routes": routes, "gate_weights": gate_weights, "expert_home": expert_home, "up_weight": up_weight, "down_weight": down_weight}


epsilon = 1e-05
highest = lax.Precision.HIGHEST

def convolve(stream, previous, conv_weight):
    length = stream.shape[0]
    padded = jnp.concatenate([previous, stream], axis=0).astype(jnp.float32)
    summed = conv_weight[0][None, :] * padded[0:length]
    for offset in range(1, conv_weight.shape[0]):
        summed = summed + conv_weight[offset][None, :] * padded[offset:offset + length]
    return jax.nn.silu(summed).astype(jnp.bfloat16)

def span_parts(value_block, inkey_block, outkey_block, decay_block):
    cumulative = jnp.cumsum(decay_block, axis=-1)
    block_len = decay_block.shape[-1]
    intersection = jnp.einsum('tgn,sgn->gts', outkey_block, inkey_block, precision=highest)
    causal = lax.broadcasted_iota(jnp.int32, (block_len, block_len), 0) >= lax.broadcasted_iota(jnp.int32, (block_len, block_len), 1)
    spread = cumulative[..., :, None] - cumulative[..., None, :]
    mixing = jnp.where(causal, jnp.exp(jnp.where(causal, spread, 0.0)), 0.0) * intersection[:, None]
    inside = jnp.einsum('gjts,sgjp->tgjp', mixing, value_block, precision=highest)
    to_end = jnp.exp(cumulative[..., -1:] - cumulative)
    end_state = jnp.einsum('gjs,sgjp,sgn->gjpn', to_end, value_block, inkey_block, precision=highest)
    return (inside, end_state, cumulative)

def entering(outkey_block, carried, cumulative):
    reach = jnp.einsum('tgn,gjpn->tgjp', outkey_block, carried, precision=highest)
    return reach * jnp.exp(jnp.transpose(cumulative, (2, 0, 1)))[..., None]

def gated_norm(ssm_out, z_stream, norm_gain, group_count):
    gated_out = ssm_out * jax.nn.silu(z_stream.astype(jnp.float32))
    row_count = gated_out.shape[0]
    grouped = gated_out.reshape(row_count, group_count, -1)
    scaled = grouped * lax.rsqrt(lax.optimization_barrier(jnp.mean(grouped * grouped, axis=-1, keepdims=True)) + epsilon)
    return (scaled.reshape(row_count, -1) * norm_gain[None, :]).astype(jnp.bfloat16)

def token_norm(stream, gain):
    widened = stream.astype(jnp.float32)
    scaled = widened * lax.rsqrt(lax.optimization_barrier(jnp.mean(widened * widened, axis=-1, keepdims=True)) + epsilon)
    return (scaled * gain[None, :]).astype(jnp.bfloat16)

def reference(hidden, conv_input, z_stream, log_decay, conv_weight, norm_gain, out_weight, moe_gain, routes, gate_weights, expert_home, up_weight, down_weight):
    kernel = conv_weight.shape[0]
    active = convolve(conv_input, jnp.zeros((kernel - 1, conv_input.shape[1]), jnp.bfloat16), conv_weight)
    inner_width = H * P_SIZE
    per_group = H // G
    blocks = TOKENS // QB
    values = active[:, :inner_width].astype(jnp.float32)
    in_keys = active[:, inner_width:inner_width + G * N].astype(jnp.float32)
    out_keys = active[:, inner_width + G * N:].astype(jnp.float32)
    value_spans = values.reshape(blocks, QB, G, per_group, P_SIZE)
    inkey_spans = in_keys.reshape(blocks, QB, G, N)
    outkey_spans = out_keys.reshape(blocks, QB, G, N)
    decay_spans = log_decay.reshape(G, per_group, blocks, QB).transpose(2, 0, 1, 3)

    def advance(carried, pieces):
        value_block, inkey_block, outkey_block, decay_block = pieces
        inside, end_state, cumulative = span_parts(value_block, inkey_block, outkey_block, decay_block)
        carried_out = entering(outkey_block, carried, cumulative)
        carried = jnp.exp(cumulative[..., -1])[..., None, None] * carried + end_state
        return (carried, inside + carried_out)
    _, ssm_spans = lax.scan(advance, jnp.zeros((G, per_group, P_SIZE, N), jnp.float32), (value_spans, inkey_spans, outkey_spans, decay_spans))
    ssm_out = ssm_spans.reshape(TOKENS, inner_width)
    mixed_norm = gated_norm(ssm_out, z_stream, norm_gain, G)
    mamba_out = jnp.dot(mixed_norm, out_weight, preferred_element_type=jnp.float32)
    residual_one = (hidden.astype(jnp.float32) + mamba_out).astype(jnp.bfloat16)
    moe_in = token_norm(residual_one, moe_gain)
    flat_routes = routes.reshape(-1)
    pair_total = flat_routes.shape[0]
    sorted_pairs = jnp.argsort(flat_routes, stable=True).astype(jnp.int32)
    expert_ids = jnp.arange(EXPERTS, dtype=jnp.int32)
    expert_loads = lax.optimization_barrier(jnp.sum((flat_routes[:, None] == expert_ids[None, :]).astype(jnp.int32), axis=0)).astype(jnp.int32)
    starts = (jnp.cumsum(expert_loads) - expert_loads).astype(jnp.int32)
    most_rows = N_SEQ * N_GRP * CAP
    positions = jnp.arange(most_rows, dtype=jnp.int32)

    def serve(outputs, expert):
        slot_index = starts[expert] + positions
        filled = positions < expert_loads[expert]
        pair_ids = sorted_pairs[jnp.minimum(slot_index, pair_total - 1)]
        home_device = expert_home[expert]
        row_data = moe_in[pair_ids // TOPK]
        up_result = jnp.dot(row_data, up_weight[home_device], preferred_element_type=jnp.float32)
        squared = jnp.square(jax.nn.relu(up_result)).astype(jnp.bfloat16)
        result = jnp.dot(squared, down_weight[home_device], preferred_element_type=jnp.float32).astype(jnp.bfloat16)
        target = jnp.where(filled, pair_ids, pair_total).astype(jnp.int32)
        return (outputs.at[target].set(result, mode='drop'), None)
    pair_out, _ = lax.scan(serve, jnp.zeros((pair_total, D), jnp.bfloat16), expert_ids)
    pair_out = pair_out.reshape(TOKENS, TOPK, D)
    mixture = residual_one.astype(jnp.float32)
    for pick_index in range(TOPK):
        mixture = mixture + gate_weights[:, pick_index:pick_index + 1] * pair_out[:, pick_index].astype(jnp.float32)
    return mixture.astype(jnp.bfloat16)
```

```python
import functools

import jax
import jax.numpy as jnp
from jax import lax
from jax.experimental import pallas as pl
from jax.experimental.pallas import tpu as pltpu
from jax.sharding import PartitionSpec as P

AXES = ("seq", "grp")
N = 64
G = 8
EPS = 1e-05
DEC = 16
VMEM_LIMIT = 48 * 1024 * 1024
f32 = jnp.float32
bf16 = jnp.bfloat16


def dot(a, b, contract, precision=None):
    return lax.dot_general(
        a, b, ((contract[0], contract[1]), ((), ())), preferred_element_type=f32, precision=precision
    )


def spread_lanes(columns, width):
    count = len(columns)
    rows = columns[0].shape[0]
    lane = lax.broadcasted_iota(jnp.int32, (rows, count * width), 1)
    out = jnp.broadcast_to(columns[-1], (rows, count * width))
    for j in range(count - 2, -1, -1):
        out = jnp.where(lane < (j + 1) * width, columns[j], out)
    return out


def split_decay(d):
    whole = jnp.floor(d)
    part = d - whole
    coarse = jnp.floor(part * 256.0) * (1.0 / 256.0)
    fine = part - coarse
    row = lax.broadcasted_iota(jnp.int32, (DEC, d.shape[1]), 0)
    rows = jnp.where(row == 0, whole, jnp.where(row == 1, coarse, jnp.where(row == 2, fine, 0.0)))
    return rows.astype(bf16)


def join_decay(rows):
    return jnp.sum(rows.astype(f32), axis=0, keepdims=True)


def silu(x):
    return x * (1.0 / (1.0 + jnp.exp(-x)))


def start_kernel(plane, r_ref, x_ref, prev_ref, cw_ref, ld_ref, act_ref, cum_ref, cumt_ref, *rest):
    outs, scr = rest[:plane], rest[plane]
    length, channels = x_ref.shape
    heads = ld_ref.shape[0]
    per_group = heads // G
    inner = channels - 2 * G * N
    width = inner // G
    head_size = width // per_group
    halo, taps = prev_ref.shape[0], cw_ref.shape[0]
    ld = ld_ref[...]
    low = (
        lax.broadcasted_iota(jnp.int32, (length, length), 0)
        >= lax.broadcasted_iota(jnp.int32, (length, length), 1)
    ).astype(f32)
    cum_ref[...] = dot(ld, low, ((1,), (1,)), lax.Precision.HIGHEST)
    cumt = dot(low, ld, ((1,), (1,)), lax.Precision.HIGHEST)
    cumt_ref[...] = cumt
    last = cumt[length - 1 : length, :]
    to_end = jnp.exp(last - cumt)
    for c in range(0, channels, width):
        cols = slice(c, c + width)
        padded = jnp.concatenate([prev_ref[:, cols], x_ref[:, cols]], axis=0).astype(f32)
        first = halo - taps + 1
        total = cw_ref[0:1, cols] * padded[first : first + length]
        for k in range(1, taps):
            total = total + cw_ref[k : k + 1, cols] * padded[first + k : first + k + length]
        act_ref[:, cols] = silu(total).astype(bf16)
    for g in range(G):
        v = act_ref[:, g * width : (g + 1) * width].astype(f32)
        ik = act_ref[:, inner + g * N : inner + (g + 1) * N]
        hs = range(g * per_group, (g + 1) * per_group)
        weighted = (v * spread_lanes([to_end[:, h : h + 1] for h in hs], head_size)).astype(bf16)
        scr[g, :N, :] = dot(ik, weighted, ((0,), (0,))).astype(bf16)
        scr[g, N:, :] = split_decay(spread_lanes([last[:, h : h + 1] for h in hs], head_size))
    r = r_ref[0]
    for m in range(plane):
        outs[m][...] = scr[r ^ m]


def plane_kernel(plane, r_ref, *rest):
    chunks, out, scr = rest[:plane], rest[plane], rest[plane + 1]
    r = r_ref[0]
    for m in range(plane):
        scr[r ^ m] = chunks[m][...]
    state = jnp.zeros((N, out.shape[1]), f32)
    total = jnp.zeros((1, out.shape[1]), f32)
    for s in range(plane):
        decay = join_decay(scr[s, N:, :])
        state = jnp.exp(decay) * state + scr[s, :N, :].astype(f32)
        total = total + decay
    out[:N, :] = state.astype(bf16)
    out[N:, :] = split_decay(total)


def enter_kernel(plane, outer, r_ref, *rest):
    chunks, earlier = rest[:plane], rest[plane : plane + outer - 1]
    outs, scr, inc = rest[plane + outer - 1 : 2 * plane + outer - 1], rest[-2], rest[-1]
    r = r_ref[0]
    for m in range(plane):
        scr[r ^ m] = chunks[m][...]
    state = jnp.zeros((N, scr.shape[2]), f32)
    passed = jnp.zeros((1, scr.shape[2]), f32)
    for e in earlier:
        state = state + jnp.exp(passed) * e[:N, :].astype(f32)
        passed = passed + join_decay(e[N:, :])
    for s in range(plane):
        inc[s] = state.astype(bf16)
        state = jnp.exp(join_decay(scr[s, N:, :])) * state + scr[s, :N, :].astype(f32)
    for m in range(plane):
        outs[m][...] = inc[r ^ m]


def inside_kernel(act_ref, cum_ref, cumt_ref, out_ref):
    length, channels = act_ref.shape
    heads = cum_ref.shape[0]
    per_group = heads // G
    inner = channels - 2 * G * N
    head_size = inner // heads
    causal = lax.broadcasted_iota(jnp.int32, (length, length), 0) >= lax.broadcasted_iota(
        jnp.int32, (length, length), 1
    )
    cum = cum_ref[...]
    cumt = cumt_ref[...]
    for g in range(G):
        ik = act_ref[:, inner + g * N : inner + (g + 1) * N]
        ok = act_ref[:, inner + (G + g) * N : inner + (G + g + 1) * N]
        meet = jnp.where(causal, dot(ok, ik, ((1,), (1,))), 0.0)
        for h in range(g * per_group, (g + 1) * per_group):
            gap = jnp.where(causal, cumt[:, h : h + 1] - cum[h : h + 1, :], 0.0)
            mixing = (jnp.exp(gap) * meet).astype(bf16)
            cols = slice(h * head_size, (h + 1) * head_size)
            out_ref[:, cols] = dot(mixing, act_ref[:, cols], ((1,), (0,)))


def norm_kernel(plane, r_ref, act_ref, cumt_ref, inside_ref, z_ref, gain_ref, *rest):
    incoming, out_ref, scr = rest[:plane], rest[plane], rest[plane + 1]
    r = r_ref[0]
    for m in range(plane):
        scr[r ^ m] = incoming[m][...]
    inner = z_ref.shape[1]
    heads = cumt_ref.shape[1]
    per_group = heads // G
    width = inner // G
    head_size = inner // heads
    reach = jnp.exp(cumt_ref[...])
    for g in range(G):
        cols = slice(g * width, (g + 1) * width)
        ok = act_ref[:, inner + (G + g) * N : inner + (G + g + 1) * N]
        hs = range(g * per_group, (g + 1) * per_group)
        far = dot(ok, scr[g], ((1,), (0,)))
        ssm = inside_ref[:, cols] + far * spread_lanes([reach[:, h : h + 1] for h in hs], head_size)
        gated = ssm * silu(z_ref[:, cols].astype(f32))
        square = jnp.mean(gated * gated, axis=1, keepdims=True)
        out_ref[g] = (gated * lax.rsqrt(square + EPS) * gain_ref[:, cols]).astype(bf16)


def call(kernel, out_shape, scratch=(), flops=0, moved=0):
    return pl.pallas_call(
        kernel,
        out_shape=out_shape,
        scratch_shapes=list(scratch),
        compiler_params=pltpu.CompilerParams(vmem_limit_bytes=VMEM_LIMIT),
        cost_estimate=pl.CostEstimate(flops=flops, bytes_accessed=moved, transcendentals=0),
    )


def token_norm(stream, gain):
    widened = stream.astype(f32)
    scaled = widened * lax.rsqrt(jnp.mean(widened * widened, axis=-1, keepdims=True) + EPS)
    return (scaled * gain[None, :]).astype(bf16)


def local(
    hidden,
    conv_input,
    z_stream,
    log_decay,
    conv_weight,
    norm_gain,
    out_weight,
    moe_gain,
    routes,
    gate_weights,
    expert_home,
    up_weight,
    down_weight,
):
    n_grp = lax.axis_size("grp")
    devices = lax.axis_size("seq") * n_grp
    plane = 2 * n_grp
    outer = devices // plane
    me = lax.axis_index("seq") * n_grp + lax.axis_index("grp")
    r = lax.rem(me, plane)
    place = lax.div(me, plane)
    rs = r.reshape(1).astype(jnp.int32)

    def swap(x, m):
        return lax.ppermute(x, AXES, [(d, d ^ m) for d in range(devices)])

    def onward(x, by):
        return lax.ppermute(
            x, AXES, [(d, d + by) for d in range(devices) if d + by < devices]
        )

    def turn(x):
        return lax.ppermute(x, AXES, [(d, (d + plane) % devices) for d in range(devices)])

    length, channels = conv_input.shape
    heads = log_decay.shape[0]
    inner = z_stream.shape[1]
    width = inner // G
    model = hidden.shape[1]
    smem = pl.BlockSpec(memory_space=pltpu.SMEM)
    halo = 16

    previous = onward(conv_input[length - halo :], 1)

    per_shard = out_weight.shape[0] // width
    half = out_weight.shape[0] // 2
    side = lax.div(r, n_grp)
    mine_half = lax.dynamic_slice_in_dim(out_weight, side * half, half, 0)
    grp = lax.axis_index("grp")
    cuts = [mine_half[: half // 2], mine_half[half // 2 :]]
    by_x = [swap(c, 2) for c in cuts]
    by_y = [swap(c, n_grp) for c in by_x]
    own_pair = swap(out_weight, 1)
    by_x_pair = [swap(c, 1) for c in by_x]
    by_y_pair = [swap(c, 1) for c in by_y]

    shapes = jax.ShapeDtypeStruct
    chunk = shapes((N + DEC, width), bf16)
    first = pl.pallas_call(
        functools.partial(start_kernel, plane),
        out_shape=[
            shapes((length, channels), bf16),
            shapes((heads, length), f32),
            shapes((length, heads), f32),
        ]
        + [chunk] * plane,
        in_specs=[smem] + [pl.BlockSpec(memory_space=pltpu.VMEM)] * 4,
        scratch_shapes=[pltpu.VMEM((G, N + DEC, width), bf16)],
        compiler_params=pltpu.CompilerParams(vmem_limit_bytes=VMEM_LIMIT),
        cost_estimate=pl.CostEstimate(flops=50000000, bytes_accessed=8000000, transcendentals=0),
    )(rs, conv_input, previous, conv_weight, log_decay)
    active, cum, cumt = first[:3]
    chunks = [first[3]] + [swap(first[3 + m], m) for m in range(1, plane)]

    inside = call(
        inside_kernel, shapes((length, inner), f32), flops=100000000, moved=15000000
    )(active, cum, cumt)

    vm = pl.BlockSpec(memory_space=pltpu.VMEM)
    whole = pl.pallas_call(
        functools.partial(plane_kernel, plane),
        out_shape=chunk,
        in_specs=[smem] + [vm] * plane,
        scratch_shapes=[pltpu.VMEM((plane, N + DEC, width), bf16)],
        compiler_params=pltpu.CompilerParams(vmem_limit_bytes=VMEM_LIMIT),
        cost_estimate=pl.CostEstimate(flops=1000000, bytes_accessed=2000000, transcendentals=0),
    )(rs, *chunks)
    earlier = [onward(whole, plane * k) for k in range(1, outer)]
    entering = pl.pallas_call(
        functools.partial(enter_kernel, plane, outer),
        out_shape=[shapes((N, width), bf16)] * plane,
        in_specs=[smem] + [vm] * (plane + outer - 1),
        scratch_shapes=[
            pltpu.VMEM((plane, N + DEC, width), bf16),
            pltpu.VMEM((plane, N, width), bf16),
        ],
        compiler_params=pltpu.CompilerParams(vmem_limit_bytes=VMEM_LIMIT),
        cost_estimate=pl.CostEstimate(flops=1000000, bytes_accessed=2000000, transcendentals=0),
    )(rs, *chunks, *earlier)
    incoming = [entering[0]] + [swap(entering[m], m) for m in range(1, plane)]
    mixed = pl.pallas_call(
        functools.partial(norm_kernel, plane),
        out_shape=shapes((G, length, width), bf16),
        in_specs=[smem] + [vm] * (5 + plane),
        scratch_shapes=[pltpu.VMEM((G, N, width), bf16)],
        compiler_params=pltpu.CompilerParams(vmem_limit_bytes=VMEM_LIMIT),
        cost_estimate=pl.CostEstimate(flops=40000000, bytes_accessed=6000000, transcendentals=0),
    )(rs, active, cumt, inside, z_stream, norm_gain[None, :], *incoming)

    flat = mixed.transpose(1, 0, 2).reshape(length, inner)
    shard = out_weight.shape[0]

    def project(rows, start):
        part = lax.dynamic_slice_in_dim(flat, start, rows.shape[0], 1)
        return jnp.dot(part, rows, preferred_element_type=f32)

    other = 1 - side
    quarter = half // 2
    total = hidden.astype(f32)
    total = total + project(out_weight, grp * shard) + project(own_pair, (grp ^ 1) * shard)
    for k in range(2):
        total = total + project(by_x[k], (grp ^ 2) * shard + side * half + k * quarter)
        total = total + project(by_x_pair[k], (grp ^ 3) * shard + side * half + k * quarter)
        total = total + project(by_y[k], (grp ^ 2) * shard + other * half + k * quarter)
        total = total + project(by_y_pair[k], (grp ^ 3) * shard + other * half + k * quarter)
    residual_one = total.astype(bf16)
    moe_in = token_norm(residual_one, moe_gain)

    top_count = routes.shape[1]
    capacity = max(2, 3 * length * top_count // (2 * devices))
    experts = expert_home.shape[0]
    picked = routes[:, :, None] == jnp.arange(experts, dtype=jnp.int32)[None, None, :]
    target = jnp.sum(jnp.where(picked, expert_home[None, None, :], 0), axis=2)
    at_device = target[:, :, None] == jnp.arange(devices, dtype=jnp.int32)[None, None, :]
    chosen = jnp.any(at_device, axis=1)
    gates = jnp.sum(jnp.where(at_device, gate_weights[:, :, None], 0.0), axis=1)
    before = (
        lax.broadcasted_iota(jnp.int32, (length, length), 0)
        > lax.broadcasted_iota(jnp.int32, (length, length), 1)
    ).astype(bf16)
    rank = jnp.dot(before, chosen.astype(bf16), preferred_element_type=f32)
    slots = jnp.where(chosen, rank, -1.0)
    gate_high = jnp.floor(gates * 128.0) * (1.0 / 128.0)
    meta = jnp.concatenate([slots, gate_high, gates - gate_high], axis=1).astype(bf16)
    extra = -(-3 * devices // 128) * 128
    meta = jnp.pad(meta, ((0, 0), (0, extra - 3 * devices)))

    up_local = up_weight[0]
    down_local = down_weight[0]
    hops = list(range(0, plane, 2))
    two = 2 * capacity

    def serve(block):
        both = jnp.concatenate([block, swap(block, 1)], axis=0)
        here = both[:, model:]
        ours = lax.dynamic_slice(
            jnp.stack([here[:, :devices], here[:, devices : 2 * devices], here[:, 2 * devices : 3 * devices]]),
            (0, 0, place * plane),
            (3, 2 * length, plane),
        ).astype(f32)
        column = [lax.dynamic_slice_in_dim(ours, r ^ m, 1, 2) for m in hops]
        column = jnp.concatenate(column, axis=2)
        slot = jnp.where(column[0] < 0, -1.0, column[0])
        late = (lax.broadcasted_iota(jnp.int32, slot.shape, 0) >= length) & (slot >= 0)
        slot = slot + jnp.where(late, float(capacity), 0.0)
        gate = column[1] + column[2]
        wanted = slot[:, :, None] == jnp.arange(two, dtype=f32)[None, None, :]
        take = wanted.astype(bf16).reshape(2 * length, len(hops) * two)
        weigh = (
            jnp.where(wanted, gate[:, :, None], 0.0).astype(bf16).reshape(2 * length, len(hops) * two)
        )
        sent = dot(take, both[:, :model], ((0,), (0,))).astype(bf16)
        sent = [sent[k * two : (k + 1) * two] for k in range(len(hops))]
        arrived = [sent[0]] + [swap(sent[k], hops[k]) for k in range(1, len(hops))]
        return weigh, arrived

    def work(arrived):
        rows = jnp.concatenate(arrived, axis=0)
        up = jnp.dot(rows, up_local, preferred_element_type=f32)
        squared = jnp.square(jax.nn.relu(up)).astype(bf16)
        result = jnp.dot(squared, down_local, preferred_element_type=f32).astype(bf16)
        parts = [result[k * two : (k + 1) * two] for k in range(len(hops))]
        return [parts[0]] + [swap(parts[k], hops[k]) for k in range(1, len(hops))]

    def gather_up(weigh, returned):
        part = jnp.dot(weigh, jnp.concatenate(returned, axis=0), preferred_element_type=f32)
        return part[:length] + swap(part[length:].astype(bf16), 1).astype(f32)

    block = jnp.concatenate([moe_in, meta], axis=1)
    blocks = [block]
    for _ in range(outer - 1):
        blocks.append(turn(blocks[-1]))
    served = [serve(b) for b in blocks]
    returned = [work(s[1]) for s in served]
    carried = None
    for step in list(range(1, outer)) + [0]:
        part = gather_up(served[step][0], returned[step])
        if carried is not None:
            part = part + carried.astype(f32)
        if step:
            carried = turn(part.astype(bf16))
    return (residual_one.astype(f32) + part).astype(bf16)


def solution(mesh):
    placed = (
        P(AXES, None),
        P(AXES, None),
        P(AXES, None),
        P(None, AXES),
        P(),
        P(),
        P("grp", None),
        P(),
        P(AXES, None),
        P(AXES, None),
        P(),
        P(AXES, None, None),
        P(AXES, None, None),
    )
    return jax.shard_map(local, mesh=mesh, in_specs=placed, out_specs=P(AXES, None), check_vma=False)
```

```python
import functools

import jax
import jax.numpy as jnp
from jax import lax
from jax.experimental import pallas as pl
from jax.experimental.pallas import tpu as pltpu
from jax.sharding import PartitionSpec as P

AXES = ("seq", "grp")
N = 64
G = 8
EPS = 1e-05
DEC = 16
VMEM_LIMIT = 48 * 1024 * 1024
f32 = jnp.float32
bf16 = jnp.bfloat16


def dot(a, b, contract, precision=None):
    return lax.dot_general(
        a, b, ((contract[0], contract[1]), ((), ())), preferred_element_type=f32, precision=precision
    )


def spread_lanes(columns, width):
    count = len(columns)
    rows = columns[0].shape[0]
    lane = lax.broadcasted_iota(jnp.int32, (rows, count * width), 1)
    out = jnp.broadcast_to(columns[-1], (rows, count * width))
    for j in range(count - 2, -1, -1):
        out = jnp.where(lane < (j + 1) * width, columns[j], out)
    return out


def split_decay(d):
    whole = jnp.floor(d)
    part = d - whole
    coarse = jnp.floor(part * 256.0) * (1.0 / 256.0)
    fine = part - coarse
    row = lax.broadcasted_iota(jnp.int32, (DEC, d.shape[1]), 0)
    rows = jnp.where(row == 0, whole, jnp.where(row == 1, coarse, jnp.where(row == 2, fine, 0.0)))
    return rows.astype(bf16)


def join_decay(rows):
    return jnp.sum(rows.astype(f32), axis=0, keepdims=True)


def silu(x):
    return x * (1.0 / (1.0 + jnp.exp(-x)))


def start_kernel(plane, r_ref, x_ref, prev_ref, cw_ref, ld_ref, act_ref, cum_ref, cumt_ref, *rest):
    outs, scr = rest[:plane], rest[plane]
    length, channels = x_ref.shape
    heads = ld_ref.shape[0]
    per_group = heads // G
    inner = channels - 2 * G * N
    width = inner // G
    head_size = width // per_group
    halo, taps = prev_ref.shape[0], cw_ref.shape[0]
    ld = ld_ref[...]
    low = (
        lax.broadcasted_iota(jnp.int32, (length, length), 0)
        >= lax.broadcasted_iota(jnp.int32, (length, length), 1)
    ).astype(f32)
    cum_ref[...] = dot(ld, low, ((1,), (1,)), lax.Precision.HIGHEST)
    cumt = dot(low, ld, ((1,), (1,)), lax.Precision.HIGHEST)
    cumt_ref[...] = cumt
    last = cumt[length - 1 : length, :]
    to_end = jnp.exp(last - cumt)
    for c in range(0, channels, width):
        cols = slice(c, c + width)
        padded = jnp.concatenate([prev_ref[:, cols], x_ref[:, cols]], axis=0).astype(f32)
        first = halo - taps + 1
        total = cw_ref[0:1, cols] * padded[first : first + length]
        for k in range(1, taps):
            total = total + cw_ref[k : k + 1, cols] * padded[first + k : first + k + length]
        act_ref[:, cols] = silu(total).astype(bf16)
    for g in range(G):
        v = act_ref[:, g * width : (g + 1) * width].astype(f32)
        ik = act_ref[:, inner + g * N : inner + (g + 1) * N]
        hs = range(g * per_group, (g + 1) * per_group)
        weighted = (v * spread_lanes([to_end[:, h : h + 1] for h in hs], head_size)).astype(bf16)
        scr[g, :N, :] = dot(ik, weighted, ((0,), (0,))).astype(bf16)
        scr[g, N:, :] = split_decay(spread_lanes([last[:, h : h + 1] for h in hs], head_size))
    r = r_ref[0]
    for m in range(plane):
        outs[m][...] = scr[r ^ m]


def plane_kernel(plane, r_ref, *rest):
    chunks, out, scr = rest[:plane], rest[plane], rest[plane + 1]
    r = r_ref[0]
    for m in range(plane):
        scr[r ^ m] = chunks[m][...]
    state = jnp.zeros((N, out.shape[1]), f32)
    total = jnp.zeros((1, out.shape[1]), f32)
    for s in range(plane):
        decay = join_decay(scr[s, N:, :])
        state = jnp.exp(decay) * state + scr[s, :N, :].astype(f32)
        total = total + decay
    out[:N, :] = state.astype(bf16)
    out[N:, :] = split_decay(total)


def enter_kernel(plane, outer, r_ref, *rest):
    chunks, earlier = rest[:plane], rest[plane : plane + outer - 1]
    outs, scr, inc = rest[plane + outer - 1 : 2 * plane + outer - 1], rest[-2], rest[-1]
    r = r_ref[0]
    for m in range(plane):
        scr[r ^ m] = chunks[m][...]
    state = jnp.zeros((N, scr.shape[2]), f32)
    passed = jnp.zeros((1, scr.shape[2]), f32)
    for e in earlier:
        state = state + jnp.exp(passed) * e[:N, :].astype(f32)
        passed = passed + join_decay(e[N:, :])
    for s in range(plane):
        inc[s] = state.astype(bf16)
        state = jnp.exp(join_decay(scr[s, N:, :])) * state + scr[s, :N, :].astype(f32)
    for m in range(plane):
        outs[m][...] = inc[r ^ m]


def inside_kernel(act_ref, cum_ref, cumt_ref, out_ref):
    length, channels = act_ref.shape
    heads = cum_ref.shape[0]
    per_group = heads // G
    inner = channels - 2 * G * N
    head_size = inner // heads
    causal = lax.broadcasted_iota(jnp.int32, (length, length), 0) >= lax.broadcasted_iota(
        jnp.int32, (length, length), 1
    )
    cum = cum_ref[...]
    cumt = cumt_ref[...]
    for g in range(G):
        ik = act_ref[:, inner + g * N : inner + (g + 1) * N]
        ok = act_ref[:, inner + (G + g) * N : inner + (G + g + 1) * N]
        meet = jnp.where(causal, dot(ok, ik, ((1,), (1,))), 0.0)
        for h in range(g * per_group, (g + 1) * per_group):
            gap = jnp.where(causal, cumt[:, h : h + 1] - cum[h : h + 1, :], 0.0)
            mixing = (jnp.exp(gap) * meet).astype(bf16)
            cols = slice(h * head_size, (h + 1) * head_size)
            out_ref[:, cols] = dot(mixing, act_ref[:, cols], ((1,), (0,)))


def norm_kernel(plane, n_grp, r_ref, act_ref, cumt_ref, inside_ref, z_ref, gain_ref, *rest):
    incoming, outs = rest[:plane], rest[plane : plane + n_grp // 2]
    scr, mix = rest[-2], rest[-1]
    r, grp = r_ref[0], r_ref[1]
    for m in range(plane):
        scr[r ^ m] = incoming[m][...]
    inner = z_ref.shape[1]
    heads = cumt_ref.shape[1]
    per_group = heads // G
    width = inner // G
    head_size = inner // heads
    per_shard = G // n_grp
    reach = jnp.exp(cumt_ref[...])
    for g in range(G):
        cols = slice(g * width, (g + 1) * width)
        ok = act_ref[:, inner + (G + g) * N : inner + (G + g + 1) * N]
        hs = range(g * per_group, (g + 1) * per_group)
        far = dot(ok, scr[g], ((1,), (0,)))
        ssm = inside_ref[:, cols] + far * spread_lanes([reach[:, h : h + 1] for h in hs], head_size)
        gated = ssm * silu(z_ref[:, cols].astype(f32))
        square = jnp.mean(gated * gated, axis=1, keepdims=True)
        mix[((g // per_shard) ^ grp) * per_shard + g % per_shard] = (
            gated * lax.rsqrt(square + EPS) * gain_ref[:, cols]
        ).astype(bf16)
    for j in range(G):
        k, at = j // (2 * per_shard), j % (2 * per_shard)
        outs[k][:, at * width : (at + 1) * width] = mix[j]


def dispatch_kernel(plane, devices, capacity, pieces, at_ref, own_ref, *rest):
    pair_refs, outs, weigh_ref = rest[:pieces], rest[pieces:-1], rest[-1]
    length, model = own_ref.shape[0], outs[0].shape[1]
    rows = outs[0].shape[0]
    lanes = len(outs) * rows
    device = lax.broadcasted_iota(jnp.int32, (devices, lanes), 0)
    lane = lax.broadcasted_iota(jnp.int32, (devices, lanes), 1)
    wanted = jnp.zeros((devices, lanes), jnp.int32)
    start = lax.broadcasted_iota(jnp.int32, (length, lanes), 1)
    for k in range(len(outs)):
        inside = (lane >= k * rows) & (lane < (k + 1) * rows)
        wanted = jnp.where(inside, at_ref[1] + (at_ref[0] ^ (2 * k)), wanted)
    place = start
    for k in range(1, len(outs)):
        place = jnp.where(start >= k * rows, start - k * rows, place)
    place = place.astype(f32)
    select = (device == wanted).astype(f32).astype(bf16)
    total = None
    first = 0
    for ref in (own_ref,) + pair_refs:
        b, count = (0 if first < length else 1), ref.shape[0]
        slot = dot(ref[:, model : model + devices], select, ((1,), (0,)))
        gate = dot(ref[:, model + devices : model + 2 * devices], select, ((1,), (0,))) + dot(
            ref[:, model + 2 * devices : model + 3 * devices], select, ((1,), (0,))
        )
        hit = (slot >= 0.0) & (slot + float(b * capacity) == place[:count])
        weigh_ref[first : first + count, :] = jnp.where(hit, gate, 0.0).astype(bf16)
        take = jnp.where(hit, 1.0, 0.0).astype(bf16)
        part = dot(take, ref[:, :model], ((0,), (0,)))
        total = part if total is None else total + part
        first += count
    for k in range(len(outs)):
        outs[k][...] = total[k * rows : (k + 1) * rows].astype(bf16)


def after(x, *others):
    return lax.optimization_barrier((x,) + others)[0]


def call(kernel, out_shape, scratch=(), flops=0, moved=0):
    return pl.pallas_call(
        kernel,
        out_shape=out_shape,
        scratch_shapes=list(scratch),
        compiler_params=pltpu.CompilerParams(vmem_limit_bytes=VMEM_LIMIT),
        cost_estimate=pl.CostEstimate(flops=flops, bytes_accessed=moved, transcendentals=0),
    )


def token_norm(stream, gain):
    widened = stream.astype(f32)
    scaled = widened * lax.rsqrt(jnp.mean(widened * widened, axis=-1, keepdims=True) + EPS)
    return (scaled * gain[None, :]).astype(bf16)


def local(
    hidden,
    conv_input,
    z_stream,
    log_decay,
    conv_weight,
    norm_gain,
    out_weight,
    moe_gain,
    routes,
    gate_weights,
    expert_home,
    up_weight,
    down_weight,
):
    n_grp = lax.axis_size("grp")
    devices = lax.axis_size("seq") * n_grp
    plane = 2 * n_grp
    outer = devices // plane
    me = lax.axis_index("seq") * n_grp + lax.axis_index("grp")
    r = lax.rem(me, plane)
    place = lax.div(me, plane)
    rs = r.reshape(1).astype(jnp.int32)

    def swap(x, m):
        return lax.ppermute(x, AXES, [(d, d ^ m) for d in range(devices)])

    def onward(x, by):
        return lax.ppermute(
            x, AXES, [(d, d + by) for d in range(devices) if d + by < devices]
        )

    def turn(x):
        return lax.ppermute(x, AXES, [(d, (d + plane) % devices) for d in range(devices)])

    length, channels = conv_input.shape
    heads = log_decay.shape[0]
    inner = z_stream.shape[1]
    width = inner // G
    model = hidden.shape[1]
    smem = pl.BlockSpec(memory_space=pltpu.SMEM)
    halo = 16

    previous = onward(conv_input[length - halo :], 1)

    grp = lax.axis_index("grp")
    rows_own = out_weight
    rows_pair = swap(out_weight, 1)
    shard = out_weight.shape[0]
    groups_shard = shard // width

    shapes = jax.ShapeDtypeStruct
    chunk = shapes((N + DEC, width), bf16)
    first = pl.pallas_call(
        functools.partial(start_kernel, plane),
        out_shape=[
            shapes((length, channels), bf16),
            shapes((heads, length), f32),
            shapes((length, heads), f32),
        ]
        + [chunk] * plane,
        in_specs=[smem] + [pl.BlockSpec(memory_space=pltpu.VMEM)] * 4,
        scratch_shapes=[pltpu.VMEM((G, N + DEC, width), bf16)],
        compiler_params=pltpu.CompilerParams(vmem_limit_bytes=VMEM_LIMIT),
        cost_estimate=pl.CostEstimate(flops=50000000, bytes_accessed=8000000, transcendentals=0),
    )(rs, conv_input, previous, conv_weight, log_decay)
    active, cum, cumt = first[:3]
    chunks = [first[3]] + [swap(first[3 + m], m) for m in range(1, plane)]

    inside = call(
        inside_kernel, shapes((length, inner), f32), flops=100000000, moved=15000000
    )(active, cum, cumt)

    vm = pl.BlockSpec(memory_space=pltpu.VMEM)
    whole = pl.pallas_call(
        functools.partial(plane_kernel, plane),
        out_shape=chunk,
        in_specs=[smem] + [vm] * plane,
        scratch_shapes=[pltpu.VMEM((plane, N + DEC, width), bf16)],
        compiler_params=pltpu.CompilerParams(vmem_limit_bytes=VMEM_LIMIT),
        cost_estimate=pl.CostEstimate(flops=1000000, bytes_accessed=2000000, transcendentals=0),
    )(rs, *chunks)
    earlier = [onward(whole, plane * k) for k in range(1, outer)]
    entering = pl.pallas_call(
        functools.partial(enter_kernel, plane, outer),
        out_shape=[shapes((N, width), bf16)] * plane,
        in_specs=[smem] + [vm] * (plane + outer - 1),
        scratch_shapes=[
            pltpu.VMEM((plane, N + DEC, width), bf16),
            pltpu.VMEM((plane, N, width), bf16),
        ],
        compiler_params=pltpu.CompilerParams(vmem_limit_bytes=VMEM_LIMIT),
        cost_estimate=pl.CostEstimate(flops=1000000, bytes_accessed=2000000, transcendentals=0),
    )(rs, *chunks, *earlier)
    incoming = [entering[0]] + [swap(entering[m], m) for m in range(1, plane)]
    split = pl.pallas_call(
        functools.partial(norm_kernel, plane, n_grp),
        out_shape=[shapes((length, 2 * shard), bf16)] * (n_grp // 2),
        in_specs=[smem] + [vm] * (5 + plane),
        scratch_shapes=[
            pltpu.VMEM((G, N, width), bf16),
            pltpu.VMEM((n_grp * groups_shard, length, width), bf16),
        ],
        compiler_params=pltpu.CompilerParams(vmem_limit_bytes=VMEM_LIMIT),
        cost_estimate=pl.CostEstimate(flops=40000000, bytes_accessed=6000000, transcendentals=0),
    )(jnp.stack([r, grp]).astype(jnp.int32), active, cumt, inside, z_stream, norm_gain[None, :], *incoming)

    def project(part):
        return jnp.dot(part[:, :shard], rows_own, preferred_element_type=f32) + jnp.dot(
            part[:, shard:], rows_pair, preferred_element_type=f32
        )

    fars = [swap(split[k], 2 * k) for k in range(1, n_grp // 2)]
    total = hidden.astype(f32) + project(split[0])
    for k in range(1, n_grp // 2):
        total = total + swap(project(fars[k - 1]).astype(bf16), 2 * k).astype(f32)
    residual_one = total.astype(bf16)
    moe_in = token_norm(residual_one, moe_gain)

    top_count = routes.shape[1]
    capacity = max(2, 3 * length * top_count // (2 * devices))
    experts = expert_home.shape[0]
    picked = routes[:, :, None] == jnp.arange(experts, dtype=jnp.int32)[None, None, :]
    target = jnp.sum(jnp.where(picked, expert_home[None, None, :], 0), axis=2)
    at_device = target[:, :, None] == jnp.arange(devices, dtype=jnp.int32)[None, None, :]
    chosen = jnp.any(at_device, axis=1)
    gates = jnp.sum(jnp.where(at_device, gate_weights[:, :, None], 0.0), axis=1)
    before = (
        lax.broadcasted_iota(jnp.int32, (length, length), 0)
        > lax.broadcasted_iota(jnp.int32, (length, length), 1)
    ).astype(bf16)
    rank = jnp.dot(before, chosen.astype(bf16), preferred_element_type=f32)
    slots = jnp.where(chosen, rank, -1.0)
    gate_high = jnp.floor(gates * 128.0) * (1.0 / 128.0)
    meta = jnp.concatenate([slots, gate_high, gates - gate_high], axis=1).astype(bf16)
    extra = -(-3 * devices // 128) * 128
    meta = jnp.pad(meta, ((0, 0), (0, extra - 3 * devices)))

    up_local = up_weight[0]
    down_local = down_weight[0]
    hops = list(range(0, plane, 2))
    two = -(-2 * capacity // 8) * 8

    at = jnp.stack([r, place * plane]).astype(jnp.int32)

    def serve(block, pair):
        out = pl.pallas_call(
            functools.partial(dispatch_kernel, plane, devices, capacity, len(pair)),
            out_shape=[shapes((two, model), bf16)] * len(hops)
            + [shapes((2 * length, len(hops) * two), bf16)],
            in_specs=[smem, vm] + [vm] * len(pair),
            compiler_params=pltpu.CompilerParams(vmem_limit_bytes=VMEM_LIMIT),
            cost_estimate=pl.CostEstimate(flops=0, bytes_accessed=0, transcendentals=0),
        )(at, block, *pair)
        sent = out[:-1]
        return out[-1], [sent[0]] + [swap(sent[k], hops[k]) for k in range(1, len(hops))], sent

    def work(arrived):
        rows = jnp.concatenate(arrived, axis=0)
        up = jnp.dot(rows, up_local, preferred_element_type=f32)
        squared = jnp.square(jax.nn.relu(up)).astype(bf16)
        return jnp.dot(squared, down_local, preferred_element_type=f32).astype(bf16)

    def send_back(result):
        parts = [result[k * two : (k + 1) * two] for k in range(len(hops))]
        return [parts[0]] + [swap(parts[k], hops[k]) for k in range(1, len(hops))]

    def gather_up(weigh, returned):
        part = jnp.dot(weigh, jnp.concatenate(returned, axis=0), preferred_element_type=f32)
        return part[:length] + swap(part[length:].astype(bf16), 1).astype(f32)

    block = jnp.concatenate([moe_in, meta], axis=1)
    weighs, results, returned = {}, {}, {}
    arrived = {}
    for step in range(outer):
        pair = [swap(block[: length // 2], 1), swap(block[length // 2 :], 1)]
        if step >= 2:
            pair[0] = after(pair[0], results[step - 2])
        weighs[step], arrived[step], sent = serve(block, pair)
        if step + 1 < outer:
            block = turn(after(block, weighs[step]))
        if step >= 1:
            results[step - 1] = work(arrived[step - 1])
            if step >= 2:
                returned[step - 1] = send_back(results[step - 1])
    results[outer - 1] = work(arrived[outer - 1])
    if outer > 1:
        returned[outer - 1] = send_back(results[outer - 1])
    returned[0] = send_back(after(results[0], results[outer - 1]))
    carried = None
    for step in list(range(1, outer)) + [0]:
        back = returned[step]
        if carried is not None and step == 0:
            back = [after(back[0], carried)] + back[1:]
        part = gather_up(weighs[step], back)
        if carried is not None:
            part = part + carried.astype(f32)
        if step:
            carried = turn(part.astype(bf16))
    return (residual_one.astype(f32) + part).astype(bf16)


def solution(mesh):
    placed = (
        P(AXES, None),
        P(AXES, None),
        P(AXES, None),
        P(None, AXES),
        P(),
        P(),
        P("grp", None),
        P(),
        P(AXES, None),
        P(AXES, None),
        P(),
        P(AXES, None, None),
        P(AXES, None, None),
    )
    return jax.shard_map(local, mesh=mesh, in_specs=placed, out_specs=P(AXES, None), check_vma=False)
```

```python
import functools

import jax
import jax.numpy as jnp
from jax import lax
from jax.experimental import pallas as pl
from jax.experimental.pallas import tpu as pltpu
from jax.sharding import PartitionSpec as P

AXES = ("seq", "grp")
N = 64
G = 8
EPS = 1e-05
DEC = 16
VMEM_LIMIT = 24 * 1024 * 1024
f32 = jnp.float32
bf16 = jnp.bfloat16


def dot(a, b, contract, precision=None):
    return lax.dot_general(
        a, b, ((contract[0], contract[1]), ((), ())), preferred_element_type=f32, precision=precision
    )


def spread_lanes(columns, width):
    count = len(columns)
    rows = columns[0].shape[0]
    lane = lax.broadcasted_iota(jnp.int32, (rows, count * width), 1)
    out = jnp.broadcast_to(columns[-1], (rows, count * width))
    for j in range(count - 2, -1, -1):
        out = jnp.where(lane < (j + 1) * width, columns[j], out)
    return out


def split_decay(d):
    whole = jnp.floor(d)
    part = d - whole
    coarse = jnp.floor(part * 256.0) * (1.0 / 256.0)
    fine = part - coarse
    row = lax.broadcasted_iota(jnp.int32, (DEC, d.shape[1]), 0)
    rows = jnp.where(row == 0, whole, jnp.where(row == 1, coarse, jnp.where(row == 2, fine, 0.0)))
    return rows.astype(bf16)


def join_decay(rows):
    return jnp.sum(rows.astype(f32), axis=0, keepdims=True)


def silu(x):
    return x * (1.0 / (1.0 + jnp.exp(-x)))


def columns(blocks, inner, keys, c, width, which):
    start, first = 0, 0
    for extent in (inner, keys, keys):
        size = extent // blocks
        if c < first + size:
            return pl.ds(pl.multiple_of(start + which * size + (c - first), width), width)
        start, first = start + extent, first + size


def pick_kernel(blocks, inner, width, at_ref, x_ref, tail_ref, *outs):
    half = at_ref[1]
    length, channels = x_ref.shape
    keys = (channels - inner) // 2
    tail_ref[...] = x_ref[length - tail_ref.shape[0] :, :]
    for b in range(1, blocks):
        for c in range(0, channels // blocks, width):
            outs[b - 1][:, c : c + width] = x_ref[
                :, columns(blocks, inner, keys, c, width, half ^ b)
            ]


def running(ld):
    length = ld.shape[1]
    low = (
        lax.broadcasted_iota(jnp.int32, (length, length), 0)
        >= lax.broadcasted_iota(jnp.int32, (length, length), 1)
    ).astype(f32)
    return (
        dot(ld, low, ((1,), (1,)), lax.Precision.HIGHEST),
        dot(low, ld, ((1,), (1,)), lax.Precision.HIGHEST),
    )


def start_kernel(members, blocks, at_ref, cw_ref, z_ref, *rest):
    xs, prevs, lds = rest[:blocks], rest[blocks : 2 * blocks], rest[2 * blocks : 3 * blocks]
    rest = rest[3 * blocks :]
    acts, outs, scr = rest[:blocks], rest[blocks : blocks + members], rest[-1]
    z_outs = rest[blocks + members : -1]
    member, half = at_ref[0], at_ref[1]
    length = xs[0].shape[0]
    channels = xs[0].shape[1] // blocks
    heads = lds[0].shape[0] // blocks
    count = scr.shape[0]
    per_group = heads // count
    inner = channels - 2 * count * N
    width = inner // count
    head_size = width // per_group
    halo, taps = prevs[0].shape[0], cw_ref.shape[0]
    for b in range(blocks):
        ld = lds[b][pl.ds(pl.multiple_of(half * heads, heads), heads), :]
        cumt = running(ld)[1]
        last = cumt[length - 1 : length, :]
        to_end = jnp.exp(last - cumt)
        act_ref = acts[b]
        for c in range(0, channels, width):
            cols = slice(c, c + width)
            at = columns(blocks, inner * blocks, count * N * blocks, c, width, half)
            padded = jnp.concatenate(
                [prevs[b][:, at], xs[b][:, cols if b else at]], axis=0
            ).astype(f32)
            first = halo - taps + 1
            total = cw_ref[0:1, at] * padded[first : first + length]
            for k in range(1, taps):
                total = total + cw_ref[k : k + 1, at] * padded[first + k : first + k + length]
            act_ref[:, cols] = silu(total).astype(bf16)
        slot = half ^ b
        for g in range(count):
            v = act_ref[:, g * width : (g + 1) * width].astype(f32)
            ik = act_ref[:, inner + g * N : inner + (g + 1) * N]
            hs = range(g * per_group, (g + 1) * per_group)
            weighted = (v * spread_lanes([to_end[:, h : h + 1] for h in hs], head_size)).astype(bf16)
            scr[g, slot, :N, :] = dot(ik, weighted, ((0,), (0,))).astype(bf16)
            scr[g, slot, N:, :] = split_decay(
                spread_lanes([last[:, h : h + 1] for h in hs], head_size)
            )
    for m in range(members):
        outs[m][...] = scr[member ^ m]
    for b in range(1, blocks):
        for c in range(0, inner, width):
            at = pl.ds(pl.multiple_of((half ^ b) * inner + c, width), width)
            z_outs[b - 1][:, c : c + width] = z_ref[:, at]


def in_order(members, blocks, member, chunks, scr):
    for m in range(members):
        who = member ^ m
        for k in range(blocks):
            scr[(who >> 1) * 2 * blocks + 2 * k + (who & 1)] = chunks[m][k]


def plane_kernel(members, blocks, at_ref, *rest):
    chunks, out, scr = rest[:members], rest[members], rest[members + 1]
    in_order(members, blocks, at_ref[0], chunks, scr)
    state = jnp.zeros((N, out.shape[1]), f32)
    total = jnp.zeros((1, out.shape[1]), f32)
    for s in range(members * blocks):
        decay = join_decay(scr[s, N:, :])
        state = jnp.exp(decay) * state + scr[s, :N, :].astype(f32)
        total = total + decay
    out[:N, :] = state.astype(bf16)
    out[N:, :] = split_decay(total)


def pair_kernel(stage, at_ref, own_ref, other_ref, out_ref):
    later = ((at_ref[3] >> stage) & 1) == 1
    own, other = own_ref[:N, :].astype(f32), other_ref[:N, :].astype(f32)
    own_decay, other_decay = join_decay(own_ref[N:, :]), join_decay(other_ref[N:, :])
    first, second = jnp.where(later, other, own), jnp.where(later, own, other)
    out_ref[:N, :] = (jnp.exp(jnp.where(later, own_decay, other_decay)) * first + second).astype(bf16)
    out_ref[N:, :] = split_decay(own_decay + other_decay)


def enter_kernel(members, blocks, stages, at_ref, scr, *rest):
    earlier, outs, inc = rest[:stages], rest[stages : stages + members], rest[-1]
    member = at_ref[0]
    state = jnp.zeros((N, scr.shape[2]), f32)
    for stage in range(stages - 1, -1, -1):
        e = earlier[stage]
        joined = jnp.exp(join_decay(e[N:, :])) * state + e[:N, :].astype(f32)
        state = jnp.where(((at_ref[3] >> stage) & 1) == 1, joined, state)
    for s in range(members * blocks):
        inc[s] = state.astype(bf16)
        state = jnp.exp(join_decay(scr[s, N:, :])) * state + scr[s, :N, :].astype(f32)
    for m in range(members):
        who = member ^ m
        for k in range(blocks):
            outs[m][k] = inc[(who >> 1) * 2 * blocks + 2 * k + (who & 1)]


def inside_kernel(count, blocks, at_ref, *refs):
    acts, lds, outs = (refs[k * blocks : (k + 1) * blocks] for k in range(3))
    length, channels = acts[0].shape
    heads = lds[0].shape[0] // blocks
    per_group = heads // count
    inner = channels - 2 * count * N
    head_size = inner // heads
    causal = lax.broadcasted_iota(jnp.int32, (length, length), 0) >= lax.broadcasted_iota(
        jnp.int32, (length, length), 1
    )
    for b in range(blocks):
        act_ref, out_ref = acts[b], outs[b]
        cum, cumt = running(lds[b][pl.ds(pl.multiple_of(at_ref[1] * heads, heads), heads), :])
        for g in range(count):
            ik = act_ref[:, inner + g * N : inner + (g + 1) * N]
            ok = act_ref[:, inner + (count + g) * N : inner + (count + g + 1) * N]
            meet = jnp.where(causal, dot(ok, ik, ((1,), (1,))), 0.0)
            for h in range(g * per_group, (g + 1) * per_group):
                gap = jnp.where(causal, cumt[:, h : h + 1] - cum[h : h + 1, :], 0.0)
                mixing = (jnp.exp(gap) * meet).astype(bf16)
                cols = slice(h * head_size, (h + 1) * head_size)
                out_ref[:, cols] = dot(mixing, act_ref[:, cols], ((1,), (0,)))


def norm_kernel(members, blocks, b, at_ref, gain_ref, act_ref, ld_ref, inside_ref, z_ref, *rest):
    incoming, own_ref, pair_ref = rest[:members], rest[members], rest[members + 1]
    out_ref, scr, mix = rest[-3], rest[-2], rest[-1]
    member, half, core = at_ref[0], at_ref[1], at_ref[2]
    for m in range(members):
        scr[member ^ m] = incoming[m][...]
    inner = z_ref.shape[1] if b else z_ref.shape[1] // blocks
    heads = ld_ref.shape[0] // blocks
    count = scr.shape[0]
    per_group = heads // count
    width = inner // count
    head_size = inner // heads
    shard = count // 2
    reach = jnp.exp(running(ld_ref[pl.ds(pl.multiple_of(half * heads, heads), heads), :])[1])
    slot = half ^ b
    for g in range(count):
        cols = slice(g * width, (g + 1) * width)
        ok = act_ref[:, inner + (count + g) * N : inner + (count + g + 1) * N]
        hs = range(g * per_group, (g + 1) * per_group)
        far = dot(ok, scr[g, slot], ((1,), (0,)))
        ssm = inside_ref[:, cols] + far * spread_lanes([reach[:, h : h + 1] for h in hs], head_size)
        at = pl.ds(pl.multiple_of(half * inner + g * width, width), width)
        gated = ssm * silu(z_ref[:, cols if b else at].astype(f32))
        square = jnp.mean(gated * gated, axis=1, keepdims=True)
        mix[((g // shard) ^ core) * shard + g % shard] = (
            gated * lax.rsqrt(square + EPS) * gain_ref[:, at]
        ).astype(bf16)
    model = out_ref.shape[1]
    tile = 384 if model % 384 == 0 else model
    for c in range(0, model, tile):
        total = None
        for g in range(count):
            rows = (own_ref, pair_ref)[g // shard]
            at = (g % shard) * width
            part = dot(mix[g], rows[at : at + width, c : c + tile], ((1,), (0,)))
            total = part if total is None else total + part
        out_ref[:, c : c + tile] = total.astype(out_ref.dtype)


def token_kernel(blocks, gain_ref, hidden_ref, own_ref, meta_ref, *rest):
    others, residual_ref, block_ref = rest[: blocks - 1], rest[blocks - 1], rest[blocks]
    model = hidden_ref.shape[1]
    total = hidden_ref[...].astype(f32) + own_ref[...]
    for other in others:
        total = total + other[...].astype(f32)
    residual = total.astype(bf16)
    residual_ref[...] = residual
    wide = residual.astype(f32)
    square = jnp.mean(wide * wide, axis=1, keepdims=True)
    block_ref[:, :model] = (wide * lax.rsqrt(square + EPS) * gain_ref[...]).astype(bf16)
    block_ref[:, model:] = meta_ref[...]


def dispatch_kernel(plane, devices, capacity, pieces, at_ref, own_ref, *rest):
    pair_refs, outs, weigh_ref = rest[:pieces], rest[pieces:-1], rest[-1]
    length, model = own_ref.shape[0], outs[0].shape[1]
    rows = outs[0].shape[0]
    lanes = len(outs) * rows
    device = lax.broadcasted_iota(jnp.int32, (devices, lanes), 0)
    lane = lax.broadcasted_iota(jnp.int32, (devices, lanes), 1)
    wanted = jnp.zeros((devices, lanes), jnp.int32)
    start = lax.broadcasted_iota(jnp.int32, (length, lanes), 1)
    for k in range(len(outs)):
        inside = (lane >= k * rows) & (lane < (k + 1) * rows)
        wanted = jnp.where(inside, at_ref[1] + (at_ref[0] ^ (2 * k)), wanted)
    place = start
    for k in range(1, len(outs)):
        place = jnp.where(start >= k * rows, start - k * rows, place)
    place = place.astype(f32)
    select = (device == wanted).astype(f32).astype(bf16)
    total = None
    first = 0
    for ref in (own_ref,) + pair_refs:
        b, count = (0 if first < length else 1), ref.shape[0]
        slot = dot(ref[:, model : model + devices], select, ((1,), (0,)))
        gate = dot(ref[:, model + devices : model + 2 * devices], select, ((1,), (0,))) + dot(
            ref[:, model + 2 * devices : model + 3 * devices], select, ((1,), (0,))
        )
        hit = (slot >= 0.0) & (slot + float(b * capacity) == place[:count])
        weigh_ref[first : first + count, :] = jnp.where(hit, gate, 0.0).astype(bf16)
        take = jnp.where(hit, 1.0, 0.0).astype(bf16)
        part = dot(take, ref[:, :model], ((0,), (0,)))
        total = part if total is None else total + part
        first += count
    for k in range(len(outs)):
        outs[k][...] = total[k * rows : (k + 1) * rows].astype(bf16)


def after(x, *others):
    return lax.optimization_barrier((x,) + others)[0]


def local(
    hidden,
    conv_input,
    z_stream,
    log_decay,
    conv_weight,
    norm_gain,
    out_weight,
    moe_gain,
    routes,
    gate_weights,
    expert_home,
    up_weight,
    down_weight,
):
    n_grp = lax.axis_size("grp")
    devices = lax.axis_size("seq") * n_grp
    plane = 2 * n_grp
    outer = devices // plane
    me = lax.axis_index("seq") * n_grp + lax.axis_index("grp")
    r = lax.rem(me, plane)
    place = lax.div(me, plane)

    def swap(x, m):
        return lax.ppermute(x, AXES, [(d, d ^ m) for d in range(devices)])

    def onward(x, by):
        return lax.ppermute(
            x, AXES, [(d, d + by) for d in range(devices) if d + by < devices]
        )

    def turn(x):
        return lax.ppermute(x, AXES, [(d, (d + plane) % devices) for d in range(devices)])

    length, channels = conv_input.shape
    inner = z_stream.shape[1]
    width = inner // G
    model = hidden.shape[1]
    smem = pl.BlockSpec(memory_space=pltpu.SMEM)
    halo = 16

    blocks = n_grp // 2
    members = plane // blocks
    grp = lax.axis_index("grp")
    half = lax.div(grp, 2)
    core = lax.rem(grp, 2)
    member = lax.div(r, n_grp) * 2 + core
    at_member = jnp.stack([member, half, core, place]).astype(jnp.int32)
    count = G // blocks

    def onward_to(x, by, m):
        return lax.ppermute(
            x, AXES, [(d, (d + by) ^ m) for d in range(devices) if d + by < devices]
        )

    shapes = jax.ShapeDtypeStruct
    vm = pl.BlockSpec(memory_space=pltpu.VMEM)
    wide = channels // blocks
    chunk = (N + DEC, width)

    def kernel_call(kernel, inputs, outs, scratch=(), flops=0, moved=0, scalars=True):
        return pl.pallas_call(
            kernel,
            out_shape=outs,
            in_specs=([smem] if scalars else []) + [vm] * (len(inputs) - (1 if scalars else 0)),
            scratch_shapes=list(scratch),
            compiler_params=pltpu.CompilerParams(vmem_limit_bytes=VMEM_LIMIT),
            cost_estimate=pl.CostEstimate(flops=flops, bytes_accessed=moved, transcendentals=0),
        )(*inputs)

    picked = kernel_call(
        functools.partial(pick_kernel, blocks, inner, width),
        [at_member, conv_input],
        [shapes((halo, channels), bf16)] + [shapes((length, wide), bf16)] * (blocks - 1),
    )
    tail = picked[0]
    xs, prevs, lds = [conv_input], [onward_to(tail, 1, 0)], [log_decay]
    for b in range(1, blocks):
        xs.append(swap(picked[b], 2 * b))
        prevs.append(onward_to(tail, 1, 2 * b))
        lds.append(swap(log_decay, 2 * b))

    rows_own = out_weight
    rows_pair = swap(out_weight, 1)
    shard = out_weight.shape[0]

    first = kernel_call(
        functools.partial(start_kernel, members, blocks),
        [at_member, conv_weight, z_stream] + xs + prevs + lds,
        [shapes((length, wide), bf16)] * blocks
        + [shapes((blocks,) + chunk, bf16)] * members
        + [shapes((length, inner // blocks), bf16)] * (blocks - 1),
        [pltpu.VMEM((count, blocks) + chunk, bf16)],
        50000000,
        8000000,
    )
    acts = first[:blocks]
    sends = first[blocks : blocks + members]
    zs = [z_stream] + [swap(first[blocks + members + b - 1], 2 * b) for b in range(1, blocks)]
    mask = [(m >> 1) * n_grp + (m & 1) for m in range(members)]
    chunks = [sends[0]] + [swap(sends[m], mask[m]) for m in range(1, members)]
    inside = kernel_call(
        functools.partial(inside_kernel, count, blocks),
        [at_member] + list(acts) + lds,
        [shapes((length, inner // blocks), f32)] * blocks,
        (),
        100000000,
        15000000,
    )
    whole, ordered = kernel_call(
        functools.partial(plane_kernel, members, blocks),
        [at_member] + chunks,
        [shapes(chunk, bf16), shapes((plane,) + chunk, bf16)],
    )
    earlier, stage = [], 0
    while (1 << stage) < outer:
        earlier.append(swap(whole, plane << stage))
        stage += 1
        if (1 << stage) < outer:
            whole = kernel_call(
                functools.partial(pair_kernel, stage - 1),
                [at_member, whole, earlier[-1]],
                shapes(chunk, bf16),
            )
    entering = kernel_call(
        functools.partial(enter_kernel, members, blocks, stage),
        [at_member, ordered] + earlier,
        [shapes((blocks, N, width), bf16)] * members,
        [pltpu.VMEM((plane, N, width), bf16)],
        1000000,
        2000000,
    )
    incoming = [entering[0]] + [swap(entering[m], mask[m]) for m in range(1, members)]
    def project(b):
        return kernel_call(
            functools.partial(norm_kernel, members, blocks, b),
            [at_member, norm_gain[None, :], acts[b], lds[b], inside[b], zs[b]]
            + incoming
            + [rows_own, rows_pair],
            shapes((length, model), bf16 if b else f32),
            [pltpu.VMEM((count, blocks, N, width), bf16), pltpu.VMEM((count, length, width), bf16)],
            800000000,
            8000000,
        )

    others = [swap(project(b), 2 * b) for b in range(1, blocks)]
    mine = project(0)

    top_count = routes.shape[1]
    capacity = max(2, 3 * length * top_count // (2 * devices))
    experts = expert_home.shape[0]
    picked = routes[:, :, None] == jnp.arange(experts, dtype=jnp.int32)[None, None, :]
    target = jnp.sum(jnp.where(picked, expert_home[None, None, :], 0), axis=2)
    at_device = target[:, :, None] == jnp.arange(devices, dtype=jnp.int32)[None, None, :]
    chosen = jnp.any(at_device, axis=1)
    gates = jnp.sum(jnp.where(at_device, gate_weights[:, :, None], 0.0), axis=1)
    before = (
        lax.broadcasted_iota(jnp.int32, (length, length), 0)
        > lax.broadcasted_iota(jnp.int32, (length, length), 1)
    ).astype(bf16)
    rank = jnp.dot(before, chosen.astype(bf16), preferred_element_type=f32)
    slots = jnp.where(chosen, rank, -1.0)
    gate_high = jnp.floor(gates * 128.0) * (1.0 / 128.0)
    meta = jnp.concatenate([slots, gate_high, gates - gate_high], axis=1).astype(bf16)
    extra = -(-3 * devices // 128) * 128
    meta = jnp.pad(meta, ((0, 0), (0, extra - 3 * devices)))

    up_local = up_weight[0]
    down_local = down_weight[0]
    hops = list(range(0, plane, 2))
    two = -(-2 * capacity // 8) * 8

    at = jnp.stack([r, place * plane]).astype(jnp.int32)

    def serve(block, pair):
        out = pl.pallas_call(
            functools.partial(dispatch_kernel, plane, devices, capacity, len(pair)),
            out_shape=[shapes((two, model), bf16)] * len(hops)
            + [shapes((2 * length, len(hops) * two), bf16)],
            in_specs=[smem, vm] + [vm] * len(pair),
            compiler_params=pltpu.CompilerParams(vmem_limit_bytes=VMEM_LIMIT),
            cost_estimate=pl.CostEstimate(flops=0, bytes_accessed=0, transcendentals=0),
        )(at, block, *pair)
        sent = out[:-1]
        return out[-1], [sent[0]] + [swap(sent[k], hops[k]) for k in range(1, len(hops))], sent

    def work(arrived):
        rows = jnp.concatenate(arrived, axis=0)
        up = jnp.dot(rows, up_local, preferred_element_type=f32)
        squared = jnp.square(jax.nn.relu(up)).astype(bf16)
        return jnp.dot(squared, down_local, preferred_element_type=f32).astype(bf16)

    def send_back(result):
        parts = [result[k * two : (k + 1) * two] for k in range(len(hops))]
        return [parts[0]] + [swap(parts[k], hops[k]) for k in range(1, len(hops))]

    def gather_up(weigh, returned):
        part = jnp.dot(weigh, jnp.concatenate(returned, axis=0), preferred_element_type=f32)
        return part[:length] + swap(part[length:].astype(bf16), 1).astype(f32)

    residual_one, block = kernel_call(
        functools.partial(token_kernel, blocks),
        [moe_gain[None, :], hidden, mine, meta] + others,
        [shapes((length, model), bf16), shapes((length, model + extra), bf16)],
        scalars=False,
    )
    weighs, results, returned = {}, {}, {}
    arrived = {}
    for step in range(outer):
        pair = [swap(block[: length // 2], 1), swap(block[length // 2 :], 1)]
        if step >= 2:
            pair[0] = after(pair[0], results[step - 2])
        weighs[step], arrived[step], sent = serve(block, pair)
        if step + 1 < outer:
            block = turn(after(block, weighs[step]))
        if step >= 1:
            results[step - 1] = work(arrived[step - 1])
            if step >= 2:
                returned[step - 1] = send_back(results[step - 1])
    results[outer - 1] = work(arrived[outer - 1])
    if outer > 1:
        returned[outer - 1] = send_back(results[outer - 1])
    returned[0] = send_back(after(results[0], results[outer - 1]))
    carried = None
    for step in list(range(1, outer)) + [0]:
        back = returned[step]
        if carried is not None and step == 0:
            back = [after(back[0], carried)] + back[1:]
        part = gather_up(weighs[step], back)
        if carried is not None:
            part = part + carried.astype(f32)
        if step:
            carried = turn(part.astype(bf16))
    return (residual_one.astype(f32) + part).astype(bf16)


def solution(mesh):
    placed = (
        P(AXES, None),
        P(AXES, None),
        P(AXES, None),
        P(None, AXES),
        P(),
        P(),
        P("grp", None),
        P(),
        P(AXES, None),
        P(AXES, None),
        P(),
        P(AXES, None, None),
        P(AXES, None, None),
    )
    return jax.shard_map(local, mesh=mesh, in_specs=placed, out_specs=P(AXES, None), check_vma=False)
```

```python
import functools

import jax
import jax.numpy as jnp
from jax import lax
from jax.experimental import pallas as pl
from jax.experimental.pallas import tpu as pltpu
from jax.sharding import PartitionSpec as P

AXES = ("seq", "grp")
N = 64
G = 8
EPS = 1e-05
DEC = 16
VMEM_LIMIT = 24 * 1024 * 1024
f32 = jnp.float32
bf16 = jnp.bfloat16


def dot(a, b, contract, precision=None):
    return lax.dot_general(
        a, b, ((contract[0], contract[1]), ((), ())), preferred_element_type=f32, precision=precision
    )


def spread_lanes(columns, width):
    count = len(columns)
    rows = columns[0].shape[0]
    lane = lax.broadcasted_iota(jnp.int32, (rows, count * width), 1)
    out = jnp.broadcast_to(columns[-1], (rows, count * width))
    for j in range(count - 2, -1, -1):
        out = jnp.where(lane < (j + 1) * width, columns[j], out)
    return out


def split_decay(d):
    whole = jnp.floor(d)
    part = d - whole
    coarse = jnp.floor(part * 256.0) * (1.0 / 256.0)
    fine = part - coarse
    row = lax.broadcasted_iota(jnp.int32, (DEC, d.shape[1]), 0)
    rows = jnp.where(row == 0, whole, jnp.where(row == 1, coarse, jnp.where(row == 2, fine, 0.0)))
    return rows.astype(bf16)


def join_decay(rows):
    return jnp.sum(rows.astype(f32), axis=0, keepdims=True)


def silu(x):
    return x * (1.0 / (1.0 + jnp.exp(-x)))


def columns(blocks, inner, keys, c, width, which):
    start, first = 0, 0
    for extent in (inner, keys, keys):
        size = extent // blocks
        if c < first + size:
            return pl.ds(pl.multiple_of(start + which * size + (c - first), width), width)
        start, first = start + extent, first + size


def pick_kernel(blocks, inner, width, at_ref, x_ref, tail_ref, *outs):
    half = at_ref[1]
    length, channels = x_ref.shape
    keys = (channels - inner) // 2
    tail_ref[...] = x_ref[length - tail_ref.shape[0] :, :]
    for b in range(1, blocks):
        for c in range(0, channels // blocks, width):
            outs[b - 1][:, c : c + width] = x_ref[
                :, columns(blocks, inner, keys, c, width, half ^ b)
            ]


def running(ld):
    length = ld.shape[1]
    low = (
        lax.broadcasted_iota(jnp.int32, (length, length), 0)
        >= lax.broadcasted_iota(jnp.int32, (length, length), 1)
    ).astype(f32)
    return (
        dot(ld, low, ((1,), (1,)), lax.Precision.HIGHEST),
        dot(low, ld, ((1,), (1,)), lax.Precision.HIGHEST),
    )


def start_kernel(members, blocks, at_ref, cw_ref, z_ref, *rest):
    xs, prevs, lds = rest[:blocks], rest[blocks : 2 * blocks], rest[2 * blocks : 3 * blocks]
    rest = rest[3 * blocks :]
    acts, outs, scr = rest[:blocks], rest[blocks : blocks + members], rest[-1]
    z_outs = rest[blocks + members : -1]
    member, half = at_ref[0], at_ref[1]
    length = xs[0].shape[0]
    channels = xs[0].shape[1] // blocks
    heads = lds[0].shape[0] // blocks
    count = scr.shape[0]
    per_group = heads // count
    inner = channels - 2 * count * N
    width = inner // count
    head_size = width // per_group
    halo, taps = prevs[0].shape[0], cw_ref.shape[0]
    for b in range(blocks):
        ld = lds[b][pl.ds(pl.multiple_of(half * heads, heads), heads), :]
        cumt = running(ld)[1]
        last = cumt[length - 1 : length, :]
        to_end = jnp.exp(last - cumt)
        act_ref = acts[b]
        for c in range(0, channels, width):
            cols = slice(c, c + width)
            at = columns(blocks, inner * blocks, count * N * blocks, c, width, half)
            padded = jnp.concatenate(
                [prevs[b][:, at], xs[b][:, cols if b else at]], axis=0
            ).astype(f32)
            first = halo - taps + 1
            total = cw_ref[0:1, at] * padded[first : first + length]
            for k in range(1, taps):
                total = total + cw_ref[k : k + 1, at] * padded[first + k : first + k + length]
            act_ref[:, cols] = silu(total).astype(bf16)
        slot = half ^ b
        for g in range(count):
            v = act_ref[:, g * width : (g + 1) * width].astype(f32)
            ik = act_ref[:, inner + g * N : inner + (g + 1) * N]
            hs = range(g * per_group, (g + 1) * per_group)
            weighted = (v * spread_lanes([to_end[:, h : h + 1] for h in hs], head_size)).astype(bf16)
            scr[g, slot, :N, :] = dot(ik, weighted, ((0,), (0,))).astype(bf16)
            scr[g, slot, N:, :] = split_decay(
                spread_lanes([last[:, h : h + 1] for h in hs], head_size)
            )
    for m in range(members):
        outs[m][...] = scr[member ^ m]
    for b in range(1, blocks):
        for c in range(0, inner, width):
            at = pl.ds(pl.multiple_of((half ^ b) * inner + c, width), width)
            z_outs[b - 1][:, c : c + width] = z_ref[:, at]


def in_order(members, blocks, member, chunks, scr):
    for m in range(members):
        who = member ^ m
        for k in range(blocks):
            scr[(who >> 1) * 2 * blocks + 2 * k + (who & 1)] = chunks[m][k]


def plane_kernel(members, blocks, at_ref, *rest):
    chunks, out, scr = rest[:members], rest[members], rest[members + 1]
    in_order(members, blocks, at_ref[0], chunks, scr)
    state = jnp.zeros((N, out.shape[1]), f32)
    total = jnp.zeros((1, out.shape[1]), f32)
    for s in range(members * blocks):
        decay = join_decay(scr[s, N:, :])
        state = jnp.exp(decay) * state + scr[s, :N, :].astype(f32)
        total = total + decay
    out[:N, :] = state.astype(bf16)
    out[N:, :] = split_decay(total)


def pair_kernel(stage, at_ref, own_ref, other_ref, out_ref):
    later = ((at_ref[3] >> stage) & 1) == 1
    own, other = own_ref[:N, :].astype(f32), other_ref[:N, :].astype(f32)
    own_decay, other_decay = join_decay(own_ref[N:, :]), join_decay(other_ref[N:, :])
    first, second = jnp.where(later, other, own), jnp.where(later, own, other)
    out_ref[:N, :] = (jnp.exp(jnp.where(later, own_decay, other_decay)) * first + second).astype(bf16)
    out_ref[N:, :] = split_decay(own_decay + other_decay)


def enter_kernel(members, blocks, stages, at_ref, scr, *rest):
    earlier, outs, inc = rest[:stages], rest[stages : stages + members], rest[-1]
    member = at_ref[0]
    state = jnp.zeros((N, scr.shape[2]), f32)
    for stage in range(stages - 1, -1, -1):
        e = earlier[stage]
        joined = jnp.exp(join_decay(e[N:, :])) * state + e[:N, :].astype(f32)
        state = jnp.where(((at_ref[3] >> stage) & 1) == 1, joined, state)
    for s in range(members * blocks):
        inc[s] = state.astype(bf16)
        state = jnp.exp(join_decay(scr[s, N:, :])) * state + scr[s, :N, :].astype(f32)
    for m in range(members):
        who = member ^ m
        for k in range(blocks):
            outs[m][k] = inc[(who >> 1) * 2 * blocks + 2 * k + (who & 1)]


def inside_kernel(count, blocks, at_ref, *refs):
    acts, lds, outs = (refs[k * blocks : (k + 1) * blocks] for k in range(3))
    length, channels = acts[0].shape
    heads = lds[0].shape[0] // blocks
    per_group = heads // count
    inner = channels - 2 * count * N
    head_size = inner // heads
    causal = lax.broadcasted_iota(jnp.int32, (length, length), 0) >= lax.broadcasted_iota(
        jnp.int32, (length, length), 1
    )
    for b in range(blocks):
        act_ref, out_ref = acts[b], outs[b]
        cum, cumt = running(lds[b][pl.ds(pl.multiple_of(at_ref[1] * heads, heads), heads), :])
        for g in range(count):
            ik = act_ref[:, inner + g * N : inner + (g + 1) * N]
            ok = act_ref[:, inner + (count + g) * N : inner + (count + g + 1) * N]
            meet = jnp.where(causal, dot(ok, ik, ((1,), (1,))), 0.0)
            for h in range(g * per_group, (g + 1) * per_group):
                gap = jnp.where(causal, cumt[:, h : h + 1] - cum[h : h + 1, :], 0.0)
                mixing = (jnp.exp(gap) * meet).astype(bf16)
                cols = slice(h * head_size, (h + 1) * head_size)
                out_ref[:, cols] = dot(mixing, act_ref[:, cols], ((1,), (0,)))


def norm_kernel(members, blocks, b, at_ref, gain_ref, act_ref, ld_ref, inside_ref, z_ref, *rest):
    incoming, own_ref, pair_ref = rest[:members], rest[members], rest[members + 1]
    out_ref, scr, mix = rest[-3], rest[-2], rest[-1]
    member, half, core = at_ref[0], at_ref[1], at_ref[2]
    for m in range(members):
        scr[member ^ m] = incoming[m][...]
    inner = z_ref.shape[1] if b else z_ref.shape[1] // blocks
    heads = ld_ref.shape[0] // blocks
    count = scr.shape[0]
    per_group = heads // count
    width = inner // count
    head_size = inner // heads
    shard = count // 2
    reach = jnp.exp(running(ld_ref[pl.ds(pl.multiple_of(half * heads, heads), heads), :])[1])
    slot = half ^ b
    for g in range(count):
        cols = slice(g * width, (g + 1) * width)
        ok = act_ref[:, inner + (count + g) * N : inner + (count + g + 1) * N]
        hs = range(g * per_group, (g + 1) * per_group)
        far = dot(ok, scr[g, slot], ((1,), (0,)))
        ssm = inside_ref[:, cols] + far * spread_lanes([reach[:, h : h + 1] for h in hs], head_size)
        at = pl.ds(pl.multiple_of(half * inner + g * width, width), width)
        gated = ssm * silu(z_ref[:, cols if b else at].astype(f32))
        square = jnp.mean(gated * gated, axis=1, keepdims=True)
        mix[((g // shard) ^ core) * shard + g % shard] = (
            gated * lax.rsqrt(square + EPS) * gain_ref[:, at]
        ).astype(bf16)
    model = out_ref.shape[1]
    tile = 384 if model % 384 == 0 else model
    for c in range(0, model, tile):
        total = None
        for g in range(count):
            rows = (own_ref, pair_ref)[g // shard]
            at = (g % shard) * width
            part = dot(mix[g], rows[at : at + width, c : c + tile], ((1,), (0,)))
            total = part if total is None else total + part
        out_ref[:, c : c + tile] = total.astype(out_ref.dtype)


def token_kernel(blocks, gain_ref, hidden_ref, own_ref, meta_ref, *rest):
    others, residual_ref, block_ref = rest[: blocks - 1], rest[blocks - 1], rest[blocks]
    model = hidden_ref.shape[1]
    total = hidden_ref[...].astype(f32) + own_ref[...]
    for other in others:
        total = total + other[...].astype(f32)
    residual = total.astype(bf16)
    residual_ref[...] = residual
    wide = residual.astype(f32)
    square = jnp.mean(wide * wide, axis=1, keepdims=True)
    block_ref[:, :model] = (wide * lax.rsqrt(square + EPS) * gain_ref[...]).astype(bf16)
    block_ref[:, model:] = meta_ref[...]


def dispatch_kernel(devices, capacity, at_ref, block_ref, *rest):
    outs, weigh_ref = rest[:-1], rest[-1]
    length = block_ref.shape[0]
    rows, model = outs[0].shape
    lanes = len(outs) * rows
    device = lax.broadcasted_iota(jnp.int32, (devices, lanes), 0)

    def layout(shape):
        lane = lax.broadcasted_iota(jnp.int32, shape, 1)
        chip, within = jnp.zeros(shape, jnp.int32), lane
        for k in range(1, len(outs)):
            chip = jnp.where(lane >= k * rows, k, chip)
            within = jnp.where(lane >= k * rows, lane - k * rows, within)
        core = jnp.where(within >= capacity, 1, 0)
        return chip, core, within - capacity * core

    chip, core, _ = layout((devices, lanes))
    select = (device == at_ref[1] + (at_ref[0] ^ (2 * chip + core))).astype(f32).astype(bf16)
    place = layout((length, lanes))[2]
    place = jnp.where(place < capacity, place, -2).astype(f32)
    slot = dot(block_ref[:, model : model + devices], select, ((1,), (0,)))
    gate = dot(block_ref[:, model + devices : model + 2 * devices], select, ((1,), (0,))) + dot(
        block_ref[:, model + 2 * devices : model + 3 * devices], select, ((1,), (0,))
    )
    hit = slot == place
    weigh_ref[...] = jnp.where(hit, gate, 0.0).astype(bf16)
    take = jnp.where(hit, 1.0, 0.0).astype(bf16)
    total = dot(take, block_ref[:, :model], ((0,), (0,)))
    for k in range(len(outs)):
        outs[k][...] = total[k * rows : (k + 1) * rows].astype(bf16)


def chosen_rows(shape, dim, chip, core, capacity):
    listed = lax.broadcasted_iota(jnp.int32, shape, 1 - dim)
    within = lax.broadcasted_iota(jnp.int32, shape, dim) - core * capacity
    hit = (listed == chip * capacity + within) & (within >= 0) & (within < capacity)
    return hit.astype(f32).astype(bf16)


def listed_rows(ins, core, capacity, count):
    total = None
    for k, ref in enumerate(ins):
        part = dot(chosen_rows((count, ref.shape[0]), 1, k, core, capacity), ref[...], ((1,), (0,)))
        total = part if total is None else total + part
    return total.astype(bf16)


def other_kernel(capacity, *refs):
    refs[-1][...] = listed_rows(refs[:-1], 1, capacity, refs[-1].shape[0])


def expert_kernel(capacity, tile, *refs):
    ins, (got_ref, up_ref, down_ref, mine_ref, other_ref, rows_ref, act_ref) = refs[:-7], refs[-7:]
    count, model = got_ref.shape
    rows_ref[:count, :] = listed_rows(ins, 0, capacity, count)
    rows_ref[count:, :] = got_ref[...]
    ffw = up_ref.shape[1]
    step = 512 if ffw % 512 == 0 else ffw
    for f in range(0, ffw, step):
        up = jnp.maximum(dot(rows_ref[...], up_ref[:, f : f + step], ((1,), (0,))), 0.0)
        act_ref[:, f : f + step] = (up * up).astype(bf16)
    for c in range(0, model, tile):
        part = dot(act_ref[...], down_ref[:, c : c + tile], ((1,), (0,)))
        mine_ref[:, c : c + tile] = part[:count].astype(bf16)
        other_ref[:, c : c + tile] = part[count:].astype(bf16)


def return_kernel(capacity, mine_ref, back_ref, *outs):
    count = mine_ref.shape[0]
    for k, out in enumerate(outs):
        shape = (out.shape[0], count)
        out[...] = (
            dot(chosen_rows(shape, 0, k, 0, capacity), mine_ref[...], ((1,), (0,)))
            + dot(chosen_rows(shape, 0, k, 1, capacity), back_ref[...], ((1,), (0,)))
        ).astype(bf16)


def after(x, *others):
    return lax.optimization_barrier((x,) + others)[0]


def local(
    hidden,
    conv_input,
    z_stream,
    log_decay,
    conv_weight,
    norm_gain,
    out_weight,
    moe_gain,
    routes,
    gate_weights,
    expert_home,
    up_weight,
    down_weight,
):
    n_grp = lax.axis_size("grp")
    devices = lax.axis_size("seq") * n_grp
    plane = 2 * n_grp
    outer = devices // plane
    me = lax.axis_index("seq") * n_grp + lax.axis_index("grp")
    r = lax.rem(me, plane)
    place = lax.div(me, plane)

    def swap(x, m):
        return lax.ppermute(x, AXES, [(d, d ^ m) for d in range(devices)])

    def onward(x, by):
        return lax.ppermute(
            x, AXES, [(d, d + by) for d in range(devices) if d + by < devices]
        )

    def turn(x):
        return lax.ppermute(x, AXES, [(d, (d + plane) % devices) for d in range(devices)])

    length, channels = conv_input.shape
    inner = z_stream.shape[1]
    width = inner // G
    model = hidden.shape[1]
    smem = pl.BlockSpec(memory_space=pltpu.SMEM)
    halo = 16

    blocks = n_grp // 2
    members = plane // blocks
    grp = lax.axis_index("grp")
    half = lax.div(grp, 2)
    core = lax.rem(grp, 2)
    member = lax.div(r, n_grp) * 2 + core
    at_member = jnp.stack([member, half, core, place]).astype(jnp.int32)
    count = G // blocks

    def onward_to(x, by, m):
        return lax.ppermute(
            x, AXES, [(d, (d + by) ^ m) for d in range(devices) if d + by < devices]
        )

    shapes = jax.ShapeDtypeStruct
    vm = pl.BlockSpec(memory_space=pltpu.VMEM)
    wide = channels // blocks
    chunk = (N + DEC, width)

    def kernel_call(kernel, inputs, outs, scratch=(), flops=0, moved=0, scalars=True):
        return pl.pallas_call(
            kernel,
            out_shape=outs,
            in_specs=([smem] if scalars else []) + [vm] * (len(inputs) - (1 if scalars else 0)),
            scratch_shapes=list(scratch),
            compiler_params=pltpu.CompilerParams(vmem_limit_bytes=VMEM_LIMIT),
            cost_estimate=pl.CostEstimate(flops=flops, bytes_accessed=moved, transcendentals=0),
        )(*inputs)

    picked = kernel_call(
        functools.partial(pick_kernel, blocks, inner, width),
        [at_member, conv_input],
        [shapes((halo, channels), bf16)] + [shapes((length, wide), bf16)] * (blocks - 1),
    )
    tail = picked[0]
    xs, prevs, lds = [conv_input], [onward_to(tail, 1, 0)], [log_decay]
    for b in range(1, blocks):
        xs.append(swap(picked[b], 2 * b))
        prevs.append(onward_to(tail, 1, 2 * b))
        lds.append(swap(log_decay, 2 * b))

    rows_own = out_weight
    rows_pair = swap(out_weight, 1)
    shard = out_weight.shape[0]

    first = kernel_call(
        functools.partial(start_kernel, members, blocks),
        [at_member, conv_weight, z_stream] + xs + prevs + lds,
        [shapes((length, wide), bf16)] * blocks
        + [shapes((blocks,) + chunk, bf16)] * members
        + [shapes((length, inner // blocks), bf16)] * (blocks - 1),
        [pltpu.VMEM((count, blocks) + chunk, bf16)],
        50000000,
        8000000,
    )
    acts = first[:blocks]
    sends = first[blocks : blocks + members]
    zs = [z_stream] + [swap(first[blocks + members + b - 1], 2 * b) for b in range(1, blocks)]
    mask = [(m >> 1) * n_grp + (m & 1) for m in range(members)]
    chunks = [sends[0]] + [swap(sends[m], mask[m]) for m in range(1, members)]
    inside = kernel_call(
        functools.partial(inside_kernel, count, blocks),
        [at_member] + list(acts) + lds,
        [shapes((length, inner // blocks), f32)] * blocks,
        (),
        100000000,
        15000000,
    )
    whole, ordered = kernel_call(
        functools.partial(plane_kernel, members, blocks),
        [at_member] + chunks,
        [shapes(chunk, bf16), shapes((plane,) + chunk, bf16)],
    )
    earlier, stage = [], 0
    while (1 << stage) < outer:
        earlier.append(swap(whole, plane << stage))
        stage += 1
        if (1 << stage) < outer:
            whole = kernel_call(
                functools.partial(pair_kernel, stage - 1),
                [at_member, whole, earlier[-1]],
                shapes(chunk, bf16),
            )
    entering = kernel_call(
        functools.partial(enter_kernel, members, blocks, stage),
        [at_member, ordered] + earlier,
        [shapes((blocks, N, width), bf16)] * members,
        [pltpu.VMEM((plane, N, width), bf16)],
        1000000,
        2000000,
    )
    incoming = [entering[0]] + [swap(entering[m], mask[m]) for m in range(1, members)]
    def project(b):
        return kernel_call(
            functools.partial(norm_kernel, members, blocks, b),
            [at_member, norm_gain[None, :], acts[b], lds[b], inside[b], zs[b]]
            + incoming
            + [rows_own, rows_pair],
            shapes((length, model), bf16 if b else f32),
            [pltpu.VMEM((count, blocks, N, width), bf16), pltpu.VMEM((count, length, width), bf16)],
            800000000,
            8000000,
        )

    others = [swap(project(b), 2 * b) for b in range(1, blocks)]
    mine = project(0)

    top_count = routes.shape[1]
    capacity = max(2, 3 * length * top_count // (2 * devices))
    experts = expert_home.shape[0]
    picked = routes[:, :, None] == jnp.arange(experts, dtype=jnp.int32)[None, None, :]
    target = jnp.sum(jnp.where(picked, expert_home[None, None, :], 0), axis=2)
    at_device = target[:, :, None] == jnp.arange(devices, dtype=jnp.int32)[None, None, :]
    chosen = jnp.any(at_device, axis=1)
    gates = jnp.sum(jnp.where(at_device, gate_weights[:, :, None], 0.0), axis=1)
    before = (
        lax.broadcasted_iota(jnp.int32, (length, length), 0)
        > lax.broadcasted_iota(jnp.int32, (length, length), 1)
    ).astype(bf16)
    rank = jnp.dot(before, chosen.astype(bf16), preferred_element_type=f32)
    slots = jnp.where(chosen, rank, -1.0)
    gate_high = jnp.floor(gates * 128.0) * (1.0 / 128.0)
    meta = jnp.concatenate([slots, gate_high, gates - gate_high], axis=1).astype(bf16)
    extra = -(-3 * devices // 128) * 128
    meta = jnp.pad(meta, ((0, 0), (0, extra - 3 * devices)))

    up_local = up_weight[0]
    down_local = down_weight[0]
    hops = list(range(0, plane, 2))
    two = -(-2 * capacity // 8) * 8

    at = jnp.stack([r, place * plane]).astype(jnp.int32)
    count_rows = -(-len(hops) * capacity // 16) * 16
    listed = shapes((count_rows, model), bf16)
    tile = 384 if model % 384 == 0 else model

    def dispatch(block):
        out = kernel_call(
            functools.partial(dispatch_kernel, devices, capacity),
            [at, block],
            [shapes((two, model), bf16)] * len(hops) + [shapes((length, len(hops) * two), bf16)],
        )
        return out[-1], [out[0]] + [swap(out[k], hops[k]) for k in range(1, len(hops))]

    def held(rows, *others):
        return list(lax.optimization_barrier(tuple(rows) + others)[: len(rows)]) if others else list(rows)

    def work(rows, before_list, before_work):
        rows = held(rows, *before_list)
        other = kernel_call(
            functools.partial(other_kernel, capacity), list(rows), listed, scalars=False
        )
        mine, theirs = kernel_call(
            functools.partial(expert_kernel, capacity, tile),
            held(rows, *before_work) + [swap(other, 1), up_local, down_local],
            [listed, listed],
            [
                pltpu.VMEM((2 * count_rows, model), bf16),
                pltpu.VMEM((2 * count_rows, up_local.shape[1]), bf16),
            ],
            scalars=False,
        )
        return mine, swap(theirs, 1)

    def sort_back(mine, theirs):
        return kernel_call(
            functools.partial(return_kernel, capacity),
            [mine, theirs],
            [shapes((two, model), bf16)] * len(hops),
            scalars=False,
        )

    def send_back(parts):
        return [parts[0]] + [swap(parts[k], hops[k]) for k in range(1, len(hops))]

    def gather_up(weigh, back):
        return jnp.dot(weigh, jnp.concatenate(back, axis=0), preferred_element_type=f32)

    residual_one, block = kernel_call(
        functools.partial(token_kernel, blocks),
        [moe_gain[None, :], hidden, mine, meta] + others,
        [shapes((length, model), bf16), shapes((length, model + extra), bf16)],
        scalars=False,
    )
    weighs, arrived, made, results, parts = {}, {}, {}, {}, {}
    end = outer - 1

    def give_back(step, *before):
        mine, theirs = made[step]
        if before:
            mine = after(mine, *before)
        results[step] = sort_back(mine, theirs)
        return send_back(results[step])

    for step in range(outer):
        following = turn(block) if step < end else None
        if step:
            before = arrived[step - 1][1:2] + ([made[step - 2][0]] if step >= 2 else [])
            block = held([block], *before)[0]
        weighs[step], arrived[step] = dispatch(block)
        block = following
        if step:
            made[step - 1] = work(arrived[step - 1], [weighs[step]], [])
        if 1 <= step - 1 < end:
            parts[step - 1] = gather_up(weighs[step - 1], give_back(step - 1))
    before = [made[end - 1][0]] if end else []
    if end >= 3:
        before.append(parts[end - 2])
    made[end] = work(arrived[end], before, [])
    if end:
        parts[end] = gather_up(weighs[end], give_back(end, *([parts[end - 1]] if end >= 2 else [])))
    back = give_back(0, *([results[end][0]] if end else []))
    carried = None
    for step in range(1, outer):
        part = parts[step]
        if carried is not None:
            part = part + carried.astype(f32)
        carried = turn(part.astype(bf16))
    if carried is not None:
        back = held(back, carried)
    part = residual_one.astype(f32) + gather_up(weighs[0], back)
    if carried is not None:
        part = part + carried.astype(f32)
    return part.astype(bf16)


def solution(mesh):
    placed = (
        P(AXES, None),
        P(AXES, None),
        P(AXES, None),
        P(None, AXES),
        P(),
        P(),
        P("grp", None),
        P(),
        P(AXES, None),
        P(AXES, None),
        P(),
        P(AXES, None, None),
        P(AXES, None, None),
    )
    return jax.shard_map(local, mesh=mesh, in_specs=placed, out_specs=P(AXES, None), check_vma=False)
```

```python
import functools

import jax
import jax.numpy as jnp
from jax import lax
from jax.experimental import pallas as pl
from jax.experimental.pallas import tpu as pltpu
from jax.sharding import PartitionSpec as P

AXES = ("seq", "grp")
N = 64
G = 8
EPS = 1e-05
DEC = 16
VMEM_LIMIT = 24 * 1024 * 1024
f32 = jnp.float32
bf16 = jnp.bfloat16


def dot(a, b, contract, precision=None):
    return lax.dot_general(
        a, b, ((contract[0], contract[1]), ((), ())), preferred_element_type=f32, precision=precision
    )


def spread_lanes(columns, width):
    count = len(columns)
    rows = columns[0].shape[0]
    lane = lax.broadcasted_iota(jnp.int32, (rows, count * width), 1)
    out = jnp.broadcast_to(columns[-1], (rows, count * width))
    for j in range(count - 2, -1, -1):
        out = jnp.where(lane < (j + 1) * width, columns[j], out)
    return out


def split_decay(d):
    whole = jnp.floor(d)
    part = d - whole
    coarse = jnp.floor(part * 256.0) * (1.0 / 256.0)
    fine = part - coarse
    row = lax.broadcasted_iota(jnp.int32, (DEC, d.shape[1]), 0)
    rows = jnp.where(row == 0, whole, jnp.where(row == 1, coarse, jnp.where(row == 2, fine, 0.0)))
    return rows.astype(bf16)


def join_decay(rows):
    return jnp.sum(rows.astype(f32), axis=0, keepdims=True)


def silu(x):
    return x * (1.0 / (1.0 + jnp.exp(-x)))


def columns(blocks, inner, keys, c, width, which):
    start, first = 0, 0
    for extent in (inner, keys, keys):
        size = extent // blocks
        if c < first + size:
            return pl.ds(pl.multiple_of(start + which * size + (c - first), width), width)
        start, first = start + extent, first + size


def pick_kernel(blocks, inner, width, at_ref, x_ref, tail_ref, *outs):
    half = at_ref[1]
    length, channels = x_ref.shape
    keys = (channels - inner) // 2
    tail_ref[...] = x_ref[length - tail_ref.shape[0] :, :]
    for b in range(1, blocks):
        for c in range(0, channels // blocks, width):
            outs[b - 1][:, c : c + width] = x_ref[
                :, columns(blocks, inner, keys, c, width, half ^ b)
            ]


def running(ld):
    length = ld.shape[1]
    low = (
        lax.broadcasted_iota(jnp.int32, (length, length), 0)
        >= lax.broadcasted_iota(jnp.int32, (length, length), 1)
    ).astype(f32)
    return (
        dot(ld, low, ((1,), (1,)), lax.Precision.HIGHEST),
        dot(low, ld, ((1,), (1,)), lax.Precision.HIGHEST),
    )


def start_kernel(members, blocks, at_ref, cw_ref, z_ref, *rest):
    xs, prevs, lds = rest[:blocks], rest[blocks : 2 * blocks], rest[2 * blocks : 3 * blocks]
    rest = rest[3 * blocks :]
    acts, outs, scr = rest[:blocks], rest[blocks : blocks + members], rest[-1]
    z_outs = rest[blocks + members : -1]
    member, half = at_ref[0], at_ref[1]
    length = xs[0].shape[0]
    channels = xs[0].shape[1] // blocks
    heads = lds[0].shape[0] // blocks
    count = scr.shape[0]
    per_group = heads // count
    inner = channels - 2 * count * N
    width = inner // count
    head_size = width // per_group
    halo, taps = prevs[0].shape[0], cw_ref.shape[0]
    for b in range(blocks):
        ld = lds[b][pl.ds(pl.multiple_of(half * heads, heads), heads), :]
        cumt = running(ld)[1]
        last = cumt[length - 1 : length, :]
        to_end = jnp.exp(last - cumt)
        act_ref = acts[b]
        for c in range(0, channels, width):
            cols = slice(c, c + width)
            at = columns(blocks, inner * blocks, count * N * blocks, c, width, half)
            padded = jnp.concatenate(
                [prevs[b][:, at], xs[b][:, cols if b else at]], axis=0
            ).astype(f32)
            first = halo - taps + 1
            total = cw_ref[0:1, at] * padded[first : first + length]
            for k in range(1, taps):
                total = total + cw_ref[k : k + 1, at] * padded[first + k : first + k + length]
            act_ref[:, cols] = silu(total).astype(bf16)
        slot = half ^ b
        for g in range(count):
            v = act_ref[:, g * width : (g + 1) * width].astype(f32)
            ik = act_ref[:, inner + g * N : inner + (g + 1) * N]
            hs = range(g * per_group, (g + 1) * per_group)
            weighted = (v * spread_lanes([to_end[:, h : h + 1] for h in hs], head_size)).astype(bf16)
            scr[g, slot, :N, :] = dot(ik, weighted, ((0,), (0,))).astype(bf16)
            scr[g, slot, N:, :] = split_decay(
                spread_lanes([last[:, h : h + 1] for h in hs], head_size)
            )
    for m in range(members):
        outs[m][...] = scr[member ^ m]
    for b in range(1, blocks):
        for c in range(0, inner, width):
            at = pl.ds(pl.multiple_of((half ^ b) * inner + c, width), width)
            z_outs[b - 1][:, c : c + width] = z_ref[:, at]


def in_order(members, blocks, member, chunks, scr):
    for m in range(members):
        who = member ^ m
        for k in range(blocks):
            scr[(who >> 1) * 2 * blocks + 2 * k + (who & 1)] = chunks[m][k]


def plane_kernel(members, blocks, at_ref, *rest):
    chunks, out, scr = rest[:members], rest[members], rest[members + 1]
    in_order(members, blocks, at_ref[0], chunks, scr)
    state = jnp.zeros((N, out.shape[1]), f32)
    total = jnp.zeros((1, out.shape[1]), f32)
    for s in range(members * blocks):
        decay = join_decay(scr[s, N:, :])
        state = jnp.exp(decay) * state + scr[s, :N, :].astype(f32)
        total = total + decay
    out[:N, :] = state.astype(bf16)
    out[N:, :] = split_decay(total)


def pair_kernel(stage, at_ref, own_ref, other_ref, out_ref):
    later = ((at_ref[3] >> stage) & 1) == 1
    own, other = own_ref[:N, :].astype(f32), other_ref[:N, :].astype(f32)
    own_decay, other_decay = join_decay(own_ref[N:, :]), join_decay(other_ref[N:, :])
    first, second = jnp.where(later, other, own), jnp.where(later, own, other)
    out_ref[:N, :] = (jnp.exp(jnp.where(later, own_decay, other_decay)) * first + second).astype(bf16)
    out_ref[N:, :] = split_decay(own_decay + other_decay)


def enter_kernel(members, blocks, stages, at_ref, scr, *rest):
    earlier, outs, inc = rest[:stages], rest[stages : stages + members], rest[-1]
    member = at_ref[0]
    state = jnp.zeros((N, scr.shape[2]), f32)
    for stage in range(stages - 1, -1, -1):
        e = earlier[stage]
        joined = jnp.exp(join_decay(e[N:, :])) * state + e[:N, :].astype(f32)
        state = jnp.where(((at_ref[3] >> stage) & 1) == 1, joined, state)
    for s in range(members * blocks):
        inc[s] = state.astype(bf16)
        state = jnp.exp(join_decay(scr[s, N:, :])) * state + scr[s, :N, :].astype(f32)
    for m in range(members):
        who = member ^ m
        for k in range(blocks):
            outs[m][k] = inc[(who >> 1) * 2 * blocks + 2 * k + (who & 1)]


def inside_kernel(count, blocks, at_ref, *refs):
    acts, lds, outs = (refs[k * blocks : (k + 1) * blocks] for k in range(3))
    length, channels = acts[0].shape
    heads = lds[0].shape[0] // blocks
    per_group = heads // count
    inner = channels - 2 * count * N
    head_size = inner // heads
    causal = lax.broadcasted_iota(jnp.int32, (length, length), 0) >= lax.broadcasted_iota(
        jnp.int32, (length, length), 1
    )
    for b in range(blocks):
        act_ref, out_ref = acts[b], outs[b]
        cum, cumt = running(lds[b][pl.ds(pl.multiple_of(at_ref[1] * heads, heads), heads), :])
        for g in range(count):
            ik = act_ref[:, inner + g * N : inner + (g + 1) * N]
            ok = act_ref[:, inner + (count + g) * N : inner + (count + g + 1) * N]
            meet = jnp.where(causal, dot(ok, ik, ((1,), (1,))), 0.0)
            for h in range(g * per_group, (g + 1) * per_group):
                gap = jnp.where(causal, cumt[:, h : h + 1] - cum[h : h + 1, :], 0.0)
                mixing = (jnp.exp(gap) * meet).astype(bf16)
                cols = slice(h * head_size, (h + 1) * head_size)
                out_ref[:, cols] = dot(mixing, act_ref[:, cols], ((1,), (0,)))


def norm_kernel(members, blocks, b, at_ref, gain_ref, act_ref, ld_ref, inside_ref, z_ref, *rest):
    incoming, own_ref, pair_ref = rest[:members], rest[members], rest[members + 1]
    out_ref, scr, mix = rest[-3], rest[-2], rest[-1]
    member, half, core = at_ref[0], at_ref[1], at_ref[2]
    for m in range(members):
        scr[member ^ m] = incoming[m][...]
    inner = z_ref.shape[1] if b else z_ref.shape[1] // blocks
    heads = ld_ref.shape[0] // blocks
    count = scr.shape[0]
    per_group = heads // count
    width = inner // count
    head_size = inner // heads
    shard = count // 2
    reach = jnp.exp(running(ld_ref[pl.ds(pl.multiple_of(half * heads, heads), heads), :])[1])
    slot = half ^ b
    for g in range(count):
        cols = slice(g * width, (g + 1) * width)
        ok = act_ref[:, inner + (count + g) * N : inner + (count + g + 1) * N]
        hs = range(g * per_group, (g + 1) * per_group)
        far = dot(ok, scr[g, slot], ((1,), (0,)))
        ssm = inside_ref[:, cols] + far * spread_lanes([reach[:, h : h + 1] for h in hs], head_size)
        at = pl.ds(pl.multiple_of(half * inner + g * width, width), width)
        gated = ssm * silu(z_ref[:, cols if b else at].astype(f32))
        square = jnp.mean(gated * gated, axis=1, keepdims=True)
        mix[((g // shard) ^ core) * shard + g % shard] = (
            gated * lax.rsqrt(square + EPS) * gain_ref[:, at]
        ).astype(bf16)
    model = out_ref.shape[1]
    tile = 384 if model % 384 == 0 else model
    for c in range(0, model, tile):
        total = None
        for g in range(count):
            rows = (own_ref, pair_ref)[g // shard]
            at = (g % shard) * width
            part = dot(mix[g], rows[at : at + width, c : c + tile], ((1,), (0,)))
            total = part if total is None else total + part
        out_ref[:, c : c + tile] = total.astype(out_ref.dtype)


def token_kernel(blocks, gain_ref, hidden_ref, own_ref, meta_ref, *rest):
    others, residual_ref, block_ref = rest[: blocks - 1], rest[blocks - 1], rest[blocks]
    model = hidden_ref.shape[1]
    total = hidden_ref[...].astype(f32) + own_ref[...]
    for other in others:
        total = total + other[...].astype(f32)
    residual = total.astype(bf16)
    residual_ref[...] = residual
    wide = residual.astype(f32)
    square = jnp.mean(wide * wide, axis=1, keepdims=True)
    block_ref[:, :model] = (wide * lax.rsqrt(square + EPS) * gain_ref[...]).astype(bf16)
    block_ref[:, model:] = meta_ref[...]


def dispatch_kernel(devices, capacity, at_ref, block_ref, *rest):
    outs, weigh_ref = rest[:-1], rest[-1]
    length = block_ref.shape[0]
    rows, model = outs[0].shape
    lanes = len(outs) * rows
    device = lax.broadcasted_iota(jnp.int32, (devices, lanes), 0)

    def layout(shape):
        lane = lax.broadcasted_iota(jnp.int32, shape, 1)
        chip, within = jnp.zeros(shape, jnp.int32), lane
        for k in range(1, len(outs)):
            chip = jnp.where(lane >= k * rows, k, chip)
            within = jnp.where(lane >= k * rows, lane - k * rows, within)
        core = jnp.where(within >= capacity, 1, 0)
        return chip, core, within - capacity * core

    chip, core, _ = layout((devices, lanes))
    select = (device == at_ref[1] + (at_ref[0] ^ (2 * chip + core))).astype(f32).astype(bf16)
    place = layout((length, lanes))[2]
    place = jnp.where(place < capacity, place, -2).astype(f32)
    slot = dot(block_ref[:, model : model + devices], select, ((1,), (0,)))
    gate = dot(block_ref[:, model + devices : model + 2 * devices], select, ((1,), (0,))) + dot(
        block_ref[:, model + 2 * devices : model + 3 * devices], select, ((1,), (0,))
    )
    hit = slot == place
    weigh_ref[...] = jnp.where(hit, gate, 0.0).astype(bf16)
    take = jnp.where(hit, 1.0, 0.0).astype(bf16)
    total = dot(take, block_ref[:, :model], ((0,), (0,)))
    for k in range(len(outs)):
        outs[k][...] = total[k * rows : (k + 1) * rows].astype(bf16)


def chosen_rows(shape, dim, chip, core, capacity):
    listed = lax.broadcasted_iota(jnp.int32, shape, 1 - dim)
    within = lax.broadcasted_iota(jnp.int32, shape, dim) - core * capacity
    hit = (listed == chip * capacity + within) & (within >= 0) & (within < capacity)
    return hit.astype(f32).astype(bf16)


def listed_rows(ins, core, capacity, count):
    total = None
    for k, ref in enumerate(ins):
        part = dot(chosen_rows((count, ref.shape[0]), 1, k, core, capacity), ref[...], ((1,), (0,)))
        total = part if total is None else total + part
    return total.astype(bf16)


def other_kernel(capacity, *refs):
    refs[-1][...] = listed_rows(refs[:-1], 1, capacity, refs[-1].shape[0])


def expert_kernel(capacity, tile, *refs):
    ins, (got_ref, up_ref, down_ref, mine_ref, other_ref, rows_ref, act_ref) = refs[:-7], refs[-7:]
    count, model = got_ref.shape
    rows_ref[:count, :] = listed_rows(ins, 0, capacity, count)
    rows_ref[count:, :] = got_ref[...]
    ffw = up_ref.shape[1]
    step = 512 if ffw % 512 == 0 else ffw

    @pl.loop(0, ffw // step)
    def _(f):
        cols = pl.ds(pl.multiple_of(f * step, step), step)
        up = jnp.maximum(dot(rows_ref[...], up_ref[:, cols], ((1,), (0,))), 0.0)
        act_ref[:, cols] = (up * up).astype(bf16)

    @pl.loop(0, model // tile)
    def _(c):
        cols = pl.ds(pl.multiple_of(c * tile, tile), tile)
        part = dot(act_ref[...], down_ref[:, cols], ((1,), (0,)))
        mine_ref[:, cols] = part[:count].astype(bf16)
        other_ref[:, cols] = part[count:].astype(bf16)


def return_kernel(capacity, mine_ref, back_ref, *outs):
    count = mine_ref.shape[0]
    for k, out in enumerate(outs):
        shape = (out.shape[0], count)
        out[...] = (
            dot(chosen_rows(shape, 0, k, 0, capacity), mine_ref[...], ((1,), (0,)))
            + dot(chosen_rows(shape, 0, k, 1, capacity), back_ref[...], ((1,), (0,)))
        ).astype(bf16)


def after(x, *others):
    return lax.optimization_barrier((x,) + others)[0]


def local(
    hidden,
    conv_input,
    z_stream,
    log_decay,
    conv_weight,
    norm_gain,
    out_weight,
    moe_gain,
    routes,
    gate_weights,
    expert_home,
    up_weight,
    down_weight,
):
    n_grp = lax.axis_size("grp")
    devices = lax.axis_size("seq") * n_grp
    plane = 2 * n_grp
    outer = devices // plane
    me = lax.axis_index("seq") * n_grp + lax.axis_index("grp")
    r = lax.rem(me, plane)
    place = lax.div(me, plane)

    def swap(x, m):
        return lax.ppermute(x, AXES, [(d, d ^ m) for d in range(devices)])

    def onward(x, by):
        return lax.ppermute(
            x, AXES, [(d, d + by) for d in range(devices) if d + by < devices]
        )

    def turn(x):
        return lax.ppermute(x, AXES, [(d, (d + plane) % devices) for d in range(devices)])

    length, channels = conv_input.shape
    inner = z_stream.shape[1]
    width = inner // G
    model = hidden.shape[1]
    smem = pl.BlockSpec(memory_space=pltpu.SMEM)
    halo = 16

    blocks = n_grp // 2
    members = plane // blocks
    grp = lax.axis_index("grp")
    half = lax.div(grp, 2)
    core = lax.rem(grp, 2)
    member = lax.div(r, n_grp) * 2 + core
    at_member = jnp.stack([member, half, core, place]).astype(jnp.int32)
    count = G // blocks

    def onward_to(x, by, m):
        return lax.ppermute(
            x, AXES, [(d, (d + by) ^ m) for d in range(devices) if d + by < devices]
        )

    shapes = jax.ShapeDtypeStruct
    vm = pl.BlockSpec(memory_space=pltpu.VMEM)
    wide = channels // blocks
    chunk = (N + DEC, width)

    def kernel_call(kernel, inputs, outs, scratch=(), flops=0, moved=0, scalars=True):
        return pl.pallas_call(
            kernel,
            out_shape=outs,
            in_specs=([smem] if scalars else []) + [vm] * (len(inputs) - (1 if scalars else 0)),
            scratch_shapes=list(scratch),
            compiler_params=pltpu.CompilerParams(vmem_limit_bytes=VMEM_LIMIT),
            cost_estimate=pl.CostEstimate(flops=flops, bytes_accessed=moved, transcendentals=0),
        )(*inputs)

    picked = kernel_call(
        functools.partial(pick_kernel, blocks, inner, width),
        [at_member, conv_input],
        [shapes((halo, channels), bf16)] + [shapes((length, wide), bf16)] * (blocks - 1),
    )
    tail = picked[0]
    xs, prevs, lds = [conv_input], [onward_to(tail, 1, 0)], [log_decay]
    for b in range(1, blocks):
        xs.append(swap(picked[b], 2 * b))
        prevs.append(onward_to(tail, 1, 2 * b))
        lds.append(swap(log_decay, 2 * b))

    rows_own = out_weight
    rows_pair = swap(out_weight, 1)
    shard = out_weight.shape[0]

    first = kernel_call(
        functools.partial(start_kernel, members, blocks),
        [at_member, conv_weight, z_stream] + xs + prevs + lds,
        [shapes((length, wide), bf16)] * blocks
        + [shapes((blocks,) + chunk, bf16)] * members
        + [shapes((length, inner // blocks), bf16)] * (blocks - 1),
        [pltpu.VMEM((count, blocks) + chunk, bf16)],
        50000000,
        8000000,
    )
    acts = first[:blocks]
    sends = first[blocks : blocks + members]
    zs = [z_stream] + [swap(first[blocks + members + b - 1], 2 * b) for b in range(1, blocks)]
    mask = [(m >> 1) * n_grp + (m & 1) for m in range(members)]
    chunks = [sends[0]] + [swap(sends[m], mask[m]) for m in range(1, members)]
    inside = kernel_call(
        functools.partial(inside_kernel, count, blocks),
        [at_member] + list(acts) + lds,
        [shapes((length, inner // blocks), f32)] * blocks,
        (),
        100000000,
        15000000,
    )
    whole, ordered = kernel_call(
        functools.partial(plane_kernel, members, blocks),
        [at_member] + chunks,
        [shapes(chunk, bf16), shapes((plane,) + chunk, bf16)],
    )
    earlier, stage = [], 0
    while (1 << stage) < outer:
        earlier.append(swap(whole, plane << stage))
        stage += 1
        if (1 << stage) < outer:
            whole = kernel_call(
                functools.partial(pair_kernel, stage - 1),
                [at_member, whole, earlier[-1]],
                shapes(chunk, bf16),
            )
    entering = kernel_call(
        functools.partial(enter_kernel, members, blocks, stage),
        [at_member, ordered] + earlier,
        [shapes((blocks, N, width), bf16)] * members,
        [pltpu.VMEM((plane, N, width), bf16)],
        1000000,
        2000000,
    )
    incoming = [entering[0]] + [swap(entering[m], mask[m]) for m in range(1, members)]
    def project(b):
        return kernel_call(
            functools.partial(norm_kernel, members, blocks, b),
            [at_member, norm_gain[None, :], acts[b], lds[b], inside[b], zs[b]]
            + incoming
            + [rows_own, rows_pair],
            shapes((length, model), bf16 if b else f32),
            [pltpu.VMEM((count, blocks, N, width), bf16), pltpu.VMEM((count, length, width), bf16)],
            800000000,
            8000000,
        )

    others = [swap(project(b), 2 * b) for b in range(1, blocks)]
    mine = project(0)

    top_count = routes.shape[1]
    capacity = max(2, 3 * length * top_count // (2 * devices))
    experts = expert_home.shape[0]
    picked = routes[:, :, None] == jnp.arange(experts, dtype=jnp.int32)[None, None, :]
    target = jnp.sum(jnp.where(picked, expert_home[None, None, :], 0), axis=2)
    at_device = target[:, :, None] == jnp.arange(devices, dtype=jnp.int32)[None, None, :]
    chosen = jnp.any(at_device, axis=1)
    gates = jnp.sum(jnp.where(at_device, gate_weights[:, :, None], 0.0), axis=1)
    before = (
        lax.broadcasted_iota(jnp.int32, (length, length), 0)
        > lax.broadcasted_iota(jnp.int32, (length, length), 1)
    ).astype(bf16)
    rank = jnp.dot(before, chosen.astype(bf16), preferred_element_type=f32)
    slots = jnp.where(chosen, rank, -1.0)
    gate_high = jnp.floor(gates * 128.0) * (1.0 / 128.0)
    meta = jnp.concatenate([slots, gate_high, gates - gate_high], axis=1).astype(bf16)
    extra = -(-3 * devices // 128) * 128
    meta = jnp.pad(meta, ((0, 0), (0, extra - 3 * devices)))

    up_local = up_weight[0]
    down_local = down_weight[0]
    hops = list(range(0, plane, 2))
    two = -(-2 * capacity // 8) * 8

    at = jnp.stack([r, place * plane]).astype(jnp.int32)
    count_rows = -(-len(hops) * capacity // 16) * 16
    listed = shapes((count_rows, model), bf16)
    tile = 896 if model % 896 == 0 else model

    def dispatch(block):
        out = kernel_call(
            functools.partial(dispatch_kernel, devices, capacity),
            [at, block],
            [shapes((two, model), bf16)] * len(hops) + [shapes((length, len(hops) * two), bf16)],
        )
        return out[-1], [out[0]] + [swap(out[k], hops[k]) for k in range(1, len(hops))]

    def held(rows, *others):
        return list(lax.optimization_barrier(tuple(rows) + others)[: len(rows)]) if others else list(rows)

    def work(rows, before_list, before_work):
        rows = held(rows, *before_list)
        other = kernel_call(
            functools.partial(other_kernel, capacity), list(rows), listed, scalars=False
        )
        mine, theirs = kernel_call(
            functools.partial(expert_kernel, capacity, tile),
            held(rows, *before_work) + [swap(other, 1), up_local, down_local],
            [listed, listed],
            [
                pltpu.VMEM((2 * count_rows, model), bf16),
                pltpu.VMEM((2 * count_rows, up_local.shape[1]), bf16),
            ],
            scalars=False,
        )
        return mine, swap(theirs, 1)

    def sort_back(mine, theirs):
        return kernel_call(
            functools.partial(return_kernel, capacity),
            [mine, theirs],
            [shapes((two, model), bf16)] * len(hops),
            scalars=False,
        )

    def send_back(parts):
        return [parts[0]] + [swap(parts[k], hops[k]) for k in range(1, len(hops))]

    def gather_up(weigh, back):
        return jnp.dot(weigh, jnp.concatenate(back, axis=0), preferred_element_type=f32)

    residual_one, block = kernel_call(
        functools.partial(token_kernel, blocks),
        [moe_gain[None, :], hidden, mine, meta] + others,
        [shapes((length, model), bf16), shapes((length, model + extra), bf16)],
        scalars=False,
    )
    weighs, arrived, made, results, parts = {}, {}, {}, {}, {}
    end = outer - 1

    def give_back(step, *before):
        mine, theirs = made[step]
        if before:
            mine = after(mine, *before)
        results[step] = sort_back(mine, theirs)
        return send_back(results[step])

    for step in range(outer):
        following = turn(block) if step < end else None
        if step:
            before = arrived[step - 1][1:2] + ([made[step - 2][0]] if step >= 2 else [])
            block = held([block], *before)[0]
        weighs[step], arrived[step] = dispatch(block)
        block = following
        if step:
            made[step - 1] = work(arrived[step - 1], [weighs[step]], [])
        if 1 <= step - 1 < end:
            parts[step - 1] = gather_up(weighs[step - 1], give_back(step - 1))
    before = [made[end - 1][0]] if end else []
    if end >= 3:
        before.append(parts[end - 2])
    made[end] = work(arrived[end], before, [])
    if end:
        parts[end] = gather_up(weighs[end], give_back(end, *([parts[end - 1]] if end >= 2 else [])))
    back = give_back(0, *([results[end][0]] if end else []))
    carried = None
    for step in range(1, outer):
        part = parts[step]
        if carried is not None:
            part = part + carried.astype(f32)
        carried = turn(part.astype(bf16))
    if carried is not None:
        back = held(back, carried)
    part = residual_one.astype(f32) + gather_up(weighs[0], back)
    if carried is not None:
        part = part + carried.astype(f32)
    return part.astype(bf16)


def solution(mesh):
    placed = (
        P(AXES, None),
        P(AXES, None),
        P(AXES, None),
        P(None, AXES),
        P(),
        P(),
        P("grp", None),
        P(),
        P(AXES, None),
        P(AXES, None),
        P(),
        P(AXES, None, None),
        P(AXES, None, None),
    )
    return jax.shard_map(local, mesh=mesh, in_specs=placed, out_specs=P(AXES, None), check_vma=False)
```

```python
import functools

import jax
import jax.numpy as jnp
from jax import lax
from jax.experimental import pallas as pl
from jax.experimental.pallas import tpu as pltpu
from jax.sharding import PartitionSpec as P

AXES = ("seq", "grp")
N = 64
G = 8
EPS = 1e-05
DEC = 16
VMEM_LIMIT = 24 * 1024 * 1024
f32 = jnp.float32
bf16 = jnp.bfloat16


def dot(a, b, contract, precision=None):
    return lax.dot_general(
        a, b, ((contract[0], contract[1]), ((), ())), preferred_element_type=f32, precision=precision
    )


def spread_lanes(columns, width):
    count = len(columns)
    rows = columns[0].shape[0]
    lane = lax.broadcasted_iota(jnp.int32, (rows, count * width), 1)
    out = jnp.broadcast_to(columns[-1], (rows, count * width))
    for j in range(count - 2, -1, -1):
        out = jnp.where(lane < (j + 1) * width, columns[j], out)
    return out


def split_decay(d):
    whole = jnp.floor(d)
    part = d - whole
    coarse = jnp.floor(part * 256.0) * (1.0 / 256.0)
    fine = part - coarse
    row = lax.broadcasted_iota(jnp.int32, (DEC, d.shape[1]), 0)
    rows = jnp.where(row == 0, whole, jnp.where(row == 1, coarse, jnp.where(row == 2, fine, 0.0)))
    return rows.astype(bf16)


def join_decay(rows):
    return jnp.sum(rows.astype(f32), axis=0, keepdims=True)


def silu(x):
    return x * (1.0 / (1.0 + jnp.exp(-x)))


def columns(blocks, inner, keys, c, width, which):
    start, first = 0, 0
    for extent in (inner, keys, keys):
        size = extent // blocks
        if c < first + size:
            return pl.ds(pl.multiple_of(start + which * size + (c - first), width), width)
        start, first = start + extent, first + size


def pick_kernel(blocks, inner, width, at_ref, x_ref, tail_ref, *outs):
    half = at_ref[1]
    length, channels = x_ref.shape
    keys = (channels - inner) // 2
    tail_ref[...] = x_ref[length - tail_ref.shape[0] :, :]
    for b in range(1, blocks):
        for c in range(0, channels // blocks, width):
            outs[b - 1][:, c : c + width] = x_ref[
                :, columns(blocks, inner, keys, c, width, half ^ b)
            ]


def running(ld):
    length = ld.shape[1]
    low = (
        lax.broadcasted_iota(jnp.int32, (length, length), 0)
        >= lax.broadcasted_iota(jnp.int32, (length, length), 1)
    ).astype(f32)
    return (
        dot(ld, low, ((1,), (1,)), lax.Precision.HIGHEST),
        dot(low, ld, ((1,), (1,)), lax.Precision.HIGHEST),
    )


def prepare_kernel(blocks, inner, width, at_ref, cw_ref, ld_ref, z_ref, cw_out, ld_out, *z_outs):
    half = at_ref[1]
    keys = (cw_ref.shape[1] - inner) // 2
    ld_out[...] = ld_ref[...]
    for c in range(0, cw_out.shape[1], width):
        cw_out[:, c : c + width] = cw_ref[:, columns(blocks, inner, keys, c, width, half)]
    for b in range(1, blocks):
        for c in range(0, inner // blocks, width):
            at = pl.ds(pl.multiple_of((half ^ b) * (inner // blocks) + c, width), width)
            z_outs[b - 1][:, c : c + width] = z_ref[:, at]


def start_kernel(members, blocks, at_ref, cw_ref, *rest):
    xs, prevs, lds = rest[:blocks], rest[blocks : 2 * blocks], rest[2 * blocks : 3 * blocks]
    rest = rest[3 * blocks :]
    acts, outs, scr = rest[:blocks], rest[blocks : blocks + members], rest[-1]
    member, half = at_ref[0], at_ref[1]
    length = xs[0].shape[0]
    channels = xs[0].shape[1] // blocks
    heads = lds[0].shape[0] // blocks
    count = scr.shape[0]
    per_group = heads // count
    inner = channels - 2 * count * N
    width = inner // count
    head_size = width // per_group
    halo, taps = prevs[0].shape[0], cw_ref.shape[0]
    for b in range(blocks):
        ld = lds[b][pl.ds(pl.multiple_of(half * heads, heads), heads), :]
        cumt = running(ld)[1]
        last = cumt[length - 1 : length, :]
        to_end = jnp.exp(last - cumt)
        act_ref = acts[b]
        for c in range(0, channels, width):
            cols = slice(c, c + width)
            at = columns(blocks, inner * blocks, count * N * blocks, c, width, half)
            padded = jnp.concatenate(
                [prevs[b][:, at], xs[b][:, cols if b else at]], axis=0
            ).astype(f32)
            first = halo - taps + 1
            total = cw_ref[0:1, cols] * padded[first : first + length]
            for k in range(1, taps):
                total = total + cw_ref[k : k + 1, cols] * padded[first + k : first + k + length]
            act_ref[:, cols] = silu(total).astype(bf16)
        slot = half ^ b
        for g in range(count):
            v = act_ref[:, g * width : (g + 1) * width].astype(f32)
            ik = act_ref[:, inner + g * N : inner + (g + 1) * N]
            hs = range(g * per_group, (g + 1) * per_group)
            weighted = (v * spread_lanes([to_end[:, h : h + 1] for h in hs], head_size)).astype(bf16)
            scr[g, slot, :N, :] = dot(ik, weighted, ((0,), (0,))).astype(bf16)
            scr[g, slot, N:, :] = split_decay(
                spread_lanes([last[:, h : h + 1] for h in hs], head_size)
            )
    for m in range(members):
        outs[m][...] = scr[member ^ m]


def in_order(members, blocks, member, chunks, scr):
    for m in range(members):
        who = member ^ m
        for k in range(blocks):
            scr[(who >> 1) * 2 * blocks + 2 * k + (who & 1)] = chunks[m][k]


def plane_kernel(members, blocks, at_ref, *rest):
    chunks, out, scr = rest[:members], rest[members], rest[members + 1]
    in_order(members, blocks, at_ref[0], chunks, scr)
    state = jnp.zeros((N, out.shape[1]), f32)
    total = jnp.zeros((1, out.shape[1]), f32)
    for s in range(members * blocks):
        decay = join_decay(scr[s, N:, :])
        state = jnp.exp(decay) * state + scr[s, :N, :].astype(f32)
        total = total + decay
    out[:N, :] = state.astype(bf16)
    out[N:, :] = split_decay(total)


def pair_kernel(stage, at_ref, own_ref, other_ref, out_ref):
    later = ((at_ref[3] >> stage) & 1) == 1
    own, other = own_ref[:N, :].astype(f32), other_ref[:N, :].astype(f32)
    own_decay, other_decay = join_decay(own_ref[N:, :]), join_decay(other_ref[N:, :])
    first, second = jnp.where(later, other, own), jnp.where(later, own, other)
    out_ref[:N, :] = (jnp.exp(jnp.where(later, own_decay, other_decay)) * first + second).astype(bf16)
    out_ref[N:, :] = split_decay(own_decay + other_decay)


def enter_kernel(members, blocks, stages, at_ref, scr, *rest):
    earlier, outs, inc = rest[:stages], rest[stages : stages + members], rest[-1]
    member = at_ref[0]
    state = jnp.zeros((N, scr.shape[2]), f32)
    for stage in range(stages - 1, -1, -1):
        e = earlier[stage]
        joined = jnp.exp(join_decay(e[N:, :])) * state + e[:N, :].astype(f32)
        state = jnp.where(((at_ref[3] >> stage) & 1) == 1, joined, state)
    for s in range(members * blocks):
        inc[s] = state.astype(bf16)
        state = jnp.exp(join_decay(scr[s, N:, :])) * state + scr[s, :N, :].astype(f32)
    for m in range(members):
        who = member ^ m
        for k in range(blocks):
            outs[m][k] = inc[(who >> 1) * 2 * blocks + 2 * k + (who & 1)]


def inside_kernel(count, blocks, at_ref, *refs):
    acts, lds, outs = (refs[k * blocks : (k + 1) * blocks] for k in range(3))
    length, channels = acts[0].shape
    heads = lds[0].shape[0] // blocks
    per_group = heads // count
    inner = channels - 2 * count * N
    head_size = inner // heads
    causal = lax.broadcasted_iota(jnp.int32, (length, length), 0) >= lax.broadcasted_iota(
        jnp.int32, (length, length), 1
    )
    for b in range(blocks):
        act_ref, out_ref = acts[b], outs[b]
        cum, cumt = running(lds[b][pl.ds(pl.multiple_of(at_ref[1] * heads, heads), heads), :])
        for g in range(count):
            ik = act_ref[:, inner + g * N : inner + (g + 1) * N]
            ok = act_ref[:, inner + (count + g) * N : inner + (count + g + 1) * N]
            meet = jnp.where(causal, dot(ok, ik, ((1,), (1,))), 0.0)
            for h in range(g * per_group, (g + 1) * per_group):
                gap = jnp.where(causal, cumt[:, h : h + 1] - cum[h : h + 1, :], 0.0)
                mixing = (jnp.exp(gap) * meet).astype(bf16)
                cols = slice(h * head_size, (h + 1) * head_size)
                out_ref[:, cols] = dot(mixing, act_ref[:, cols], ((1,), (0,)))


def norm_kernel(members, blocks, b, at_ref, gain_ref, act_ref, ld_ref, inside_ref, z_ref, *rest):
    incoming, own_ref, pair_ref = rest[:members], rest[members], rest[members + 1]
    out_ref, scr, mix = rest[-3], rest[-2], rest[-1]
    member, half, core = at_ref[0], at_ref[1], at_ref[2]
    for m in range(members):
        scr[member ^ m] = incoming[m][...]
    inner = z_ref.shape[1] if b else z_ref.shape[1] // blocks
    heads = ld_ref.shape[0] // blocks
    count = scr.shape[0]
    per_group = heads // count
    width = inner // count
    head_size = inner // heads
    shard = count // 2
    reach = jnp.exp(running(ld_ref[pl.ds(pl.multiple_of(half * heads, heads), heads), :])[1])
    slot = half ^ b
    for g in range(count):
        cols = slice(g * width, (g + 1) * width)
        ok = act_ref[:, inner + (count + g) * N : inner + (count + g + 1) * N]
        hs = range(g * per_group, (g + 1) * per_group)
        far = dot(ok, scr[g, slot], ((1,), (0,)))
        ssm = inside_ref[:, cols] + far * spread_lanes([reach[:, h : h + 1] for h in hs], head_size)
        at = pl.ds(pl.multiple_of(half * inner + g * width, width), width)
        gated = ssm * silu(z_ref[:, cols if b else at].astype(f32))
        square = jnp.mean(gated * gated, axis=1, keepdims=True)
        mix[((g // shard) ^ core) * shard + g % shard] = (
            gated * lax.rsqrt(square + EPS) * gain_ref[:, at]
        ).astype(bf16)
    model = out_ref.shape[1]
    tile = 384 if model % 384 == 0 else model
    for c in range(0, model, tile):
        total = None
        for g in range(count):
            rows = (own_ref, pair_ref)[g // shard]
            at = (g % shard) * width
            part = dot(mix[g], rows[at : at + width, c : c + tile], ((1,), (0,)))
            total = part if total is None else total + part
        out_ref[:, c : c + tile] = total.astype(out_ref.dtype)


def token_kernel(blocks, gain_ref, hidden_ref, own_ref, meta_ref, *rest):
    others, residual_ref, block_ref = rest[: blocks - 1], rest[blocks - 1], rest[blocks]
    model = hidden_ref.shape[1]
    total = hidden_ref[...].astype(f32) + own_ref[...]
    for other in others:
        total = total + other[...].astype(f32)
    residual = total.astype(bf16)
    residual_ref[...] = residual
    wide = residual.astype(f32)
    square = jnp.mean(wide * wide, axis=1, keepdims=True)
    block_ref[:, :model] = (wide * lax.rsqrt(square + EPS) * gain_ref[...]).astype(bf16)
    block_ref[:, model:] = meta_ref[...]


def dispatch_kernel(devices, capacity, at_ref, block_ref, *rest):
    outs, weigh_ref = rest[:-1], rest[-1]
    length = block_ref.shape[0]
    rows, model = outs[0].shape
    lanes = len(outs) * rows
    device = lax.broadcasted_iota(jnp.int32, (devices, lanes), 0)

    def layout(shape):
        lane = lax.broadcasted_iota(jnp.int32, shape, 1)
        chip, within = jnp.zeros(shape, jnp.int32), lane
        for k in range(1, len(outs)):
            chip = jnp.where(lane >= k * rows, k, chip)
            within = jnp.where(lane >= k * rows, lane - k * rows, within)
        core = jnp.where(within >= capacity, 1, 0)
        return chip, core, within - capacity * core

    chip, core, _ = layout((devices, lanes))
    select = (device == at_ref[1] + (at_ref[0] ^ (2 * chip + core))).astype(f32).astype(bf16)
    place = layout((length, lanes))[2]
    place = jnp.where(place < capacity, place, -2).astype(f32)
    slot = dot(block_ref[:, model : model + devices], select, ((1,), (0,)))
    gate = dot(block_ref[:, model + devices : model + 2 * devices], select, ((1,), (0,))) + dot(
        block_ref[:, model + 2 * devices : model + 3 * devices], select, ((1,), (0,))
    )
    hit = slot == place
    weigh_ref[...] = jnp.where(hit, gate, 0.0).astype(bf16)
    take = jnp.where(hit, 1.0, 0.0).astype(bf16)
    total = dot(take, block_ref[:, :model], ((0,), (0,)))
    for k in range(len(outs)):
        outs[k][...] = total[k * rows : (k + 1) * rows].astype(bf16)


def chosen_rows(shape, dim, chip, core, capacity):
    listed = lax.broadcasted_iota(jnp.int32, shape, 1 - dim)
    within = lax.broadcasted_iota(jnp.int32, shape, dim) - core * capacity
    hit = (listed == chip * capacity + within) & (within >= 0) & (within < capacity)
    return hit.astype(f32).astype(bf16)


def listed_rows(ins, core, capacity, count):
    total = None
    for k, ref in enumerate(ins):
        part = dot(chosen_rows((count, ref.shape[0]), 1, k, core, capacity), ref[...], ((1,), (0,)))
        total = part if total is None else total + part
    return total.astype(bf16)


def other_kernel(capacity, *refs):
    refs[-1][...] = listed_rows(refs[:-1], 1, capacity, refs[-1].shape[0])


def expert_kernel(capacity, tile, *refs):
    ins, (got_ref, up_ref, down_ref, mine_ref, other_ref, rows_ref, act_ref) = refs[:-7], refs[-7:]
    count, model = got_ref.shape
    rows_ref[:count, :] = listed_rows(ins, 0, capacity, count)
    rows_ref[count:, :] = got_ref[...]
    ffw = up_ref.shape[1]
    step = 512 if ffw % 512 == 0 else ffw

    @pl.loop(0, ffw // step)
    def _(f):
        cols = pl.ds(pl.multiple_of(f * step, step), step)
        up = jnp.maximum(dot(rows_ref[...], up_ref[:, cols], ((1,), (0,))), 0.0)
        act_ref[:, cols] = (up * up).astype(bf16)

    @pl.loop(0, model // tile)
    def _(c):
        cols = pl.ds(pl.multiple_of(c * tile, tile), tile)
        part = dot(act_ref[...], down_ref[:, cols], ((1,), (0,)))
        mine_ref[:, cols] = part[:count].astype(bf16)
        other_ref[:, cols] = part[count:].astype(bf16)


def return_kernel(capacity, mine_ref, back_ref, *outs):
    count = mine_ref.shape[0]
    for k, out in enumerate(outs):
        shape = (out.shape[0], count)
        out[...] = (
            dot(chosen_rows(shape, 0, k, 0, capacity), mine_ref[...], ((1,), (0,)))
            + dot(chosen_rows(shape, 0, k, 1, capacity), back_ref[...], ((1,), (0,)))
        ).astype(bf16)


def after(x, *others):
    return lax.optimization_barrier((x,) + others)[0]


def local(
    hidden,
    conv_input,
    z_stream,
    log_decay,
    conv_weight,
    norm_gain,
    out_weight,
    moe_gain,
    routes,
    gate_weights,
    expert_home,
    up_weight,
    down_weight,
):
    n_grp = lax.axis_size("grp")
    devices = lax.axis_size("seq") * n_grp
    plane = 2 * n_grp
    outer = devices // plane
    me = lax.axis_index("seq") * n_grp + lax.axis_index("grp")
    r = lax.rem(me, plane)
    place = lax.div(me, plane)

    def swap(x, m):
        return lax.ppermute(x, AXES, [(d, d ^ m) for d in range(devices)])

    def onward(x, by):
        return lax.ppermute(
            x, AXES, [(d, d + by) for d in range(devices) if d + by < devices]
        )

    def turn(x):
        return lax.ppermute(x, AXES, [(d, (d + plane) % devices) for d in range(devices)])

    length, channels = conv_input.shape
    inner = z_stream.shape[1]
    width = inner // G
    model = hidden.shape[1]
    smem = pl.BlockSpec(memory_space=pltpu.SMEM)
    halo = 16

    blocks = n_grp // 2
    members = plane // blocks
    grp = lax.axis_index("grp")
    half = lax.div(grp, 2)
    core = lax.rem(grp, 2)
    member = lax.div(r, n_grp) * 2 + core
    at_member = jnp.stack([member, half, core, place]).astype(jnp.int32)
    count = G // blocks

    def onward_to(x, by, m):
        return lax.ppermute(
            x, AXES, [(d, (d + by) ^ m) for d in range(devices) if d + by < devices]
        )

    shapes = jax.ShapeDtypeStruct
    vm = pl.BlockSpec(memory_space=pltpu.VMEM)
    wide = channels // blocks
    chunk = (N + DEC, width)

    def kernel_call(kernel, inputs, outs, scratch=(), flops=0, moved=0, scalars=True):
        return pl.pallas_call(
            kernel,
            out_shape=outs,
            in_specs=([smem] if scalars else []) + [vm] * (len(inputs) - (1 if scalars else 0)),
            scratch_shapes=list(scratch),
            compiler_params=pltpu.CompilerParams(vmem_limit_bytes=VMEM_LIMIT),
            cost_estimate=pl.CostEstimate(flops=flops, bytes_accessed=moved, transcendentals=0),
        )(*inputs)

    picked = kernel_call(
        functools.partial(pick_kernel, blocks, inner, width),
        [at_member, conv_input],
        [shapes((halo, channels), bf16)] + [shapes((length, wide), bf16)] * (blocks - 1),
    )
    tail = picked[0]
    prepared = kernel_call(
        functools.partial(prepare_kernel, blocks, inner, width),
        [at_member, conv_weight, log_decay, z_stream],
        [shapes((conv_weight.shape[0], wide), f32), shapes(log_decay.shape, f32)]
        + [shapes((length, inner // blocks), bf16)] * (blocks - 1),
    )
    xs, prevs, lds = [conv_input], [onward_to(tail, 1, 0)], [prepared[1]]
    for b in range(1, blocks):
        xs.append(swap(picked[b], 2 * b))
        prevs.append(onward_to(tail, 1, 2 * b))
        lds.append(swap(prepared[1], 2 * b))

    rows_own = out_weight
    rows_pair = swap(out_weight, 1)
    shard = out_weight.shape[0]

    first = kernel_call(
        functools.partial(start_kernel, members, blocks),
        [at_member, prepared[0]] + xs + prevs + lds,
        [shapes((length, wide), bf16)] * blocks
        + [shapes((blocks,) + chunk, bf16)] * members,
        [pltpu.VMEM((count, blocks) + chunk, bf16)],
        50000000,
        8000000,
    )
    acts = first[:blocks]
    sends = first[blocks : blocks + members]
    zs = [z_stream] + [swap(prepared[1 + b], 2 * b) for b in range(1, blocks)]
    mask = [(m >> 1) * n_grp + (m & 1) for m in range(members)]
    chunks = [sends[0]] + [swap(sends[m], mask[m]) for m in range(1, members)]
    inside = kernel_call(
        functools.partial(inside_kernel, count, blocks),
        [at_member] + list(acts) + lds,
        [shapes((length, inner // blocks), f32)] * blocks,
        (),
        100000000,
        15000000,
    )
    whole, ordered = kernel_call(
        functools.partial(plane_kernel, members, blocks),
        [at_member] + chunks,
        [shapes(chunk, bf16), shapes((plane,) + chunk, bf16)],
    )
    earlier, stage = [], 0
    while (1 << stage) < outer:
        earlier.append(swap(whole, plane << stage))
        stage += 1
        if (1 << stage) < outer:
            whole = kernel_call(
                functools.partial(pair_kernel, stage - 1),
                [at_member, whole, earlier[-1]],
                shapes(chunk, bf16),
            )
    entering = kernel_call(
        functools.partial(enter_kernel, members, blocks, stage),
        [at_member, ordered] + earlier,
        [shapes((blocks, N, width), bf16)] * members,
        [pltpu.VMEM((plane, N, width), bf16)],
        1000000,
        2000000,
    )
    incoming = [entering[0]] + [swap(entering[m], mask[m]) for m in range(1, members)]
    def project(b):
        return kernel_call(
            functools.partial(norm_kernel, members, blocks, b),
            [at_member, norm_gain[None, :], acts[b], lds[b], inside[b], zs[b]]
            + incoming
            + [rows_own, rows_pair],
            shapes((length, model), bf16 if b else f32),
            [pltpu.VMEM((count, blocks, N, width), bf16), pltpu.VMEM((count, length, width), bf16)],
            800000000,
            8000000,
        )

    others = [swap(project(b), 2 * b) for b in range(1, blocks)]
    mine = project(0)

    top_count = routes.shape[1]
    capacity = max(2, 3 * length * top_count // (2 * devices))
    experts = expert_home.shape[0]
    picked = routes[:, :, None] == jnp.arange(experts, dtype=jnp.int32)[None, None, :]
    target = jnp.sum(jnp.where(picked, expert_home[None, None, :], 0), axis=2)
    at_device = target[:, :, None] == jnp.arange(devices, dtype=jnp.int32)[None, None, :]
    chosen = jnp.any(at_device, axis=1)
    gates = jnp.sum(jnp.where(at_device, gate_weights[:, :, None], 0.0), axis=1)
    before = (
        lax.broadcasted_iota(jnp.int32, (length, length), 0)
        > lax.broadcasted_iota(jnp.int32, (length, length), 1)
    ).astype(bf16)
    rank = jnp.dot(before, chosen.astype(bf16), preferred_element_type=f32)
    slots = jnp.where(chosen, rank, -1.0)
    gate_high = jnp.floor(gates * 128.0) * (1.0 / 128.0)
    meta = jnp.concatenate([slots, gate_high, gates - gate_high], axis=1).astype(bf16)
    extra = -(-3 * devices // 128) * 128
    meta = jnp.pad(meta, ((0, 0), (0, extra - 3 * devices)))

    up_local = up_weight[0]
    down_local = down_weight[0]
    hops = list(range(0, plane, 2))
    two = -(-2 * capacity // 8) * 8

    at = jnp.stack([r, place * plane]).astype(jnp.int32)
    count_rows = -(-len(hops) * capacity // 16) * 16
    listed = shapes((count_rows, model), bf16)
    tile = 896 if model % 896 == 0 else model

    def dispatch(block):
        out = kernel_call(
            functools.partial(dispatch_kernel, devices, capacity),
            [at, block],
            [shapes((two, model), bf16)] * len(hops) + [shapes((length, len(hops) * two), bf16)],
        )
        return out[-1], [out[0]] + [swap(out[k], hops[k]) for k in range(1, len(hops))]

    def held(rows, *others):
        return list(lax.optimization_barrier(tuple(rows) + others)[: len(rows)]) if others else list(rows)

    def work(rows, before_list, before_work):
        rows = held(rows, *before_list)
        other = kernel_call(
            functools.partial(other_kernel, capacity), list(rows), listed, scalars=False
        )
        mine, theirs = kernel_call(
            functools.partial(expert_kernel, capacity, tile),
            held(rows, *before_work) + [swap(other, 1), up_local, down_local],
            [listed, listed],
            [
                pltpu.VMEM((2 * count_rows, model), bf16),
                pltpu.VMEM((2 * count_rows, up_local.shape[1]), bf16),
            ],
            scalars=False,
        )
        return mine, swap(theirs, 1)

    def sort_back(mine, theirs):
        return kernel_call(
            functools.partial(return_kernel, capacity),
            [mine, theirs],
            [shapes((two, model), bf16)] * len(hops),
            scalars=False,
        )

    def send_back(parts):
        return [parts[0]] + [swap(parts[k], hops[k]) for k in range(1, len(hops))]

    def gather_up(weigh, back):
        return jnp.dot(weigh, jnp.concatenate(back, axis=0), preferred_element_type=f32)

    residual_one, block = kernel_call(
        functools.partial(token_kernel, blocks),
        [moe_gain[None, :], hidden, mine, meta] + others,
        [shapes((length, model), bf16), shapes((length, model + extra), bf16)],
        scalars=False,
    )
    weighs, arrived, made, results, parts = {}, {}, {}, {}, {}
    end = outer - 1

    def give_back(step, *before):
        mine, theirs = made[step]
        if before:
            mine = after(mine, *before)
        results[step] = sort_back(mine, theirs)
        return send_back(results[step])

    for step in range(outer):
        following = turn(block) if step < end else None
        if step:
            before = arrived[step - 1][1:2] + ([made[step - 2][0]] if step >= 2 else [])
            block = held([block], *before)[0]
        weighs[step], arrived[step] = dispatch(block)
        block = following
        if step:
            made[step - 1] = work(arrived[step - 1], [weighs[step]], [])
        if 1 <= step - 1 < end:
            parts[step - 1] = gather_up(weighs[step - 1], give_back(step - 1))
    before = [made[end - 1][0]] if end else []
    if end >= 3:
        before.append(parts[end - 2])
    made[end] = work(arrived[end], before, [])
    if end:
        parts[end] = gather_up(weighs[end], give_back(end, *([parts[end - 1]] if end >= 2 else [])))
    back = give_back(0, *([results[end][0]] if end else []))
    carried = None
    for step in range(1, outer):
        part = parts[step]
        if carried is not None:
            part = part + carried.astype(f32)
        carried = turn(part.astype(bf16))
    if carried is not None:
        back = held(back, carried)
    part = residual_one.astype(f32) + gather_up(weighs[0], back)
    if carried is not None:
        part = part + carried.astype(f32)
    return part.astype(bf16)


def solution(mesh):
    placed = (
        P(AXES, None),
        P(AXES, None),
        P(AXES, None),
        P(None, AXES),
        P(),
        P(),
        P("grp", None),
        P(),
        P(AXES, None),
        P(AXES, None),
        P(),
        P(AXES, None, None),
        P(AXES, None, None),
    )
    return jax.shard_map(local, mesh=mesh, in_specs=placed, out_specs=P(AXES, None), check_vma=False)
```

```python
import functools

import jax
import jax.numpy as jnp
from jax import lax
from jax.experimental import pallas as pl
from jax.experimental.pallas import tpu as pltpu
from jax.sharding import PartitionSpec as P

AXES = ("seq", "grp")
N = 64
G = 8
EPS = 1e-05
DEC = 16
VMEM_LIMIT = 24 * 1024 * 1024
f32 = jnp.float32
bf16 = jnp.bfloat16


def dot(a, b, contract, precision=None):
    return lax.dot_general(
        a, b, ((contract[0], contract[1]), ((), ())), preferred_element_type=f32, precision=precision
    )


def spread_lanes(columns, width):
    count = len(columns)
    rows = columns[0].shape[0]
    lane = lax.broadcasted_iota(jnp.int32, (rows, count * width), 1)
    out = jnp.broadcast_to(columns[-1], (rows, count * width))
    for j in range(count - 2, -1, -1):
        out = jnp.where(lane < (j + 1) * width, columns[j], out)
    return out


def split_decay(d):
    whole = jnp.floor(d)
    part = d - whole
    coarse = jnp.floor(part * 256.0) * (1.0 / 256.0)
    fine = part - coarse
    row = lax.broadcasted_iota(jnp.int32, (DEC, d.shape[1]), 0)
    rows = jnp.where(row == 0, whole, jnp.where(row == 1, coarse, jnp.where(row == 2, fine, 0.0)))
    return rows.astype(bf16)


def join_decay(rows):
    return jnp.sum(rows.astype(f32), axis=0, keepdims=True)


def silu(x):
    return x * (1.0 / (1.0 + jnp.exp(-x)))


def columns(blocks, inner, keys, c, width, which):
    start, first = 0, 0
    for extent in (inner, keys, keys):
        size = extent // blocks
        if c < first + size:
            return pl.ds(pl.multiple_of(start + which * size + (c - first), width), width)
        start, first = start + extent, first + size


def pick_kernel(blocks, inner, width, at_ref, x_ref, tail_ref, *outs):
    half = at_ref[1]
    length, channels = x_ref.shape
    keys = (channels - inner) // 2
    tail_ref[...] = x_ref[length - tail_ref.shape[0] :, :]
    for b in range(1, blocks):
        for c in range(0, channels // blocks, width):
            outs[b - 1][:, c : c + width] = x_ref[
                :, columns(blocks, inner, keys, c, width, half ^ b)
            ]


def running(ld):
    length = ld.shape[1]
    low = (
        lax.broadcasted_iota(jnp.int32, (length, length), 0)
        >= lax.broadcasted_iota(jnp.int32, (length, length), 1)
    ).astype(f32)
    return (
        dot(ld, low, ((1,), (1,)), lax.Precision.HIGHEST),
        dot(low, ld, ((1,), (1,)), lax.Precision.HIGHEST),
    )


def prepare_kernel(blocks, inner, width, at_ref, cw_ref, ld_ref, z_ref, cw_out, ld_out, *z_outs):
    half = at_ref[1]
    keys = (cw_ref.shape[1] - inner) // 2
    ld_out[...] = ld_ref[...]
    for c in range(0, cw_out.shape[1], width):
        cw_out[:, c : c + width] = cw_ref[:, columns(blocks, inner, keys, c, width, half)]
    for b in range(1, blocks):
        for c in range(0, inner // blocks, width):
            at = pl.ds(pl.multiple_of((half ^ b) * (inner // blocks) + c, width), width)
            z_outs[b - 1][:, c : c + width] = z_ref[:, at]


def start_kernel(members, blocks, at_ref, cw_ref, *rest):
    xs, prevs, lds = rest[:blocks], rest[blocks : 2 * blocks], rest[2 * blocks : 3 * blocks]
    rest = rest[3 * blocks :]
    acts, outs, scr = rest[:blocks], rest[blocks : blocks + members], rest[-1]
    member, half = at_ref[0], at_ref[1]
    length = xs[0].shape[0]
    channels = xs[0].shape[1] // blocks
    heads = lds[0].shape[0] // blocks
    count = scr.shape[0]
    per_group = heads // count
    inner = channels - 2 * count * N
    width = inner // count
    head_size = width // per_group
    halo, taps = prevs[0].shape[0], cw_ref.shape[0]
    for b in range(blocks):
        ld = lds[b][pl.ds(pl.multiple_of(half * heads, heads), heads), :]
        cumt = running(ld)[1]
        last = cumt[length - 1 : length, :]
        to_end = jnp.exp(last - cumt)
        act_ref = acts[b]
        for c in range(0, channels, width):
            cols = slice(c, c + width)
            at = columns(blocks, inner * blocks, count * N * blocks, c, width, half)
            padded = jnp.concatenate(
                [prevs[b][:, at], xs[b][:, cols if b else at]], axis=0
            ).astype(f32)
            first = halo - taps + 1
            total = cw_ref[0:1, cols] * padded[first : first + length]
            for k in range(1, taps):
                total = total + cw_ref[k : k + 1, cols] * padded[first + k : first + k + length]
            act_ref[:, cols] = silu(total).astype(bf16)
        slot = half ^ b
        for g in range(count):
            v = act_ref[:, g * width : (g + 1) * width].astype(f32)
            ik = act_ref[:, inner + g * N : inner + (g + 1) * N]
            hs = range(g * per_group, (g + 1) * per_group)
            weighted = (v * spread_lanes([to_end[:, h : h + 1] for h in hs], head_size)).astype(bf16)
            scr[g, slot, :N, :] = dot(ik, weighted, ((0,), (0,))).astype(bf16)
            scr[g, slot, N:, :] = split_decay(
                spread_lanes([last[:, h : h + 1] for h in hs], head_size)
            )
    for m in range(members):
        outs[m][...] = scr[member ^ m]


def in_order(members, blocks, member, chunks, scr):
    for m in range(members):
        who = member ^ m
        for k in range(blocks):
            scr[(who >> 1) * 2 * blocks + 2 * k + (who & 1)] = chunks[m][k]


def plane_kernel(members, blocks, at_ref, *rest):
    chunks, out, scr = rest[:members], rest[members], rest[members + 1]
    in_order(members, blocks, at_ref[0], chunks, scr)
    state = jnp.zeros((N, out.shape[1]), f32)
    total = jnp.zeros((1, out.shape[1]), f32)
    for s in range(members * blocks):
        decay = join_decay(scr[s, N:, :])
        state = jnp.exp(decay) * state + scr[s, :N, :].astype(f32)
        total = total + decay
    out[:N, :] = state.astype(bf16)
    out[N:, :] = split_decay(total)


def pair_kernel(stage, at_ref, own_ref, other_ref, out_ref):
    later = ((at_ref[3] >> stage) & 1) == 1
    own, other = own_ref[:N, :].astype(f32), other_ref[:N, :].astype(f32)
    own_decay, other_decay = join_decay(own_ref[N:, :]), join_decay(other_ref[N:, :])
    first, second = jnp.where(later, other, own), jnp.where(later, own, other)
    out_ref[:N, :] = (jnp.exp(jnp.where(later, own_decay, other_decay)) * first + second).astype(bf16)
    out_ref[N:, :] = split_decay(own_decay + other_decay)


def enter_kernel(members, blocks, stages, at_ref, scr, *rest):
    earlier, outs, inc = rest[:stages], rest[stages : stages + members], rest[-1]
    member = at_ref[0]
    state = jnp.zeros((N, scr.shape[2]), f32)
    for stage in range(stages - 1, -1, -1):
        e = earlier[stage]
        joined = jnp.exp(join_decay(e[N:, :])) * state + e[:N, :].astype(f32)
        state = jnp.where(((at_ref[3] >> stage) & 1) == 1, joined, state)
    for s in range(members * blocks):
        inc[s] = state.astype(bf16)
        state = jnp.exp(join_decay(scr[s, N:, :])) * state + scr[s, :N, :].astype(f32)
    for m in range(members):
        who = member ^ m
        for k in range(blocks):
            outs[m][k] = inc[(who >> 1) * 2 * blocks + 2 * k + (who & 1)]


def inside_kernel(count, blocks, at_ref, *refs):
    acts, lds, outs = (refs[k * blocks : (k + 1) * blocks] for k in range(3))
    length, channels = acts[0].shape
    heads = lds[0].shape[0] // blocks
    per_group = heads // count
    inner = channels - 2 * count * N
    head_size = inner // heads
    causal = lax.broadcasted_iota(jnp.int32, (length, length), 0) >= lax.broadcasted_iota(
        jnp.int32, (length, length), 1
    )
    for b in range(blocks):
        act_ref, out_ref = acts[b], outs[b]
        cum, cumt = running(lds[b][pl.ds(pl.multiple_of(at_ref[1] * heads, heads), heads), :])
        for g in range(count):
            ik = act_ref[:, inner + g * N : inner + (g + 1) * N]
            ok = act_ref[:, inner + (count + g) * N : inner + (count + g + 1) * N]
            meet = jnp.where(causal, dot(ok, ik, ((1,), (1,))), 0.0)
            for h in range(g * per_group, (g + 1) * per_group):
                gap = jnp.where(causal, cumt[:, h : h + 1] - cum[h : h + 1, :], 0.0)
                mixing = (jnp.exp(gap) * meet).astype(bf16)
                cols = slice(h * head_size, (h + 1) * head_size)
                out_ref[:, cols] = dot(mixing, act_ref[:, cols], ((1,), (0,)))


def norm_kernel(members, blocks, b, at_ref, gain_ref, act_ref, ld_ref, inside_ref, z_ref, *rest):
    incoming, own_ref, pair_ref = rest[:members], rest[members], rest[members + 1]
    out_ref, scr, mix = rest[-3], rest[-2], rest[-1]
    member, half, core = at_ref[0], at_ref[1], at_ref[2]
    for m in range(members):
        scr[member ^ m] = incoming[m][...]
    inner = z_ref.shape[1] if b else z_ref.shape[1] // blocks
    heads = ld_ref.shape[0] // blocks
    count = scr.shape[0]
    per_group = heads // count
    width = inner // count
    head_size = inner // heads
    shard = count // 2
    reach = jnp.exp(running(ld_ref[pl.ds(pl.multiple_of(half * heads, heads), heads), :])[1])
    slot = half ^ b
    for g in range(count):
        cols = slice(g * width, (g + 1) * width)
        ok = act_ref[:, inner + (count + g) * N : inner + (count + g + 1) * N]
        hs = range(g * per_group, (g + 1) * per_group)
        far = dot(ok, scr[g, slot], ((1,), (0,)))
        ssm = inside_ref[:, cols] + far * spread_lanes([reach[:, h : h + 1] for h in hs], head_size)
        at = pl.ds(pl.multiple_of(half * inner + g * width, width), width)
        gated = ssm * silu(z_ref[:, cols if b else at].astype(f32))
        square = jnp.mean(gated * gated, axis=1, keepdims=True)
        mix[((g // shard) ^ core) * shard + g % shard] = (
            gated * lax.rsqrt(square + EPS) * gain_ref[:, at]
        ).astype(bf16)
    model = out_ref.shape[1]
    tile = 384 if model % 384 == 0 else model
    for c in range(0, model, tile):
        total = None
        for g in range(count):
            rows = (own_ref, pair_ref)[g // shard]
            at = (g % shard) * width
            part = dot(mix[g], rows[at : at + width, c : c + tile], ((1,), (0,)))
            total = part if total is None else total + part
        out_ref[:, c : c + tile] = total.astype(out_ref.dtype)


def token_kernel(blocks, gain_ref, hidden_ref, own_ref, meta_ref, *rest):
    others, residual_ref, block_ref = rest[: blocks - 1], rest[blocks - 1], rest[blocks]
    model = hidden_ref.shape[1]
    total = hidden_ref[...].astype(f32) + own_ref[...]
    for other in others:
        total = total + other[...].astype(f32)
    residual = total.astype(bf16)
    residual_ref[...] = residual
    wide = residual.astype(f32)
    square = jnp.mean(wide * wide, axis=1, keepdims=True)
    block_ref[:, :model] = (wide * lax.rsqrt(square + EPS) * gain_ref[...]).astype(bf16)
    block_ref[:, model:] = meta_ref[...]


def dispatch_kernel(devices, capacity, at_ref, block_ref, *rest):
    outs, weigh_ref = rest[:-1], rest[-1]
    length = block_ref.shape[0]
    rows, model = outs[0].shape
    lanes = len(outs) * rows
    device = lax.broadcasted_iota(jnp.int32, (devices, lanes), 0)

    def layout(shape):
        lane = lax.broadcasted_iota(jnp.int32, shape, 1)
        chip, within = jnp.zeros(shape, jnp.int32), lane
        for k in range(1, len(outs)):
            chip = jnp.where(lane >= k * rows, k, chip)
            within = jnp.where(lane >= k * rows, lane - k * rows, within)
        core = jnp.where(within >= capacity, 1, 0)
        return chip, core, within - capacity * core

    chip, core, _ = layout((devices, lanes))
    select = (device == at_ref[1] + (at_ref[0] ^ (2 * chip + core))).astype(f32).astype(bf16)
    place = layout((length, lanes))[2]
    place = jnp.where(place < capacity, place, -2).astype(f32)
    slot = dot(block_ref[:, model : model + devices], select, ((1,), (0,)))
    gate = dot(block_ref[:, model + devices : model + 2 * devices], select, ((1,), (0,))) + dot(
        block_ref[:, model + 2 * devices : model + 3 * devices], select, ((1,), (0,))
    )
    hit = slot == place
    weigh_ref[...] = jnp.where(hit, gate, 0.0).astype(bf16)
    take = jnp.where(hit, 1.0, 0.0).astype(bf16)
    total = dot(take, block_ref[:, :model], ((0,), (0,)))
    for k in range(len(outs)):
        outs[k][...] = total[k * rows : (k + 1) * rows].astype(bf16)


def chosen_rows(shape, dim, chip, core, capacity):
    listed = lax.broadcasted_iota(jnp.int32, shape, 1 - dim)
    within = lax.broadcasted_iota(jnp.int32, shape, dim) - core * capacity
    hit = (listed == chip * capacity + within) & (within >= 0) & (within < capacity)
    return hit.astype(f32).astype(bf16)


def listed_rows(ins, core, capacity, count):
    total = None
    for k, ref in enumerate(ins):
        part = dot(chosen_rows((count, ref.shape[0]), 1, k, core, capacity), ref[...], ((1,), (0,)))
        total = part if total is None else total + part
    return total.astype(bf16)


def other_kernel(capacity, *refs):
    refs[-1][...] = listed_rows(refs[:-1], 1, capacity, refs[-1].shape[0])


def expert_kernel(capacity, tile, *refs):
    ins, (got_ref, up_ref, down_ref, mine_ref, other_ref, rows_ref, act_ref) = refs[:-7], refs[-7:]
    count, model = got_ref.shape
    rows_ref[:count, :] = listed_rows(ins, 0, capacity, count)
    rows_ref[count:, :] = got_ref[...]
    ffw = up_ref.shape[1]
    step = 512 if ffw % 512 == 0 else ffw

    @pl.loop(0, ffw // step)
    def _(f):
        cols = pl.ds(pl.multiple_of(f * step, step), step)
        up = jnp.maximum(dot(rows_ref[...], up_ref[:, cols], ((1,), (0,))), 0.0)
        act_ref[:, cols] = (up * up).astype(bf16)

    @pl.loop(0, model // tile)
    def _(c):
        cols = pl.ds(pl.multiple_of(c * tile, tile), tile)
        part = dot(act_ref[...], down_ref[:, cols], ((1,), (0,)))
        mine_ref[:, cols] = part[:count].astype(bf16)
        other_ref[:, cols] = part[count:].astype(bf16)


def return_kernel(capacity, mine_ref, back_ref, *outs):
    count = mine_ref.shape[0]
    for k, out in enumerate(outs):
        shape = (out.shape[0], count)
        out[...] = (
            dot(chosen_rows(shape, 0, k, 0, capacity), mine_ref[...], ((1,), (0,)))
            + dot(chosen_rows(shape, 0, k, 1, capacity), back_ref[...], ((1,), (0,)))
        ).astype(bf16)


def after(x, *others):
    return lax.optimization_barrier((x,) + others)[0]


def local(
    hidden,
    conv_input,
    z_stream,
    log_decay,
    conv_weight,
    norm_gain,
    out_weight,
    moe_gain,
    routes,
    gate_weights,
    expert_home,
    up_weight,
    down_weight,
):
    n_grp = lax.axis_size("grp")
    devices = lax.axis_size("seq") * n_grp
    plane = 2 * n_grp
    outer = devices // plane
    me = lax.axis_index("seq") * n_grp + lax.axis_index("grp")
    r = lax.rem(me, plane)
    place = lax.div(me, plane)

    def swap(x, m):
        return lax.ppermute(x, AXES, [(d, d ^ m) for d in range(devices)])

    def onward(x, by):
        return lax.ppermute(
            x, AXES, [(d, d + by) for d in range(devices) if d + by < devices]
        )

    def turn(x):
        return lax.ppermute(x, AXES, [(d, (d + plane) % devices) for d in range(devices)])

    length, channels = conv_input.shape
    inner = z_stream.shape[1]
    width = inner // G
    model = hidden.shape[1]
    smem = pl.BlockSpec(memory_space=pltpu.SMEM)
    halo = 16

    blocks = n_grp // 2
    members = plane // blocks
    grp = lax.axis_index("grp")
    half = lax.div(grp, 2)
    core = lax.rem(grp, 2)
    member = lax.div(r, n_grp) * 2 + core
    at_member = jnp.stack([member, half, core, place]).astype(jnp.int32)
    count = G // blocks

    def onward_to(x, by, m):
        return lax.ppermute(
            x, AXES, [(d, (d + by) ^ m) for d in range(devices) if d + by < devices]
        )

    shapes = jax.ShapeDtypeStruct
    vm = pl.BlockSpec(memory_space=pltpu.VMEM)
    wide = channels // blocks
    chunk = (N + DEC, width)

    def kernel_call(kernel, inputs, outs, scratch=(), flops=0, moved=0, scalars=True):
        return pl.pallas_call(
            kernel,
            out_shape=outs,
            in_specs=([smem] if scalars else []) + [vm] * (len(inputs) - (1 if scalars else 0)),
            scratch_shapes=list(scratch),
            compiler_params=pltpu.CompilerParams(vmem_limit_bytes=VMEM_LIMIT),
            cost_estimate=pl.CostEstimate(flops=flops, bytes_accessed=moved, transcendentals=0),
        )(*inputs)

    picked = kernel_call(
        functools.partial(pick_kernel, blocks, inner, width),
        [at_member, conv_input],
        [shapes((halo, channels), bf16)] + [shapes((length, wide), bf16)] * (blocks - 1),
    )
    tail = picked[0]
    prepared = kernel_call(
        functools.partial(prepare_kernel, blocks, inner, width),
        [at_member, conv_weight, log_decay, z_stream],
        [shapes((conv_weight.shape[0], wide), f32), shapes(log_decay.shape, f32)]
        + [shapes((length, inner // blocks), bf16)] * (blocks - 1),
    )
    xs, prevs, lds = [conv_input], [onward_to(tail, 1, 0)], [prepared[1]]
    for b in range(1, blocks):
        xs.append(swap(picked[b], 2 * b))
        prevs.append(onward_to(tail, 1, 2 * b))
        lds.append(swap(prepared[1], 2 * b))

    rows_own = out_weight
    rows_pair = swap(out_weight, 1)
    shard = out_weight.shape[0]

    first = kernel_call(
        functools.partial(start_kernel, members, blocks),
        [at_member, prepared[0]] + xs + prevs + lds,
        [shapes((length, wide), bf16)] * blocks
        + [shapes((blocks,) + chunk, bf16)] * members,
        [pltpu.VMEM((count, blocks) + chunk, bf16)],
        50000000,
        8000000,
    )
    acts = first[:blocks]
    sends = first[blocks : blocks + members]
    zs = [z_stream] + [swap(prepared[1 + b], 2 * b) for b in range(1, blocks)]
    mask = [(m >> 1) * n_grp + (m & 1) for m in range(members)]
    chunks = [sends[0]] + [swap(sends[m], mask[m]) for m in range(1, members)]
    inside = kernel_call(
        functools.partial(inside_kernel, count, blocks),
        [at_member] + list(acts) + lds,
        [shapes((length, inner // blocks), f32)] * blocks,
        (),
        100000000,
        15000000,
    )
    whole, ordered = kernel_call(
        functools.partial(plane_kernel, members, blocks),
        [at_member] + chunks,
        [shapes(chunk, bf16), shapes((plane,) + chunk, bf16)],
    )
    earlier, stage = [], 0
    while (1 << stage) < outer:
        earlier.append(swap(whole, plane << stage))
        stage += 1
        if (1 << stage) < outer:
            whole = kernel_call(
                functools.partial(pair_kernel, stage - 1),
                [at_member, whole, earlier[-1]],
                shapes(chunk, bf16),
            )
    entering = kernel_call(
        functools.partial(enter_kernel, members, blocks, stage),
        [at_member, ordered] + earlier,
        [shapes((blocks, N, width), bf16)] * members,
        [pltpu.VMEM((plane, N, width), bf16)],
        1000000,
        2000000,
    )
    incoming = [entering[0]] + [swap(entering[m], mask[m]) for m in range(1, members)]
    def project(b):
        return kernel_call(
            functools.partial(norm_kernel, members, blocks, b),
            [at_member, norm_gain[None, :], acts[b], lds[b], inside[b], zs[b]]
            + incoming
            + [rows_own, rows_pair],
            shapes((length, model), bf16 if b else f32),
            [pltpu.VMEM((count, blocks, N, width), bf16), pltpu.VMEM((count, length, width), bf16)],
            800000000,
            8000000,
        )

    others = [swap(project(b), 2 * b) for b in range(1, blocks)]
    mine = project(0)

    top_count = routes.shape[1]
    capacity = max(2, 3 * length * top_count // (2 * devices))
    experts = expert_home.shape[0]
    picked = routes[:, :, None] == jnp.arange(experts, dtype=jnp.int32)[None, None, :]
    target = jnp.sum(jnp.where(picked, expert_home[None, None, :], 0), axis=2)
    at_device = target[:, :, None] == jnp.arange(devices, dtype=jnp.int32)[None, None, :]
    chosen = jnp.any(at_device, axis=1)
    gates = jnp.sum(jnp.where(at_device, gate_weights[:, :, None], 0.0), axis=1)
    before = (
        lax.broadcasted_iota(jnp.int32, (length, length), 0)
        > lax.broadcasted_iota(jnp.int32, (length, length), 1)
    ).astype(bf16)
    rank = jnp.dot(before, chosen.astype(bf16), preferred_element_type=f32)
    slots = jnp.where(chosen, rank, -1.0)
    gate_high = jnp.floor(gates * 128.0) * (1.0 / 128.0)
    meta = jnp.concatenate([slots, gate_high, gates - gate_high], axis=1).astype(bf16)
    extra = -(-3 * devices // 128) * 128
    meta = jnp.pad(meta, ((0, 0), (0, extra - 3 * devices)))

    up_local = up_weight[0]
    down_local = down_weight[0]
    hops = list(range(0, plane, 2))
    two = -(-2 * capacity // 8) * 8

    at = jnp.stack([r, place * plane]).astype(jnp.int32)
    count_rows = -(-len(hops) * capacity // 16) * 16
    listed = shapes((count_rows, model), bf16)
    tile = 896 if model % 896 == 0 else model

    def dispatch(block):
        out = kernel_call(
            functools.partial(dispatch_kernel, devices, capacity),
            [at, block],
            [shapes((two, model), bf16)] * len(hops) + [shapes((length, len(hops) * two), bf16)],
        )
        return out[-1], [out[0]] + [swap(out[k], hops[k]) for k in range(1, len(hops))]

    def held(rows, *others):
        return list(lax.optimization_barrier(tuple(rows) + others)[: len(rows)]) if others else list(rows)

    def work(rows, before_list, before_work):
        rows = held(rows, *before_list)
        other = kernel_call(
            functools.partial(other_kernel, capacity), list(rows), listed, scalars=False
        )
        mine, theirs = kernel_call(
            functools.partial(expert_kernel, capacity, tile),
            held(rows, *before_work) + [swap(other, 1), up_local, down_local],
            [listed, listed],
            [
                pltpu.VMEM((2 * count_rows, model), bf16),
                pltpu.VMEM((2 * count_rows, up_local.shape[1]), bf16),
            ],
            scalars=False,
        )
        return mine, swap(theirs, 1)

    def sort_back(mine, theirs):
        return kernel_call(
            functools.partial(return_kernel, capacity),
            [mine, theirs],
            [shapes((two, model), bf16)] * len(hops),
            scalars=False,
        )

    def send_back(parts):
        return [parts[0]] + [swap(parts[k], hops[k]) for k in range(1, len(hops))]

    def gather_up(weigh, back):
        return jnp.dot(weigh, jnp.concatenate(back, axis=0), preferred_element_type=f32)

    residual_one, block = kernel_call(
        functools.partial(token_kernel, blocks),
        [moe_gain[None, :], hidden, mine, meta] + others,
        [shapes((length, model), bf16), shapes((length, model + extra), bf16)],
        scalars=False,
    )
    weighs, arrived, made, results, parts = {}, {}, {}, {}, {}
    end = outer - 1

    def give_back(step, *before):
        mine, theirs = made[step]
        if before:
            mine = after(mine, *before)
        results[step] = sort_back(mine, theirs)
        return send_back(results[step])

    for step in range(outer):
        following = turn(block) if step < end else None
        if step:
            before = arrived[step - 1][1:2] + ([made[step - 2][0]] if step >= 2 else [])
            block = held([block], *before)[0]
        weighs[step], arrived[step] = dispatch(block)
        block = following
        if step:
            made[step - 1] = work(arrived[step - 1], [weighs[step]], [])
        if 1 <= step - 1 < end:
            parts[step - 1] = gather_up(weighs[step - 1], give_back(step - 1))
    before = [made[end - 1][0]] if end else []
    if end >= 3:
        before.append(parts[end - 2])
    made[end] = work(arrived[end], before, [])
    results[0] = sort_back(*made[0])
    if end:
        back = give_back(end, *([parts[end - 1]] if end >= 2 else []))
        parts[end] = gather_up(weighs[end], held(back, results[0][0]))
    back = send_back(held(results[0], *([results[end][0]] if end else [])))
    carried = None
    for step in range(1, outer):
        part = parts[step]
        if carried is not None:
            part = part + carried.astype(f32)
        carried = turn(part.astype(bf16))
    if carried is not None:
        back = held(back, carried)
    part = residual_one.astype(f32) + gather_up(weighs[0], back)
    if carried is not None:
        part = part + carried.astype(f32)
    return part.astype(bf16)


def solution(mesh):
    placed = (
        P(AXES, None),
        P(AXES, None),
        P(AXES, None),
        P(None, AXES),
        P(),
        P(),
        P("grp", None),
        P(),
        P(AXES, None),
        P(AXES, None),
        P(),
        P(AXES, None, None),
        P(AXES, None, None),
    )
    return jax.shard_map(local, mesh=mesh, in_specs=placed, out_specs=P(AXES, None), check_vma=False)
```

```python
import functools

import jax
import jax.numpy as jnp
from jax import lax
from jax.experimental import pallas as pl
from jax.experimental.pallas import tpu as pltpu
from jax.sharding import PartitionSpec as P

AXES = ("seq", "grp")
N = 64
G = 8
EPS = 1e-05
DEC = 16
VMEM_LIMIT = 24 * 1024 * 1024
f32 = jnp.float32
bf16 = jnp.bfloat16


def dot(a, b, contract, precision=None):
    return lax.dot_general(
        a, b, ((contract[0], contract[1]), ((), ())), preferred_element_type=f32, precision=precision
    )


def spread_lanes(columns, width):
    count = len(columns)
    rows = columns[0].shape[0]
    lane = lax.broadcasted_iota(jnp.int32, (rows, count * width), 1)
    out = jnp.broadcast_to(columns[-1], (rows, count * width))
    for j in range(count - 2, -1, -1):
        out = jnp.where(lane < (j + 1) * width, columns[j], out)
    return out


def split_decay(d):
    whole = jnp.floor(d)
    part = d - whole
    coarse = jnp.floor(part * 256.0) * (1.0 / 256.0)
    fine = part - coarse
    row = lax.broadcasted_iota(jnp.int32, (DEC, d.shape[1]), 0)
    rows = jnp.where(row == 0, whole, jnp.where(row == 1, coarse, jnp.where(row == 2, fine, 0.0)))
    return rows.astype(bf16)


def join_decay(rows):
    return jnp.sum(rows.astype(f32), axis=0, keepdims=True)


def silu(x):
    return x * (1.0 / (1.0 + jnp.exp(-x)))


def columns(blocks, inner, keys, c, width, which):
    start, first = 0, 0
    for extent in (inner, keys, keys):
        size = extent // blocks
        if c < first + size:
            return pl.ds(pl.multiple_of(start + which * size + (c - first), width), width)
        start, first = start + extent, first + size


def pick_kernel(blocks, inner, width, at_ref, x_ref, tail_ref, *outs):
    half = at_ref[1]
    length, channels = x_ref.shape
    keys = (channels - inner) // 2
    tail_ref[...] = x_ref[length - tail_ref.shape[0] :, :]
    for b in range(1, blocks):
        for c in range(0, channels // blocks, width):
            outs[b - 1][:, c : c + width] = x_ref[
                :, columns(blocks, inner, keys, c, width, half ^ b)
            ]


def running(ld):
    length = ld.shape[1]
    low = (
        lax.broadcasted_iota(jnp.int32, (length, length), 0)
        >= lax.broadcasted_iota(jnp.int32, (length, length), 1)
    ).astype(f32)
    return (
        dot(ld, low, ((1,), (1,)), lax.Precision.HIGHEST),
        dot(low, ld, ((1,), (1,)), lax.Precision.HIGHEST),
    )


def prepare_kernel(blocks, inner, width, at_ref, cw_ref, ld_ref, z_ref, cw_out, ld_out, *z_outs):
    half = at_ref[1]
    keys = (cw_ref.shape[1] - inner) // 2
    ld_out[...] = ld_ref[...]
    for c in range(0, cw_out.shape[1], width):
        cw_out[:, c : c + width] = cw_ref[:, columns(blocks, inner, keys, c, width, half)]
    for b in range(1, blocks):
        for c in range(0, inner // blocks, width):
            at = pl.ds(pl.multiple_of((half ^ b) * (inner // blocks) + c, width), width)
            z_outs[b - 1][:, c : c + width] = z_ref[:, at]


def start_kernel(members, blocks, at_ref, cw_ref, *rest):
    xs, prevs, lds = rest[:blocks], rest[blocks : 2 * blocks], rest[2 * blocks : 3 * blocks]
    rest = rest[3 * blocks :]
    acts, outs, scr = rest[:blocks], rest[blocks : blocks + members], rest[-1]
    member, half = at_ref[0], at_ref[1]
    length = xs[0].shape[0]
    channels = xs[0].shape[1] // blocks
    heads = lds[0].shape[0] // blocks
    count = scr.shape[0]
    per_group = heads // count
    inner = channels - 2 * count * N
    width = inner // count
    head_size = width // per_group
    halo, taps = prevs[0].shape[0], cw_ref.shape[0]
    for b in range(blocks):
        ld = lds[b][pl.ds(pl.multiple_of(half * heads, heads), heads), :]
        cumt = running(ld)[1]
        last = cumt[length - 1 : length, :]
        to_end = jnp.exp(last - cumt)
        act_ref = acts[b]
        for c in range(0, channels, width):
            cols = slice(c, c + width)
            at = columns(blocks, inner * blocks, count * N * blocks, c, width, half)
            padded = jnp.concatenate(
                [prevs[b][:, at], xs[b][:, cols if b else at]], axis=0
            ).astype(f32)
            first = halo - taps + 1
            total = cw_ref[0:1, cols] * padded[first : first + length]
            for k in range(1, taps):
                total = total + cw_ref[k : k + 1, cols] * padded[first + k : first + k + length]
            act_ref[:, cols] = silu(total).astype(bf16)
        slot = half ^ b
        for g in range(count):
            v = act_ref[:, g * width : (g + 1) * width].astype(f32)
            ik = act_ref[:, inner + g * N : inner + (g + 1) * N]
            hs = range(g * per_group, (g + 1) * per_group)
            weighted = (v * spread_lanes([to_end[:, h : h + 1] for h in hs], head_size)).astype(bf16)
            scr[g, slot, :N, :] = dot(ik, weighted, ((0,), (0,))).astype(bf16)
            scr[g, slot, N:, :] = split_decay(
                spread_lanes([last[:, h : h + 1] for h in hs], head_size)
            )
    for m in range(members):
        outs[m][...] = scr[member ^ m]


def in_order(members, blocks, member, chunks, scr):
    for m in range(members):
        who = member ^ m
        for k in range(blocks):
            scr[(who >> 1) * 2 * blocks + 2 * k + (who & 1)] = chunks[m][k]


def plane_kernel(members, blocks, at_ref, *rest):
    chunks, out, scr = rest[:members], rest[members], rest[members + 1]
    in_order(members, blocks, at_ref[0], chunks, scr)
    state = jnp.zeros((N, out.shape[1]), f32)
    total = jnp.zeros((1, out.shape[1]), f32)
    for s in range(members * blocks):
        decay = join_decay(scr[s, N:, :])
        state = jnp.exp(decay) * state + scr[s, :N, :].astype(f32)
        total = total + decay
    out[:N, :] = state.astype(bf16)
    out[N:, :] = split_decay(total)


def pair_kernel(stage, at_ref, own_ref, other_ref, out_ref):
    later = ((at_ref[3] >> stage) & 1) == 1
    own, other = own_ref[:N, :].astype(f32), other_ref[:N, :].astype(f32)
    own_decay, other_decay = join_decay(own_ref[N:, :]), join_decay(other_ref[N:, :])
    first, second = jnp.where(later, other, own), jnp.where(later, own, other)
    out_ref[:N, :] = (jnp.exp(jnp.where(later, own_decay, other_decay)) * first + second).astype(bf16)
    out_ref[N:, :] = split_decay(own_decay + other_decay)


def enter_kernel(members, blocks, stages, at_ref, scr, *rest):
    earlier, outs, inc = rest[:stages], rest[stages : stages + members], rest[-1]
    member = at_ref[0]
    state = jnp.zeros((N, scr.shape[2]), f32)
    for stage in range(stages - 1, -1, -1):
        e = earlier[stage]
        joined = jnp.exp(join_decay(e[N:, :])) * state + e[:N, :].astype(f32)
        state = jnp.where(((at_ref[3] >> stage) & 1) == 1, joined, state)
    for s in range(members * blocks):
        inc[s] = state.astype(bf16)
        state = jnp.exp(join_decay(scr[s, N:, :])) * state + scr[s, :N, :].astype(f32)
    for m in range(members):
        who = member ^ m
        for k in range(blocks):
            outs[m][k] = inc[(who >> 1) * 2 * blocks + 2 * k + (who & 1)]


def inside_kernel(count, blocks, at_ref, *refs):
    acts, lds, outs = (refs[k * blocks : (k + 1) * blocks] for k in range(3))
    length, channels = acts[0].shape
    heads = lds[0].shape[0] // blocks
    per_group = heads // count
    inner = channels - 2 * count * N
    head_size = inner // heads
    causal = lax.broadcasted_iota(jnp.int32, (length, length), 0) >= lax.broadcasted_iota(
        jnp.int32, (length, length), 1
    )
    for b in range(blocks):
        act_ref, out_ref = acts[b], outs[b]
        cum, cumt = running(lds[b][pl.ds(pl.multiple_of(at_ref[1] * heads, heads), heads), :])
        for g in range(count):
            ik = act_ref[:, inner + g * N : inner + (g + 1) * N]
            ok = act_ref[:, inner + (count + g) * N : inner + (count + g + 1) * N]
            meet = jnp.where(causal, dot(ok, ik, ((1,), (1,))), 0.0)
            for h in range(g * per_group, (g + 1) * per_group):
                gap = jnp.where(causal, cumt[:, h : h + 1] - cum[h : h + 1, :], 0.0)
                mixing = (jnp.exp(gap) * meet).astype(bf16)
                cols = slice(h * head_size, (h + 1) * head_size)
                out_ref[:, cols] = dot(mixing, act_ref[:, cols], ((1,), (0,)))


def norm_kernel(members, blocks, b, at_ref, gain_ref, act_ref, ld_ref, inside_ref, z_ref, *rest):
    incoming, own_ref, pair_ref = rest[:members], rest[members], rest[members + 1]
    out_ref, scr, mix = rest[-3], rest[-2], rest[-1]
    member, half, core = at_ref[0], at_ref[1], at_ref[2]
    for m in range(members):
        scr[member ^ m] = incoming[m][...]
    inner = z_ref.shape[1] if b else z_ref.shape[1] // blocks
    heads = ld_ref.shape[0] // blocks
    count = scr.shape[0]
    per_group = heads // count
    width = inner // count
    head_size = inner // heads
    shard = count // 2
    reach = jnp.exp(running(ld_ref[pl.ds(pl.multiple_of(half * heads, heads), heads), :])[1])
    slot = half ^ b
    for g in range(count):
        cols = slice(g * width, (g + 1) * width)
        ok = act_ref[:, inner + (count + g) * N : inner + (count + g + 1) * N]
        hs = range(g * per_group, (g + 1) * per_group)
        far = dot(ok, scr[g, slot], ((1,), (0,)))
        ssm = inside_ref[:, cols] + far * spread_lanes([reach[:, h : h + 1] for h in hs], head_size)
        at = pl.ds(pl.multiple_of(half * inner + g * width, width), width)
        gated = ssm * silu(z_ref[:, cols if b else at].astype(f32))
        square = jnp.mean(gated * gated, axis=1, keepdims=True)
        mix[(g // shard) ^ core, :, g % shard * width : (g % shard + 1) * width] = (
            gated * lax.rsqrt(square + EPS) * gain_ref[:, at]
        ).astype(bf16)
    model = out_ref.shape[1]
    tile = 384 if model % 384 == 0 else model
    for c in range(0, model, tile):
        total = dot(mix[0], own_ref[:, c : c + tile], ((1,), (0,)))
        total = total + dot(mix[1], pair_ref[:, c : c + tile], ((1,), (0,)))
        out_ref[:, c : c + tile] = total.astype(out_ref.dtype)


def token_kernel(blocks, gain_ref, hidden_ref, own_ref, meta_ref, *rest):
    others, residual_ref, block_ref = rest[: blocks - 1], rest[blocks - 1], rest[blocks]
    model = hidden_ref.shape[1]
    total = hidden_ref[...].astype(f32) + own_ref[...]
    for other in others:
        total = total + other[...].astype(f32)
    residual = total.astype(bf16)
    residual_ref[...] = residual
    wide = residual.astype(f32)
    square = jnp.mean(wide * wide, axis=1, keepdims=True)
    block_ref[:, :model] = (wide * lax.rsqrt(square + EPS) * gain_ref[...]).astype(bf16)
    block_ref[:, model:] = meta_ref[...]


def dispatch_kernel(devices, capacity, at_ref, block_ref, *rest):
    outs, weigh_ref = rest[:-1], rest[-1]
    length = block_ref.shape[0]
    rows, model = outs[0].shape
    lanes = len(outs) * rows
    device = lax.broadcasted_iota(jnp.int32, (devices, lanes), 0)

    def layout(shape):
        lane = lax.broadcasted_iota(jnp.int32, shape, 1)
        chip, within = jnp.zeros(shape, jnp.int32), lane
        for k in range(1, len(outs)):
            chip = jnp.where(lane >= k * rows, k, chip)
            within = jnp.where(lane >= k * rows, lane - k * rows, within)
        core = jnp.where(within >= capacity, 1, 0)
        return chip, core, within - capacity * core

    chip, core, _ = layout((devices, lanes))
    select = (device == at_ref[1] + (at_ref[0] ^ (2 * chip + core))).astype(f32).astype(bf16)
    place = layout((length, lanes))[2]
    place = jnp.where(place < capacity, place, -2).astype(f32)
    slot = dot(block_ref[:, model : model + devices], select, ((1,), (0,)))
    gate = dot(block_ref[:, model + devices : model + 2 * devices], select, ((1,), (0,))) + dot(
        block_ref[:, model + 2 * devices : model + 3 * devices], select, ((1,), (0,))
    )
    hit = slot == place
    weigh_ref[...] = jnp.where(hit, gate, 0.0).astype(bf16)
    take = jnp.where(hit, 1.0, 0.0).astype(bf16)
    total = dot(take, block_ref[:, :model], ((0,), (0,)))
    for k in range(len(outs)):
        outs[k][...] = total[k * rows : (k + 1) * rows].astype(bf16)


def chosen_rows(shape, dim, chip, core, capacity):
    listed = lax.broadcasted_iota(jnp.int32, shape, 1 - dim)
    within = lax.broadcasted_iota(jnp.int32, shape, dim) - core * capacity
    hit = (listed == chip * capacity + within) & (within >= 0) & (within < capacity)
    return hit.astype(f32).astype(bf16)


def listed_rows(ins, core, capacity, count):
    total = None
    for k, ref in enumerate(ins):
        part = dot(chosen_rows((count, ref.shape[0]), 1, k, core, capacity), ref[...], ((1,), (0,)))
        total = part if total is None else total + part
    return total.astype(bf16)


def other_kernel(capacity, *refs):
    refs[-1][...] = listed_rows(refs[:-1], 1, capacity, refs[-1].shape[0])


def expert_kernel(capacity, tile, *refs):
    ins, (got_ref, up_ref, down_ref, mine_ref, other_ref, rows_ref, act_ref) = refs[:-7], refs[-7:]
    count, model = got_ref.shape
    rows_ref[:count, :] = listed_rows(ins, 0, capacity, count)
    rows_ref[count:, :] = got_ref[...]
    ffw = up_ref.shape[1]
    step = 512 if ffw % 512 == 0 else ffw

    @pl.loop(0, ffw // step)
    def _(f):
        cols = pl.ds(pl.multiple_of(f * step, step), step)
        up = jnp.maximum(dot(rows_ref[...], up_ref[:, cols], ((1,), (0,))), 0.0)
        act_ref[:, cols] = (up * up).astype(bf16)

    @pl.loop(0, model // tile)
    def _(c):
        cols = pl.ds(pl.multiple_of(c * tile, tile), tile)
        part = dot(act_ref[...], down_ref[:, cols], ((1,), (0,)))
        mine_ref[:, cols] = part[:count].astype(bf16)
        other_ref[:, cols] = part[count:].astype(bf16)


def return_kernel(capacity, mine_ref, back_ref, *outs):
    count = mine_ref.shape[0]
    for k, out in enumerate(outs):
        shape = (out.shape[0], count)
        out[...] = (
            dot(chosen_rows(shape, 0, k, 0, capacity), mine_ref[...], ((1,), (0,)))
            + dot(chosen_rows(shape, 0, k, 1, capacity), back_ref[...], ((1,), (0,)))
        ).astype(bf16)


def after(x, *others):
    return lax.optimization_barrier((x,) + others)[0]


def local(
    hidden,
    conv_input,
    z_stream,
    log_decay,
    conv_weight,
    norm_gain,
    out_weight,
    moe_gain,
    routes,
    gate_weights,
    expert_home,
    up_weight,
    down_weight,
):
    n_grp = lax.axis_size("grp")
    devices = lax.axis_size("seq") * n_grp
    plane = 2 * n_grp
    outer = devices // plane
    me = lax.axis_index("seq") * n_grp + lax.axis_index("grp")
    r = lax.rem(me, plane)
    place = lax.div(me, plane)

    def swap(x, m):
        return lax.ppermute(x, AXES, [(d, d ^ m) for d in range(devices)])

    def onward(x, by):
        return lax.ppermute(
            x, AXES, [(d, d + by) for d in range(devices) if d + by < devices]
        )

    def turn(x):
        return lax.ppermute(x, AXES, [(d, (d + plane) % devices) for d in range(devices)])

    length, channels = conv_input.shape
    inner = z_stream.shape[1]
    width = inner // G
    model = hidden.shape[1]
    smem = pl.BlockSpec(memory_space=pltpu.SMEM)
    halo = 16

    blocks = n_grp // 2
    members = plane // blocks
    grp = lax.axis_index("grp")
    half = lax.div(grp, 2)
    core = lax.rem(grp, 2)
    member = lax.div(r, n_grp) * 2 + core
    at_member = jnp.stack([member, half, core, place]).astype(jnp.int32)
    count = G // blocks

    def onward_to(x, by, m):
        return lax.ppermute(
            x, AXES, [(d, (d + by) ^ m) for d in range(devices) if d + by < devices]
        )

    shapes = jax.ShapeDtypeStruct
    vm = pl.BlockSpec(memory_space=pltpu.VMEM)
    wide = channels // blocks
    chunk = (N + DEC, width)

    def kernel_call(kernel, inputs, outs, scratch=(), flops=0, moved=0, scalars=True):
        return pl.pallas_call(
            kernel,
            out_shape=outs,
            in_specs=([smem] if scalars else []) + [vm] * (len(inputs) - (1 if scalars else 0)),
            scratch_shapes=list(scratch),
            compiler_params=pltpu.CompilerParams(vmem_limit_bytes=VMEM_LIMIT),
            cost_estimate=pl.CostEstimate(flops=flops, bytes_accessed=moved, transcendentals=0),
        )(*inputs)

    picked = kernel_call(
        functools.partial(pick_kernel, blocks, inner, width),
        [at_member, conv_input],
        [shapes((halo, channels), bf16)] + [shapes((length, wide), bf16)] * (blocks - 1),
    )
    tail = picked[0]
    prepared = kernel_call(
        functools.partial(prepare_kernel, blocks, inner, width),
        [at_member, conv_weight, log_decay, z_stream],
        [shapes((conv_weight.shape[0], wide), f32), shapes(log_decay.shape, f32)]
        + [shapes((length, inner // blocks), bf16)] * (blocks - 1),
    )
    xs, prevs, lds = [conv_input], [onward_to(tail, 1, 0)], [prepared[1]]
    for b in range(1, blocks):
        xs.append(swap(picked[b], 2 * b))
        prevs.append(onward_to(tail, 1, 2 * b))
        lds.append(swap(prepared[1], 2 * b))

    rows_own = out_weight
    rows_pair = swap(out_weight, 1)
    shard = out_weight.shape[0]

    first = kernel_call(
        functools.partial(start_kernel, members, blocks),
        [at_member, prepared[0]] + xs + prevs + lds,
        [shapes((length, wide), bf16)] * blocks
        + [shapes((blocks,) + chunk, bf16)] * members,
        [pltpu.VMEM((count, blocks) + chunk, bf16)],
        50000000,
        8000000,
    )
    acts = first[:blocks]
    sends = first[blocks : blocks + members]
    zs = [z_stream] + [swap(prepared[1 + b], 2 * b) for b in range(1, blocks)]
    mask = [(m >> 1) * n_grp + (m & 1) for m in range(members)]
    chunks = [sends[0]] + [swap(sends[m], mask[m]) for m in range(1, members)]
    inside = kernel_call(
        functools.partial(inside_kernel, count, blocks),
        [at_member] + list(acts) + lds,
        [shapes((length, inner // blocks), f32)] * blocks,
        (),
        100000000,
        15000000,
    )
    whole, ordered = kernel_call(
        functools.partial(plane_kernel, members, blocks),
        [at_member] + chunks,
        [shapes(chunk, bf16), shapes((plane,) + chunk, bf16)],
    )
    earlier, stage = [], 0
    while (1 << stage) < outer:
        earlier.append(swap(whole, plane << stage))
        stage += 1
        if (1 << stage) < outer:
            whole = kernel_call(
                functools.partial(pair_kernel, stage - 1),
                [at_member, whole, earlier[-1]],
                shapes(chunk, bf16),
            )
    entering = kernel_call(
        functools.partial(enter_kernel, members, blocks, stage),
        [at_member, ordered] + earlier,
        [shapes((blocks, N, width), bf16)] * members,
        [pltpu.VMEM((plane, N, width), bf16)],
        1000000,
        2000000,
    )
    incoming = [entering[0]] + [swap(entering[m], mask[m]) for m in range(1, members)]
    def project(b):
        return kernel_call(
            functools.partial(norm_kernel, members, blocks, b),
            [at_member, norm_gain[None, :], acts[b], lds[b], inside[b], zs[b]]
            + incoming
            + [rows_own, rows_pair],
            shapes((length, model), bf16 if b else f32),
            [pltpu.VMEM((count, blocks, N, width), bf16), pltpu.VMEM((2, length, shard), bf16)],
            800000000,
            8000000,
        )

    others = [swap(project(b), 2 * b) for b in range(1, blocks)]
    mine = project(0)

    top_count = routes.shape[1]
    capacity = max(2, 3 * length * top_count // (2 * devices))
    experts = expert_home.shape[0]
    picked = routes[:, :, None] == jnp.arange(experts, dtype=jnp.int32)[None, None, :]
    target = jnp.sum(jnp.where(picked, expert_home[None, None, :], 0), axis=2)
    at_device = target[:, :, None] == jnp.arange(devices, dtype=jnp.int32)[None, None, :]
    chosen = jnp.any(at_device, axis=1)
    gates = jnp.sum(jnp.where(at_device, gate_weights[:, :, None], 0.0), axis=1)
    before = (
        lax.broadcasted_iota(jnp.int32, (length, length), 0)
        > lax.broadcasted_iota(jnp.int32, (length, length), 1)
    ).astype(bf16)
    rank = jnp.dot(before, chosen.astype(bf16), preferred_element_type=f32)
    slots = jnp.where(chosen, rank, -1.0)
    gate_high = jnp.floor(gates * 128.0) * (1.0 / 128.0)
    meta = jnp.concatenate([slots, gate_high, gates - gate_high], axis=1).astype(bf16)
    extra = -(-3 * devices // 128) * 128
    meta = jnp.pad(meta, ((0, 0), (0, extra - 3 * devices)))

    up_local = up_weight[0]
    down_local = down_weight[0]
    hops = list(range(0, plane, 2))
    two = -(-2 * capacity // 8) * 8

    at = jnp.stack([r, place * plane]).astype(jnp.int32)
    count_rows = -(-len(hops) * capacity // 16) * 16
    listed = shapes((count_rows, model), bf16)
    tile = 896 if model % 896 == 0 else model

    def dispatch(block):
        out = kernel_call(
            functools.partial(dispatch_kernel, devices, capacity),
            [at, block],
            [shapes((two, model), bf16)] * len(hops) + [shapes((length, len(hops) * two), bf16)],
        )
        return out[-1], [out[0]] + [swap(out[k], hops[k]) for k in range(1, len(hops))]

    def held(rows, *others):
        return list(lax.optimization_barrier(tuple(rows) + others)[: len(rows)]) if others else list(rows)

    def work(rows, before_list, before_work):
        rows = held(rows, *before_list)
        other = kernel_call(
            functools.partial(other_kernel, capacity), list(rows), listed, scalars=False
        )
        mine, theirs = kernel_call(
            functools.partial(expert_kernel, capacity, tile),
            held(rows, *before_work) + [swap(other, 1), up_local, down_local],
            [listed, listed],
            [
                pltpu.VMEM((2 * count_rows, model), bf16),
                pltpu.VMEM((2 * count_rows, up_local.shape[1]), bf16),
            ],
            scalars=False,
        )
        return mine, swap(theirs, 1)

    def sort_back(mine, theirs):
        return kernel_call(
            functools.partial(return_kernel, capacity),
            [mine, theirs],
            [shapes((two, model), bf16)] * len(hops),
            scalars=False,
        )

    def send_back(parts):
        return [parts[0]] + [swap(parts[k], hops[k]) for k in range(1, len(hops))]

    def gather_up(weigh, back):
        return jnp.dot(weigh, jnp.concatenate(back, axis=0), preferred_element_type=f32)

    residual_one, block = kernel_call(
        functools.partial(token_kernel, blocks),
        [moe_gain[None, :], hidden, mine, meta] + others,
        [shapes((length, model), bf16), shapes((length, model + extra), bf16)],
        scalars=False,
    )
    weighs, arrived, made, results, parts = {}, {}, {}, {}, {}
    end = outer - 1

    def give_back(step, *before):
        mine, theirs = made[step]
        if before:
            mine = after(mine, *before)
        results[step] = sort_back(mine, theirs)
        return send_back(results[step])

    for step in range(outer):
        following = turn(block) if step < end else None
        if step:
            before = arrived[step - 1][1:2] + ([made[step - 2][0]] if step >= 2 else [])
            block = held([block], *before)[0]
        weighs[step], arrived[step] = dispatch(block)
        block = following
        if step:
            made[step - 1] = work(arrived[step - 1], [weighs[step]], [])
        if 1 <= step - 1 < end:
            parts[step - 1] = gather_up(weighs[step - 1], give_back(step - 1))
    before = [made[end - 1][0]] if end else []
    if end >= 3:
        before.append(parts[end - 2])
    made[end] = work(arrived[end], before, [])
    results[0] = sort_back(*made[0])
    if end:
        back = give_back(end, *([parts[end - 1]] if end >= 2 else []))
        parts[end] = gather_up(weighs[end], held(back, results[0][0]))
    back = send_back(held(results[0], *([results[end][0]] if end else [])))
    carried = None
    for step in range(1, outer):
        part = parts[step]
        if carried is not None:
            part = part + carried.astype(f32)
        carried = turn(part.astype(bf16))
    if carried is not None:
        back = held(back, carried)
    part = residual_one.astype(f32) + gather_up(weighs[0], back)
    if carried is not None:
        part = part + carried.astype(f32)
    return part.astype(bf16)


def solution(mesh):
    placed = (
        P(AXES, None),
        P(AXES, None),
        P(AXES, None),
        P(None, AXES),
        P(),
        P(),
        P("grp", None),
        P(),
        P(AXES, None),
        P(AXES, None),
        P(),
        P(AXES, None, None),
        P(AXES, None, None),
    )
    return jax.shard_map(local, mesh=mesh, in_specs=placed, out_specs=P(AXES, None), check_vma=False)
```
